256 devices in a mesh: ctx: 32 (over x, z), tp: 8 (over y, core).
Axes of the slice: x: 4, y: 4, z: 8, core: 2. Of those that a mesh axis runs over, the one named last changes fastest.
Arguments:
- first_input: bfloat16 [8192, 8192], P('ctx', 'tp'), may hold values from -6 to 6
- second_input: bfloat16 [8192, 8192], P('ctx', 'tp'), may hold values from -6 to 6
- value_input: bfloat16 [8192, 8192], P('ctx', 'tp'), may hold values from -6 to 6
- filter_taps: bfloat16 [8192, 8192], P('ctx', 'tp'), may hold values from -1.5 to 1.5
- skip_gain: float32 [8192], P('tp'), may hold values from -1 to 1
- out_weight: bfloat16 [8192, 4096], P('tp'), may hold values from -0.0625 to 0.0625
- queries: bfloat16 [8192, 4096], P('ctx', 'tp'), may hold values from -6 to 6
- keys: bfloat16 [8192, 4096], P('ctx', 'tp'), may hold values from -6 to 6
Outputs:
- mixed: bfloat16 [8192, 4096], P('ctx', 'tp')
- attended: bfloat16 [8192, 4096], P('ctx', 'tp')
The draws below stay inside these ranges and needn't reach their ends.
All inputs are finite; a program needn't handle non-finite values.
Results may differ from the reference program's by a relative error of at most 0.02.
Values may be sent and summed in bfloat16 or wider, within the bound.
A program may use at most 256 MiB of HBM per device.

```python
import math
import jax
import jax.numpy as jnp
from jax import lax

D = 8192
HEADS = 32
HS = 128
TOKENS = 8192
OUT_WIDTH = 4096


def draw_queries(key, part):
    key = jax.random.fold_in(key, 11)
    values = jax.random.uniform(key, (TOKENS, HEADS * HS), jnp.float32, -6.0, 6.0)
    return values.astype(jnp.bfloat16)


def draw_keys(key, part):
    key = jax.random.fold_in(key, 23)
    values = 0.3 * jnp.clip(jax.random.normal(key, (TOKENS, HEADS * HS), jnp.float32), -5.0, 5.0)
    return values.astype(jnp.bfloat16)


def draw_filter_taps(key, part):
    key = jax.random.fold_in(key, 5)
    rate_key, kind_key, noise_key, tail_key = jax.random.split(key, 4)
    lags = jnp.arange(TOKENS, dtype=jnp.float32)
    draws = jax.random.uniform(rate_key, (D,), jnp.float32)
    slow_rate = (0.2 + 1.8 * draws) / TOKENS
    fast_rate = jnp.exp(math.log(1.0 / 50.0) + draws * (math.log(1.0 / 30.0) - math.log(1.0 / 50.0)))
    slow = jax.random.bernoulli(kind_key, 0.5, (D,))
    noise = jnp.clip(jax.random.normal(noise_key, (TOKENS, D), jnp.float32), -5.0, 5.0)
    rates = jnp.where(slow, slow_rate, fast_rate)
    energy = (1.0 - jnp.exp(-2.0 * rates * TOKENS)) / (1.0 - jnp.exp(-2.0 * rates))
    envelope = jnp.exp(-rates[None, :] * lags[:, None]) / jnp.sqrt(energy)[None, :]
    tail = 0.004 * jax.random.uniform(tail_key, (TOKENS, D), jnp.float32, -1.0, 1.0) + 0.002
    tail = jnp.where((lags >= 128.0)[:, None], tail, 0.0)
    return (noise * envelope + tail).astype(jnp.bfloat16)


def steps_of(key, extent, cuts, least, top_value):
    loudness = 1.0
    for position, parts in cuts:
        steps = jax.random.uniform(jax.random.fold_in(jax.random.fold_in(key, 6), position), (parts,), jnp.float32, least / len(cuts), top_value / len(cuts))
        loudness = loudness * jnp.repeat(jnp.exp(steps), extent[position] // parts).reshape((-1,) + (1,) * (len(extent) - 1 - position))
    return loudness


def gaussian(key, dims, spread, limit, cuts=(), kind=jnp.bfloat16):
    loudness = steps_of(key, dims, cuts, -0.22, 0.18) if cuts else 1.0
    drawn = jax.random.normal(key, dims, jnp.float32) * spread * loudness
    return jnp.minimum(jnp.maximum(drawn, -limit), limit).astype(kind)


def setup_inputs(seed: int = 0) -> dict:
    streams_of = jax.random.split(jax.random.key(seed), 9)
    first_input = gaussian(streams_of[0], (TOKENS, D), 1.0, 6.0, ((0, 32), (1, 8)))
    second_input = gaussian(streams_of[1], (TOKENS, D), 1.0, 6.0, ((0, 32), (1, 8)))
    value_input = gaussian(streams_of[2], (TOKENS, D), 1.0, 6.0, ((0, 32), (1, 8)))
    filter_taps = draw_filter_taps(jax.random.fold_in(streams_of[8], 71), 0)
    skip_gain = jnp.clip(jax.random.uniform(streams_of[4], (D,), jnp.float32, -1.0, 1.0) * steps_of(streams_of[4], (D,), ((0, 8),), -0.4, 0.0), -1.0, 1.0)
    out_weight = gaussian(streams_of[5], (D, OUT_WIDTH), D ** -0.5, 0.0625, ((0, 8),))
    queries = draw_queries(jax.random.fold_in(streams_of[8], 71), 0)
    keys = draw_keys(jax.random.fold_in(streams_of[8], 71), 0)
    return {"first_input": first_input, "second_input": second_input, "value_input": value_input, "filter_taps": filter_taps, "skip_gain": skip_gain, "out_weight": out_weight, "queries": queries, "keys": keys}


def causal_filter(signal, kernel):
    length = signal.shape[0]
    width = signal.shape[1]
    block_width = min(width, 512)
    groups = width // block_width
    signal_blocks = signal.reshape(length, groups, block_width).transpose(1, 0, 2)
    kernel_blocks = kernel.reshape(length, groups, block_width).transpose(1, 0, 2)

    def one_group(operands):
        signal_block, kernel_block = operands
        spectrum = jnp.fft.rfft(signal_block, n=2 * length, axis=0) * jnp.fft.rfft(kernel_block, n=2 * length, axis=0)
        return jnp.fft.irfft(spectrum, n=2 * length, axis=0)[:length]
    result = lax.map(one_group, (signal_blocks, kernel_blocks))
    return result.transpose(1, 0, 2).reshape(length, width)

def causal_attention(queries, keys, mixed):
    block_rows = min(512, TOKENS)
    score_scale = 1.0 / math.sqrt(HS)
    key_pos = jnp.arange(TOKENS, dtype=jnp.int32)

    def one_head(head_index):
        query_head = lax.dynamic_slice_in_dim(queries, head_index * HS, HS, 1)
        key_head = lax.dynamic_slice_in_dim(keys, head_index * HS, HS, 1)
        value_head = lax.dynamic_slice_in_dim(mixed, head_index * HS, HS, 1)

        def one_block(block_index):
            query_block = lax.dynamic_slice_in_dim(query_head, block_index * block_rows, block_rows, 0)
            scores = jnp.dot(query_block, key_head.T, preferred_element_type=jnp.float32) * score_scale
            query_pos = block_index * block_rows + jnp.arange(block_rows, dtype=jnp.int32)
            allowed = key_pos[None, :] <= query_pos[:, None]
            scores = jnp.where(allowed, scores, -jnp.inf)
            top_score = lax.optimization_barrier(jnp.max(scores, axis=1, keepdims=True))
            weights = jnp.where(allowed, jnp.exp(scores - top_score), 0.0)
            totals = lax.optimization_barrier(jnp.sum(weights, axis=1, keepdims=True))
            rounded = weights.astype(jnp.bfloat16)
            return jnp.dot(rounded, value_head, preferred_element_type=jnp.float32) / totals
        blocks = lax.map(one_block, jnp.arange(TOKENS // block_rows, dtype=jnp.int32))
        return blocks.reshape(TOKENS, HS)
    heads_out = lax.map(one_head, jnp.arange(HEADS, dtype=jnp.int32))
    return heads_out.transpose(1, 0, 2).reshape(TOKENS, HEADS * HS).astype(jnp.bfloat16)

def reference(first_input, second_input, value_input, filter_taps, skip_gain, out_weight, queries, keys):
    product = (first_input.astype(jnp.float32) * value_input.astype(jnp.float32)).astype(jnp.bfloat16)
    product_wide = lax.optimization_barrier(product).astype(jnp.float32)
    filtered = causal_filter(product_wide, filter_taps.astype(jnp.float32)).astype(jnp.bfloat16)
    filtered_wide = lax.optimization_barrier(filtered).astype(jnp.float32)
    gated = (second_input.astype(jnp.float32) * (filtered_wide + skip_gain[None, :] * product_wide)).astype(jnp.bfloat16)
    mixed = jnp.dot(gated, out_weight, preferred_element_type=jnp.float32).astype(jnp.bfloat16)
    attended = causal_attention(queries, keys, mixed)
    return (mixed, attended)
```

```python
import functools
import math

import jax
import jax.numpy as jnp
import numpy as np
from jax import lax
from jax.experimental import pallas as pl
from jax.experimental.pallas import tpu as pltpu
from jax.sharding import PartitionSpec as P

HS = 128
MESH = pl.DeviceIdType.MESH
BF = jnp.bfloat16
F32 = jnp.float32
CTX = 32
ROWS = 256
GROUP = 16
TOTAL = CTX * ROWS


def nt(a, b):
    return lax.dot_general(a, b, (((1,), (1,)), ((), ())), preferred_element_type=F32)


def nn(a, b):
    return jnp.dot(a, b, preferred_element_type=F32)


def tables():
    r = np.arange(CTX, dtype=np.float64)
    q = np.arange(CTX, dtype=np.float64)
    a = np.arange(ROWS, dtype=np.float64)
    rows = np.exp(-2j * np.pi * np.outer(q + 0.25, r) / CTX)
    turn = np.exp(-2j * np.pi * np.outer(q + 0.25, a) / TOTAL)
    cols = np.exp(-2j * np.pi * np.outer(a, a) / ROWS)
    eye = np.eye(GROUP)
    spread = lambda m: np.einsum("qr,cd->cqrd", m, eye).reshape(GROUP * CTX, CTX * GROUP)
    first = np.concatenate([spread(rows.real), spread(rows.imag)], axis=0)
    back = np.conj(rows).T
    gather = lambda m: np.einsum("rq,cd->rcdq", m, eye).reshape(CTX * GROUP, GROUP * CTX)
    last = np.concatenate([gather(back.real), -gather(back.imag)], axis=1)
    mix = np.block([[cols.real, cols.imag], [-cols.imag, cols.real]])
    unmix = np.block([[cols.real, -cols.imag], [cols.imag, cols.real]]) / TOTAL
    cast = lambda m: np.asarray(m, np.float32).astype(jnp.bfloat16)
    return (cast(first), cast(mix), cast(unmix), cast(last),
            np.asarray(turn.real, np.float32), np.asarray(turn.imag, np.float32))


def spectrum(x, first, mix, turn_re, turn_im):
    half = GROUP * CTX
    a = nn(first, x)
    a_re = a[:half].reshape(GROUP, CTX, ROWS)
    a_im = a[half:].reshape(GROUP, CTX, ROWS)
    z_re = (a_re * turn_re - a_im * turn_im).reshape(half, ROWS).astype(BF)
    z_im = (a_re * turn_im + a_im * turn_re).reshape(half, ROWS).astype(BF)
    return nn(jnp.concatenate([z_re, z_im], axis=1), mix)


def filter_kernel(
    first_ref, value_ref, taps_ref, second_ref, skip_ref, eye_ref, first_t, mix_t, unmix_t, last_t,
    turn_re, turn_im, gated_ref, product, send, recv, out_send, out_recv,
    send_sem, recv_sem, back_send_sem, back_recv_sem,
):
    me = lax.axis_index("ctx")
    half = GROUP * CTX
    barrier = pltpu.get_barrier_semaphore()

    def greet(k, carry):
        pl.semaphore_signal(
            barrier, inc=1, device_id={"ctx": lax.rem(me + k, CTX)}, device_id_type=MESH
        )
        return carry

    lax.fori_loop(1, CTX, greet, 0)
    eye = eye_ref[...]
    for cb in range(4):
        cols = slice(cb * 256, (cb + 1) * 256)
        prod = (first_ref[:, cols].astype(F32) * value_ref[:, cols].astype(F32)).astype(BF)
        product[:, cols] = prod
        for kind, block in ((0, prod), (1, taps_ref[:, cols])):
            turned = nt(eye, block).astype(BF)
            for dl in range(8):
                for h in range(2):
                    at = dl * 32 + h * GROUP
                    send[h, cb * 8 + dl, kind] = turned[at:at + GROUP]
    pl.semaphore_wait(barrier, CTX - 1)

    for h in range(2):
        def post(k, carry, h=h):
            to = lax.rem(me + k, CTX)
            pltpu.make_async_remote_copy(
                src_ref=send.at[h, to], dst_ref=recv.at[h, me],
                send_sem=send_sem.at[h], recv_sem=recv_sem.at[h],
                device_id={"ctx": to}, device_id_type=MESH,
            ).start()
            return carry

        pltpu.make_async_copy(send.at[h, me], recv.at[h, me], recv_sem.at[h]).start()
        lax.fori_loop(1, CTX, post, 0)

    for h in range(2):
        pltpu.make_async_copy(recv.at[h], recv.at[h], recv_sem.at[h]).wait()
        tr, ti = turn_re[...], turn_im[...]
        x = recv[h, :, 0].reshape(half, ROWS)
        w = recv[h, :, 1].reshape(half, ROWS)
        d = spectrum(x, first_t[...], mix_t[...], tr, ti)
        e = spectrum(w, first_t[...], mix_t[...], tr, ti)
        d_re, d_im, e_re, e_im = d[:, :ROWS], d[:, ROWS:], e[:, :ROWS], e[:, ROWS:]
        y_re = (d_re * e_re - d_im * e_im).astype(BF)
        y_im = (d_re * e_im + d_im * e_re).astype(BF)
        b = nn(jnp.concatenate([y_re, y_im], axis=1), unmix_t[...])
        b_re = b[:, :ROWS].reshape(GROUP, CTX, ROWS)
        b_im = b[:, ROWS:].reshape(GROUP, CTX, ROWS)
        c_re = (b_re * tr + b_im * ti).reshape(half, ROWS).astype(BF)
        c_im = (b_im * tr - b_re * ti).reshape(half, ROWS).astype(BF)
        y = nn(last_t[...], jnp.concatenate([c_re, c_im], axis=0))
        out_send[h] = y.astype(BF).reshape(CTX, GROUP, ROWS)

        def reply(k, carry, h=h):
            to = lax.rem(me + k, CTX)
            pltpu.make_async_remote_copy(
                src_ref=out_send.at[h, to], dst_ref=out_recv.at[h, me],
                send_sem=back_send_sem.at[h], recv_sem=back_recv_sem.at[h],
                device_id={"ctx": to}, device_id_type=MESH,
            ).start()
            return carry

        pltpu.make_async_copy(out_send.at[h, me], out_recv.at[h, me], back_recv_sem.at[h]).start()
        lax.fori_loop(1, CTX, reply, 0)

    for h in range(2):
        sent = send.at[h, pl.ds(0, CTX - 1)]
        pltpu.make_async_copy(sent, sent, send_sem.at[h]).wait()
    for h in range(2):
        pltpu.make_async_copy(out_recv.at[h], out_recv.at[h], back_recv_sem.at[h]).wait()
        sent = out_send.at[h, pl.ds(0, CTX - 1)]
        pltpu.make_async_copy(sent, sent, back_send_sem.at[h]).wait()
    for cb in range(4):
        cols = slice(cb * 256, (cb + 1) * 256)
        parts = [out_recv[h, cb * 8 + dl] for dl in range(8) for h in range(2)]
        filtered = nt(eye, jnp.concatenate(parts, axis=0)).astype(BF).astype(F32)
        prod = product[:, cols].astype(F32)
        gated_ref[:, cols] = (
            second_ref[:, cols].astype(F32) * (filtered + skip_ref[:, cols] * prod)
        ).astype(BF)


def vmem(count):
    return [pl.BlockSpec(memory_space=pltpu.VMEM)] * count


def filtered_and_gated(first_input, value_input, filter_taps, second_input, skip_gain):
    first, mix, unmix, last, turn_re, turn_im = (jnp.asarray(t) for t in tables())
    eye = jnp.eye(ROWS, dtype=BF)
    return pl.pallas_call(
        filter_kernel,
        out_shape=jax.ShapeDtypeStruct((ROWS, 1024), BF),
        in_specs=vmem(12),
        out_specs=pl.BlockSpec(memory_space=pltpu.VMEM),
        scratch_shapes=[
            pltpu.VMEM((ROWS, 1024), BF),
            pltpu.VMEM((2, CTX, 2, GROUP, ROWS), BF),
            pltpu.VMEM((2, CTX, 2, GROUP, ROWS), BF),
            pltpu.VMEM((2, CTX, GROUP, ROWS), BF),
            pltpu.VMEM((2, CTX, GROUP, ROWS), BF),
            pltpu.SemaphoreType.DMA((2,)),
            pltpu.SemaphoreType.DMA((2,)),
            pltpu.SemaphoreType.DMA((2,)),
            pltpu.SemaphoreType.DMA((2,)),
        ],
        compiler_params=pltpu.CompilerParams(
            collective_id=0, has_side_effects=True, vmem_limit_bytes=40 * 1024 * 1024
        ),
        name="filter_and_gate",
    )(first_input, value_input, filter_taps, second_input, skip_gain.reshape(1, 1024), eye,
      first, mix, unmix, last, turn_re, turn_im)


BIG_NEGATIVE = -1e30


def fold_block(state, query_heads, query_pos, key_heads, value_heads, key_pos, score_scale):
    top_score, weight_sum, weighted = state
    scores = (
        jnp.einsum("qhd,khd->qhk", query_heads, key_heads, preferred_element_type=jnp.float32)
        * score_scale
    )
    allowed = (key_pos[None, :] <= query_pos[:, None])[:, None, :]
    scores = jnp.where(allowed, scores, BIG_NEGATIVE)
    new_top = jnp.maximum(top_score, jnp.max(scores, axis=2))
    weights = jnp.where(allowed, jnp.exp(scores - new_top[:, :, None]), 0.0)
    shrink = jnp.exp(top_score - new_top)
    weight_sum = weight_sum * shrink + jnp.sum(weights, axis=2)
    weighted = weighted * shrink[:, :, None] + jnp.einsum(
        "qhk,khd->qhd",
        weights.astype(jnp.bfloat16),
        value_heads,
        preferred_element_type=jnp.float32,
    )
    return (new_top, weight_sum, weighted)


def fold_keys(state, query_heads, query_pos, key_heads, value_heads, key_pos, score_scale):
    key_rows = key_heads.shape[0]
    step_rows = 1024

    def scan_step(carry, step_index):
        first_row = step_index * step_rows
        key_part = lax.dynamic_slice_in_dim(key_heads, first_row, step_rows, 0)
        value_part = lax.dynamic_slice_in_dim(value_heads, first_row, step_rows, 0)
        pos_part = lax.dynamic_slice_in_dim(key_pos, first_row, step_rows, 0)
        return (
            fold_block(carry, query_heads, query_pos, key_part, value_part, pos_part, score_scale),
            None,
        )

    state, leftover = lax.scan(scan_step, state, jnp.arange(key_rows // step_rows, dtype=jnp.int32))
    return state


def per_device(
    first_input, second_input, value_input, filter_taps, skip_gain, out_weight, queries, keys
):
    tok_rows = first_input.shape[0]
    gated = filtered_and_gated(
        first_input, value_input, filter_taps, second_input, skip_gain
    )
    partial_sums = jnp.dot(gated, out_weight, preferred_element_type=jnp.float32)
    mixed = lax.psum_scatter(
        partial_sums.astype(jnp.bfloat16), "tp", scatter_dimension=1, tiled=True
    )
    head_count = queries.shape[1] // HS
    score_scale = 1.0 / math.sqrt(HS)
    ctx_rank = lax.axis_index("ctx")
    query_pos = ctx_rank * tok_rows + jnp.arange(tok_rows, dtype=jnp.int32)
    row_spans = ((0, tok_rows),)
    query_heads = queries.reshape(tok_rows, head_count, HS)
    initial = (
        jnp.full((tok_rows, head_count), BIG_NEGATIVE, jnp.float32),
        jnp.zeros((tok_rows, head_count), jnp.float32),
        jnp.zeros((tok_rows, head_count, HS), jnp.float32),
    )
    key_piece = lax.all_gather(keys, "ctx", axis=0, tiled=True)
    value_piece = lax.all_gather(mixed, "ctx", axis=0, tiled=True)
    piece_rows = key_piece.shape[0]
    key_heads = key_piece.reshape(piece_rows, head_count, HS)
    value_heads = value_piece.reshape(piece_rows, head_count, HS)
    key_pos = jnp.arange(piece_rows, dtype=jnp.int32)
    span_start, span_stop = row_spans[0]
    sub_state = (initial[0], initial[1], initial[2])

    def visit(inner_state, span_start=span_start, span_stop=span_stop):
        return fold_keys(
            inner_state, query_heads, query_pos, key_heads, value_heads, key_pos, score_scale
        )

    def unchanged(inner_state):
        return inner_state

    sub_state = lax.cond(jnp.int32(0) <= query_pos[span_stop - 1], visit, unchanged, sub_state)
    span_states = [sub_state]
    top_score, weight_sum, weighted = tuple(
        (
            jnp.concatenate([group_state[member_index] for group_state in span_states], axis=0)
            for member_index in range(3)
        )
    )
    outcome = (
        (weighted / weight_sum[:, :, None]).reshape(tok_rows, head_count * HS).astype(jnp.bfloat16)
    )
    return (mixed, outcome)


def solution(mesh):
    return jax.shard_map(
        per_device,
        mesh=mesh,
        in_specs=(
            P("ctx", "tp"),
            P("ctx", "tp"),
            P("ctx", "tp"),
            P("ctx", "tp"),
            P("tp"),
            P("tp", None),
            P("ctx", "tp"),
            P("ctx", "tp"),
        ),
        out_specs=(P("ctx", "tp"), P("ctx", "tp")),
        check_vma=False,
    )
```

```python
import functools
import math

import jax
import jax.numpy as jnp
import numpy as np
from jax import lax
from jax.experimental import pallas as pl
from jax.experimental.pallas import tpu as pltpu
from jax.sharding import PartitionSpec as P

HS = 128
MESH = pl.DeviceIdType.MESH
BF = jnp.bfloat16
F32 = jnp.float32
CTX = 32
ROWS = 256
GROUP = 16
TOTAL = CTX * ROWS


def nt(a, b):
    return lax.dot_general(a, b, (((1,), (1,)), ((), ())), preferred_element_type=F32)


def nn(a, b):
    return jnp.dot(a, b, preferred_element_type=F32)


def tables():
    r = np.arange(CTX, dtype=np.float64)
    q = np.arange(CTX, dtype=np.float64)
    a = np.arange(ROWS, dtype=np.float64)
    rows = np.exp(-2j * np.pi * np.outer(q + 0.25, r) / CTX)
    turn = np.exp(-2j * np.pi * np.outer(q + 0.25, a) / TOTAL)
    cols = np.exp(-2j * np.pi * np.outer(a, a) / ROWS)
    eye = np.eye(GROUP)
    spread = lambda m: np.einsum("qr,cd->cqrd", m, eye).reshape(GROUP * CTX, CTX * GROUP)
    first = np.concatenate([spread(rows.real), spread(rows.imag)], axis=0)
    back = np.conj(rows).T
    gather = lambda m: np.einsum("rq,cd->rcdq", m, eye).reshape(CTX * GROUP, GROUP * CTX)
    last = np.concatenate([gather(back.real), -gather(back.imag)], axis=1)
    mix = np.block([[cols.real, cols.imag], [-cols.imag, cols.real]])
    unmix = np.block([[cols.real, -cols.imag], [cols.imag, cols.real]]) / TOTAL
    cast = lambda m: np.asarray(m, np.float32).astype(jnp.bfloat16)
    return (cast(first), cast(mix), cast(unmix), cast(last),
            np.asarray(turn.real, np.float32), np.asarray(turn.imag, np.float32))


def spectrum(x, first, mix, turn_re, turn_im):
    half = GROUP * CTX
    a = nn(first, x)
    a_re = a[:half].reshape(GROUP, CTX, ROWS)
    a_im = a[half:].reshape(GROUP, CTX, ROWS)
    z_re = (a_re * turn_re - a_im * turn_im).reshape(half, ROWS).astype(BF)
    z_im = (a_re * turn_im + a_im * turn_re).reshape(half, ROWS).astype(BF)
    return nn(jnp.concatenate([z_re, z_im], axis=1), mix)


def filter_kernel(
    first_ref, value_ref, taps_ref, second_ref, skip_ref, eye_ref, first_t, mix_t, unmix_t, last_t,
    turn_re, turn_im, gated_ref, product, send, recv, out_send, out_recv,
    send_sem, recv_sem, back_send_sem, back_recv_sem,
):
    me = lax.axis_index("ctx")
    half = GROUP * CTX
    barrier = pltpu.get_barrier_semaphore()

    def greet(k, carry):
        pl.semaphore_signal(
            barrier, inc=1, device_id={"ctx": lax.rem(me + k, CTX)}, device_id_type=MESH
        )
        return carry

    lax.fori_loop(1, CTX, greet, 0)
    eye = eye_ref[...]
    for cb in range(4):
        cols = slice(cb * 256, (cb + 1) * 256)
        prod = (first_ref[:, cols].astype(F32) * value_ref[:, cols].astype(F32)).astype(BF)
        product[:, cols] = prod
        for kind, block in ((0, prod), (1, taps_ref[:, cols])):
            turned = nt(eye, block).astype(BF)
            for dl in range(8):
                for h in range(2):
                    at = dl * 32 + h * GROUP
                    send[h, cb * 8 + dl, kind] = turned[at:at + GROUP]
    pl.semaphore_wait(barrier, CTX - 1)

    for h in range(2):
        def post(k, carry, h=h):
            to = lax.rem(me + k, CTX)
            pltpu.make_async_remote_copy(
                src_ref=send.at[h, to], dst_ref=recv.at[h, me],
                send_sem=send_sem.at[h], recv_sem=recv_sem.at[h],
                device_id={"ctx": to}, device_id_type=MESH,
            ).start()
            return carry

        pltpu.make_async_copy(send.at[h, me], recv.at[h, me], recv_sem.at[h]).start()
        lax.fori_loop(1, CTX, post, 0)

    for h in range(2):
        pltpu.make_async_copy(recv.at[h], recv.at[h], recv_sem.at[h]).wait()
        tr, ti = turn_re[...], turn_im[...]
        x = recv[h, :, 0].reshape(half, ROWS)
        w = recv[h, :, 1].reshape(half, ROWS)
        d = spectrum(x, first_t[...], mix_t[...], tr, ti)
        e = spectrum(w, first_t[...], mix_t[...], tr, ti)
        d_re, d_im, e_re, e_im = d[:, :ROWS], d[:, ROWS:], e[:, :ROWS], e[:, ROWS:]
        y_re = (d_re * e_re - d_im * e_im).astype(BF)
        y_im = (d_re * e_im + d_im * e_re).astype(BF)
        b = nn(jnp.concatenate([y_re, y_im], axis=1), unmix_t[...])
        b_re = b[:, :ROWS].reshape(GROUP, CTX, ROWS)
        b_im = b[:, ROWS:].reshape(GROUP, CTX, ROWS)
        c_re = (b_re * tr + b_im * ti).reshape(half, ROWS).astype(BF)
        c_im = (b_im * tr - b_re * ti).reshape(half, ROWS).astype(BF)
        y = nn(last_t[...], jnp.concatenate([c_re, c_im], axis=0))
        out_send[h] = y.astype(BF).reshape(CTX, GROUP, ROWS)

        def reply(k, carry, h=h):
            to = lax.rem(me + k, CTX)
            pltpu.make_async_remote_copy(
                src_ref=out_send.at[h, to], dst_ref=out_recv.at[h, me],
                send_sem=back_send_sem.at[h], recv_sem=back_recv_sem.at[h],
                device_id={"ctx": to}, device_id_type=MESH,
            ).start()
            return carry

        pltpu.make_async_copy(out_send.at[h, me], out_recv.at[h, me], back_recv_sem.at[h]).start()
        lax.fori_loop(1, CTX, reply, 0)

    for h in range(2):
        sent = send.at[h, pl.ds(0, CTX - 1)]
        pltpu.make_async_copy(sent, sent, send_sem.at[h]).wait()
    for h in range(2):
        pltpu.make_async_copy(out_recv.at[h], out_recv.at[h], back_recv_sem.at[h]).wait()
        sent = out_send.at[h, pl.ds(0, CTX - 1)]
        pltpu.make_async_copy(sent, sent, back_send_sem.at[h]).wait()
    for cb in range(4):
        cols = slice(cb * 256, (cb + 1) * 256)
        parts = [out_recv[h, cb * 8 + dl] for dl in range(8) for h in range(2)]
        filtered = nt(eye, jnp.concatenate(parts, axis=0)).astype(BF).astype(F32)
        prod = product[:, cols].astype(F32)
        gated_ref[:, cols] = (
            second_ref[:, cols].astype(F32) * (filtered + skip_ref[:, cols] * prod)
        ).astype(BF)


def vmem(count):
    return [pl.BlockSpec(memory_space=pltpu.VMEM)] * count


def filtered_and_gated(first_input, value_input, filter_taps, second_input, skip_gain):
    first, mix, unmix, last, turn_re, turn_im = (jnp.asarray(t) for t in tables())
    eye = jnp.eye(ROWS, dtype=BF)
    return pl.pallas_call(
        filter_kernel,
        out_shape=jax.ShapeDtypeStruct((ROWS, 1024), BF),
        in_specs=vmem(12),
        out_specs=pl.BlockSpec(memory_space=pltpu.VMEM),
        scratch_shapes=[
            pltpu.VMEM((ROWS, 1024), BF),
            pltpu.VMEM((2, CTX, 2, GROUP, ROWS), BF),
            pltpu.VMEM((2, CTX, 2, GROUP, ROWS), BF),
            pltpu.VMEM((2, CTX, GROUP, ROWS), BF),
            pltpu.VMEM((2, CTX, GROUP, ROWS), BF),
            pltpu.SemaphoreType.DMA((2,)),
            pltpu.SemaphoreType.DMA((2,)),
            pltpu.SemaphoreType.DMA((2,)),
            pltpu.SemaphoreType.DMA((2,)),
        ],
        compiler_params=pltpu.CompilerParams(
            collective_id=0, has_side_effects=True, vmem_limit_bytes=40 * 1024 * 1024
        ),
        name="filter_and_gate",
    )(first_input, value_input, filter_taps, second_input, skip_gain.reshape(1, 1024), eye,
      first, mix, unmix, last, turn_re, turn_im)


XS, ZS, YS = 4, 8, 4
HEAD = 512
KEYS = 512
NEG = -1e30


class Spread:
    def __init__(self, place, buf, z_send, own, left, right, far, sib, sent):
        self.x, self.z, self.y, self.c = place
        self.buf, self.z_send, self.own, self.left, self.right, self.far, self.sib, self.sent = (
            buf, z_send, own, left, right, far, sib, sent
        )
        self.xl, self.xr, self.x2 = (lax.rem(self.x + k, XS) for k in (3, 1, 2))

    def device(self, x, z, c):
        return {"ctx": x * ZS + z, "tp": self.y * 2 + c}

    def scatter(self, source, start):
        x, z, c = self.x, self.z, self.c
        core, i = lax.rem(z, 2), lax.div(z, 2)
        for j in range(4):
            to = 4 * c + j
            alone = (to == z) & (core == c)
            part = source.at[:, pl.ds(j * HS, HS)]
            slot = self.buf.at[x, z]
            local = pltpu.make_async_copy(part, slot, self.own.at[i])
            away = pltpu.make_async_remote_copy(
                src_ref=part, dst_ref=slot, send_sem=self.z_send.at[j], recv_sem=self.own.at[i],
                device_id=self.device(x, to, core), device_id_type=MESH,
            )
            if start:
                pl.when(alone)(local.start)
                pl.when(jnp.logical_not(alone))(away.start)
            else:
                pl.when(jnp.logical_not(alone))(away.wait_send)

    def push(self, block, i, x, c, sem):
        pltpu.make_async_remote_copy(
            src_ref=block, dst_ref=block, send_sem=self.sent.at[i], recv_sem=sem,
            device_id=self.device(x, self.z, c), device_id_type=MESH,
        ).start()

    def arrived(self, block, sem):
        pltpu.make_async_copy(block, block, sem).wait()

    def step_own(self, i):
        block = self.buf.at[self.x, 2 * i + self.c]
        self.arrived(block, self.own.at[i])
        self.push(block, i, self.xr, self.c, self.left.at[i])
        self.push(block, i, self.xl, self.c, self.right.at[i])
        self.push(block, i, self.x, 1 - self.c, self.sib.at[i])

    def step_near(self, i):
        zi = 2 * i + self.c
        block = self.buf.at[self.xl, zi]
        self.arrived(block, self.left.at[i])
        half = self.buf.at[self.xl, zi, pl.ds(0, 128)]
        self.push(half, i, self.xr, self.c, self.far.at[0, i])
        self.push(block, i, self.x, 1 - self.c, self.sib.at[i])
        block = self.buf.at[self.xr, zi]
        self.arrived(block, self.right.at[i])
        half = self.buf.at[self.xr, zi, pl.ds(128, 128)]
        self.push(half, i, self.xl, self.c, self.far.at[1, i])
        self.push(block, i, self.x, 1 - self.c, self.sib.at[i])

    def step_far(self, i):
        for h in range(2):
            half = self.buf.at[self.x2, 2 * i + self.c, pl.ds(h * 128, 128)]
            self.arrived(half, self.far.at[h, i])
            self.push(half, i, self.x, 1 - self.c, self.sib.at[i])

    def finish(self, i):
        blocks = self.buf.at[:, 2 * i + 1 - self.c]
        self.arrived(blocks, self.sib.at[i])
        some = self.buf.at[0, pl.ds(0, 7)]
        self.arrived(some, self.sent.at[i])


def attend_kernel(
    gated_ref, weight_ref, queries_ref, keys_ref, mixed_ref, attended_ref,
    weights, own_part, sib_send, sib_recv, y_send, y_recv, near_send, near_recv, mine,
    k_buf, v_buf, q_buf, scores, rounded, totals, o_send, o_recv,
    w_sem, sib_send_sem, sib_recv_sem, y_send_sem, y_recv_sem, near_send_sem, near_recv_sem,
    q_send_sem, q_recv_sem, o_send_sem, o_recv_sem,
    kz, k_own, k_left, k_right, k_far, k_sib, k_sent,
    vz, v_own, v_left, v_right, v_far, v_sib, v_sent,
):
    ctx, tp = lax.axis_index("ctx"), lax.axis_index("tp")
    x, z = lax.div(ctx, ZS), lax.rem(ctx, ZS)
    y, c = lax.div(tp, 2), lax.rem(tp, 2)
    place = (x, z, y, c)
    keys_of = Spread(place, k_buf, kz, k_own, k_left, k_right, k_far, k_sib, k_sent)
    values_of = Spread(place, v_buf, vz, v_own, v_left, v_right, v_far, v_sib, v_sent)
    barrier = pltpu.get_barrier_semaphore()

    def greet(to_ctx, to_tp):
        pl.semaphore_signal(
            barrier, inc=1, device_id={"ctx": to_ctx, "tp": to_tp}, device_id_type=MESH
        )

    for k in range(1, ZS):
        to = x * ZS + lax.rem(z + k, ZS)
        greet(to, tp)
        greet(to, y * 2 + 1 - c)
    greet(ctx, y * 2 + 1 - c)
    for k in (1, 3):
        greet(lax.rem(x + k, XS) * ZS + z, tp)
        greet(ctx, lax.rem(y + k, YS) * 2 + c)

    order = [(other, lax.rem(y + k, YS)) for other in (1, 0) for k in (2, 1, 3, 0)]
    loads = []
    for k, (other, to_y) in enumerate(order):
        col = to_y * 2 + (1 - c if other else c)
        loads.append(pltpu.make_async_copy(
            weight_ref.at[:, pl.ds(pl.multiple_of(col * HEAD, HEAD), HEAD)], weights.at[k], w_sem.at[k]
        ))
        loads[-1].start()
    pl.semaphore_wait(barrier, 2 * (ZS - 1) + 1 + 4)

    keys_of.scatter(keys_ref, True)
    q_core = lax.rem(lax.div(z + 1, 2), 2)

    def query_copies(j):
        to = 4 * c + j
        alone = (to == z) & (q_core == c)
        part = queries_ref.at[:, pl.ds(j * HS, HS)]
        slot = q_buf.at[lax.div(z, 2)]
        sem = q_recv_sem.at[lax.div(z, 2)]
        return alone, pltpu.make_async_copy(part, slot, sem), pltpu.make_async_remote_copy(
            src_ref=part, dst_ref=slot, send_sem=q_send_sem.at[j], recv_sem=sem,
            device_id={"ctx": x * ZS + to, "tp": y * 2 + q_core}, device_id_type=MESH,
        )

    for j in range(4):
        alone, local, away = query_copies(j)
        pl.when(alone)(local.start)
        pl.when(jnp.logical_not(alone))(away.start)

    gated = gated_ref[...]
    swaps = []
    for k in range(4):
        loads[k].wait()
        sib_send[k] = nn(gated, weights[k]).astype(BF)
        swaps.append(pltpu.make_async_remote_copy(
            src_ref=sib_send.at[k], dst_ref=sib_recv.at[k],
            send_sem=sib_send_sem.at[k], recv_sem=sib_recv_sem.at[k],
            device_id={"tp": y * 2 + 1 - c}, device_id_type=MESH,
        ))
        swaps[-1].start()
    for i in range(4):
        keys_of.step_own(i)
    for k in range(4):
        loads[4 + k].wait()
        own_part[k] = nn(gated, weights[4 + k])
    for i in range(4):
        keys_of.step_near(i)

    def chip_sum(k):
        swaps[k].wait_recv()
        return own_part[k] + sib_recv[k].astype(F32)

    right, left = lax.rem(y + 1, YS) * 2 + c, lax.rem(y + 3, YS) * 2 + c
    far = chip_sum(0).astype(BF)
    hops = []
    for h, to in ((0, right), (1, left)):
        y_send[h] = far[:, h * 256:(h + 1) * 256]
        hops.append(pltpu.make_async_remote_copy(
            src_ref=y_send.at[h], dst_ref=y_recv.at[h],
            send_sem=y_send_sem.at[h], recv_sem=y_recv_sem.at[h],
            device_id={"tp": to}, device_id_type=MESH,
        ))
        hops[-1].start()
    for k in range(1, 4):
        own_part[k] = chip_sum(k)
    for i in range(4):
        keys_of.step_far(i)
    for h, to in ((0, right), (1, left)):
        hops[h].wait_recv()
        cols = pl.ds(h * 256, 256)
        own_part[1 + h, :, cols] += y_recv[h].astype(F32)
        near_send[h] = own_part[1 + h].astype(BF)
        hops.append(pltpu.make_async_remote_copy(
            src_ref=near_send.at[h], dst_ref=near_recv.at[h],
            send_sem=near_send_sem.at[h], recv_sem=near_recv_sem.at[h],
            device_id={"tp": to}, device_id_type=MESH,
        ))
        hops[-1].start()
    for i in range(4):
        keys_of.finish(i)
    for h in range(2):
        hops[2 + h].wait_recv()
    mixed = (own_part[3] + near_recv[0].astype(F32) + near_recv[1].astype(F32)).astype(BF)
    mine[...] = mixed
    values_of.scatter(mine, True)
    mixed_ref[...] = mixed

    scale = 1.0 / math.sqrt(HS) * math.log2(math.e)

    def block_of(i):
        zq = 2 * i + (c if i % 2 == 0 else 1 - c)
        rank = x * ZS + zq
        return zq, rank, lax.div(rank, 2)

    def chunk(buf, step):
        return buf[lax.div(step, 4), pl.ds(lax.rem(step, 4) * 2, 2)].reshape(KEYS, HS)

    def fold(op, top, s):
        for at in range(0, KEYS, 128):
            top = op(top, s[:, at:at + 128])
        return top

    def weigh(i):
        zq, rank, last = block_of(i)
        pltpu.make_async_copy(q_buf.at[i], q_buf.at[i], q_recv_sem.at[i]).wait()
        query = q_buf[i]

        def score(step, top):
            s = nt(query, chunk(k_buf, step))
            scores[:, pl.ds(pl.multiple_of(step * KEYS, KEYS), KEYS)] = s
            return fold(jnp.maximum, top, s)

        top = lax.fori_loop(0, last, score, jnp.full((ROWS, 128), NEG, F32))
        s = nt(query, chunk(k_buf, last))
        key_pos = lax.broadcasted_iota(jnp.int32, (ROWS, KEYS), 1) + last * KEYS
        query_pos = lax.broadcasted_iota(jnp.int32, (ROWS, KEYS), 0) + rank * ROWS
        s = jnp.where(key_pos <= query_pos, s, NEG)
        scores[:, pl.ds(pl.multiple_of(last * KEYS, KEYS), KEYS)] = s
        top = jnp.max(fold(jnp.maximum, top, s), axis=1, keepdims=True)

        def weight(step, total):
            cols = pl.ds(pl.multiple_of(step * KEYS, KEYS), KEYS)
            w = jnp.exp2((scores[:, cols] - top) * scale)
            rounded[i, :, cols] = w.astype(BF)
            return fold(jnp.add, total, w)

        total = lax.fori_loop(0, last + 1, weight, jnp.zeros((ROWS, 128), F32))
        totals[i] = jnp.broadcast_to(jnp.sum(total, axis=1, keepdims=True), (ROWS, 128))

    weigh(0)
    for i in range(4):
        values_of.step_own(i)
    weigh(1)
    for i in range(4):
        values_of.step_near(i)
    weigh(2)
    for i in range(4):
        values_of.step_far(i)
    weigh(3)
    for i in range(4):
        values_of.finish(i)

    def output_copies(i):
        zq, rank, last = block_of(i)
        core, j = lax.div(z, 4), lax.rem(z, 4)
        alone = (zq == z) & (core == c)
        return alone, pltpu.make_async_copy(
            o_send.at[i], o_recv.at[j], o_recv_sem.at[j]
        ), pltpu.make_async_remote_copy(
            src_ref=o_send.at[i], dst_ref=o_recv.at[j],
            send_sem=o_send_sem.at[i], recv_sem=o_recv_sem.at[j],
            device_id={"ctx": x * ZS + zq, "tp": y * 2 + core}, device_id_type=MESH,
        )

    for i in range(4):
        zq, rank, last = block_of(i)

        def value(step, acc, i=i):
            cols = pl.ds(pl.multiple_of(step * KEYS, KEYS), KEYS)
            return acc + nn(rounded[i, :, cols], chunk(v_buf, step))

        acc = lax.fori_loop(0, last + 1, value, jnp.zeros((ROWS, HS), F32))
        o_send[i] = (acc / totals[i]).astype(BF)
        alone, local, away = output_copies(i)
        pl.when(alone)(local.start)
        pl.when(jnp.logical_not(alone))(away.start)

    keys_of.scatter(keys_ref, False)
    values_of.scatter(mine, False)
    for j in range(4):
        alone, local, away = query_copies(j)
        pl.when(jnp.logical_not(alone))(away.wait_send)
        swaps[j].wait_send()
        hops[j].wait_send()
    for j in range(4):
        pltpu.make_async_copy(o_recv.at[j], o_recv.at[j], o_recv_sem.at[j]).wait()
        attended_ref[:, j * HS:(j + 1) * HS] = o_recv[j]
    for i in range(4):
        alone, local, away = output_copies(i)
        pl.when(jnp.logical_not(alone))(away.wait_send)


def project_and_attend(gated, out_weight, queries, keys):
    dma = lambda *shape: pltpu.SemaphoreType.DMA(shape)
    spread = [dma(4), dma(4), dma(4), dma(4), dma(2, 4), dma(4), dma(4)]
    out = jax.ShapeDtypeStruct((ROWS, HEAD), BF)
    return pl.pallas_call(
        attend_kernel,
        out_shape=(out, out),
        in_specs=[pl.BlockSpec(memory_space=pltpu.VMEM)] + [pl.BlockSpec(memory_space=pl.ANY)] * 3,
        out_specs=tuple(vmem(2)),
        scratch_shapes=[
            pltpu.VMEM((8, 1024, HEAD), BF),
            pltpu.VMEM((4, ROWS, HEAD), F32),
            pltpu.VMEM((4, ROWS, HEAD), BF),
            pltpu.VMEM((4, ROWS, HEAD), BF),
            pltpu.VMEM((2, ROWS, 256), BF),
            pltpu.VMEM((2, ROWS, 256), BF),
            pltpu.VMEM((2, ROWS, HEAD), BF),
            pltpu.VMEM((2, ROWS, HEAD), BF),
            pltpu.VMEM((ROWS, HEAD), BF),
            pltpu.VMEM((XS, ZS, ROWS, HS), BF),
            pltpu.VMEM((XS, ZS, ROWS, HS), BF),
            pltpu.VMEM((4, ROWS, HS), BF),
            pltpu.VMEM((ROWS, TOTAL), F32),
            pltpu.VMEM((4, ROWS, TOTAL), BF),
            pltpu.VMEM((4, ROWS, 128), F32),
            pltpu.VMEM((4, ROWS, HS), BF),
            pltpu.VMEM((4, ROWS, HS), BF),
            dma(8), dma(4), dma(4), dma(2), dma(2), dma(2), dma(2),
            dma(4), dma(4), dma(4), dma(4),
        ] + spread + spread,
        compiler_params=pltpu.CompilerParams(
            collective_id=1, has_side_effects=True, vmem_limit_bytes=56 * 1024 * 1024
        ),
        name="project_and_attend",
    )(gated, out_weight, queries, keys)


def per_device(
    first_input, second_input, value_input, filter_taps, skip_gain, out_weight, queries, keys
):
    gated = filtered_and_gated(first_input, value_input, filter_taps, second_input, skip_gain)
    return project_and_attend(gated, out_weight, queries, keys)


def solution(mesh):
    return jax.shard_map(
        per_device,
        mesh=mesh,
        in_specs=(
            P("ctx", "tp"),
            P("ctx", "tp"),
            P("ctx", "tp"),
            P("ctx", "tp"),
            P("tp"),
            P("tp", None),
            P("ctx", "tp"),
            P("ctx", "tp"),
        ),
        out_specs=(P("ctx", "tp"), P("ctx", "tp")),
        check_vma=False,
    )
```

```python
import functools
import math

import jax
import jax.numpy as jnp
import numpy as np
from jax import lax
from jax.experimental import pallas as pl
from jax.experimental.pallas import tpu as pltpu
from jax.sharding import PartitionSpec as P

HS = 128
MESH = pl.DeviceIdType.MESH
BF = jnp.bfloat16
F32 = jnp.float32
CTX = 32
ROWS = 256
GROUP = 16
TOTAL = CTX * ROWS


def nt(a, b):
    return lax.dot_general(a, b, (((1,), (1,)), ((), ())), preferred_element_type=F32)


def nn(a, b):
    return jnp.dot(a, b, preferred_element_type=F32)


def tables():
    r = np.arange(CTX, dtype=np.float64)
    q = np.arange(CTX, dtype=np.float64)
    a = np.arange(ROWS, dtype=np.float64)
    rows = np.exp(-2j * np.pi * np.outer(q + 0.25, r) / CTX)
    turn = np.exp(-2j * np.pi * np.outer(q + 0.25, a) / TOTAL)
    cols = np.exp(-2j * np.pi * np.outer(a, a) / ROWS)
    eye = np.eye(GROUP)
    spread = lambda m: np.einsum("qr,cd->cqrd", m, eye).reshape(GROUP * CTX, CTX * GROUP)
    first = np.concatenate([spread(rows.real), spread(rows.imag)], axis=0)
    back = np.conj(rows).T
    gather = lambda m: np.einsum("rq,cd->rcdq", m, eye).reshape(CTX * GROUP, GROUP * CTX)
    last = np.concatenate([gather(back.real), -gather(back.imag)], axis=1)
    mix = np.block([[cols.real, cols.imag], [-cols.imag, cols.real]])
    unmix = np.block([[cols.real, -cols.imag], [cols.imag, cols.real]]) / TOTAL
    cast = lambda m: np.asarray(m, np.float32).astype(jnp.bfloat16)
    return (cast(first), cast(mix), cast(unmix), cast(last),
            np.asarray(turn.real, np.float32), np.asarray(turn.imag, np.float32))


def spectrum(x, first, mix, turn_re, turn_im):
    half = GROUP * CTX
    a = nn(first, x)
    a_re = a[:half].reshape(GROUP, CTX, ROWS)
    a_im = a[half:].reshape(GROUP, CTX, ROWS)
    z_re = (a_re * turn_re - a_im * turn_im).reshape(half, ROWS).astype(BF)
    z_im = (a_re * turn_im + a_im * turn_re).reshape(half, ROWS).astype(BF)
    return nn(jnp.concatenate([z_re, z_im], axis=1), mix)


XS, ZS, YS = 4, 8, 4
HEAD = 512
KEYS = 512
NEG = -1e30


class Spread:
    def __init__(self, place, buf, z_send, own, left, right, far, sib, sent):
        self.x, self.z, self.y, self.c = place
        self.buf, self.z_send, self.own, self.left, self.right, self.far, self.sib, self.sent = (
            buf, z_send, own, left, right, far, sib, sent
        )
        self.xl, self.xr, self.x2 = (lax.rem(self.x + k, XS) for k in (3, 1, 2))

    def device(self, x, z, c):
        return {"ctx": x * ZS + z, "tp": self.y * 2 + c}

    def scatter(self, source, start):
        x, z, c = self.x, self.z, self.c
        core, i = lax.rem(z, 2), lax.div(z, 2)
        for j in range(4):
            to = 4 * c + j
            alone = (to == z) & (core == c)
            part = source.at[:, pl.ds(j * HS, HS)]
            slot = self.buf.at[x, z]
            local = lambda: pltpu.make_async_copy(part, slot, self.own.at[i])
            away = lambda: pltpu.make_async_remote_copy(
                src_ref=part, dst_ref=slot, send_sem=self.z_send.at[j], recv_sem=self.own.at[i],
                device_id=self.device(x, to, core), device_id_type=MESH,
            )
            if start:
                start_either(alone, local, away)
            else:
                pl.when(jnp.logical_not(alone))(lambda: away().wait_send())

    def push(self, block, i, x, c, sem):
        pltpu.make_async_remote_copy(
            src_ref=block, dst_ref=block, send_sem=self.sent.at[i], recv_sem=sem,
            device_id=self.device(x, self.z, c), device_id_type=MESH,
        ).start()

    def arrived(self, block, sem):
        pltpu.make_async_copy(block, block, sem).wait()

    def step_own(self, i):
        block = self.buf.at[self.x, 2 * i + self.c]
        self.arrived(block, self.own.at[i])
        self.push(block, i, self.xr, self.c, self.left.at[i])
        self.push(block, i, self.xl, self.c, self.right.at[i])
        self.push(block, i, self.x, 1 - self.c, self.sib.at[i])

    def step_near(self, i):
        zi = 2 * i + self.c
        block = self.buf.at[self.xl, zi]
        self.arrived(block, self.left.at[i])
        half = self.buf.at[self.xl, zi, pl.ds(0, 128)]
        self.push(half, i, self.xr, self.c, self.far.at[0, i])
        self.push(block, i, self.x, 1 - self.c, self.sib.at[i])
        block = self.buf.at[self.xr, zi]
        self.arrived(block, self.right.at[i])
        half = self.buf.at[self.xr, zi, pl.ds(128, 128)]
        self.push(half, i, self.xl, self.c, self.far.at[1, i])
        self.push(block, i, self.x, 1 - self.c, self.sib.at[i])

    def step_far(self, i):
        for h in range(2):
            half = self.buf.at[self.x2, 2 * i + self.c, pl.ds(h * 128, 128)]
            self.arrived(half, self.far.at[h, i])
            self.push(half, i, self.x, 1 - self.c, self.sib.at[i])

    def finish(self, i):
        blocks = self.buf.at[:, 2 * i + 1 - self.c]
        self.arrived(blocks, self.sib.at[i])
        some = self.buf.at[0, pl.ds(0, 7)]
        self.arrived(some, self.sent.at[i])

CHUNKS = 36


def whole_kernel(
    first_hbm, second_hbm, value_hbm, taps_hbm, skip_hbm, weight_ref, queries_ref, keys_ref,
    spread_hbm, mix_hbm, unmix_hbm, gather_hbm, turn_hbm, mixed_ref, attended_ref,
    first_in, value_in, taps_in, second_in, skip, spread_t, mix_t, unmix_t, gather_t, turn,
    product, send, recv, out_send, out_recv, gated_ref,
    weights, own_part, sib_send, sib_recv, y_send, y_recv, near_send, near_recv, mine,
    k_buf, v_buf, q_buf, scores, rounded, totals, o_send, o_recv,
    in_sem, table_sem, send_sem, recv_sem, back_send_sem, back_recv_sem,
    w_sem, sib_send_sem, sib_recv_sem, y_send_sem, y_recv_sem, near_send_sem, near_recv_sem,
    q_send_sem, q_recv_sem, o_send_sem, o_recv_sem,
    kz, k_own, k_left, k_right, k_far, k_sib, k_sent,
    vz, v_own, v_left, v_right, v_far, v_sib, v_sent,
):
    me, tp = lax.axis_index("ctx"), lax.axis_index("tp")
    x, z = lax.div(me, ZS), lax.rem(me, ZS)
    y, c = lax.div(tp, 2), lax.rem(tp, 2)
    place = (x, z, y, c)
    keys_of = Spread(place, k_buf, kz, k_own, k_left, k_right, k_far, k_sib, k_sent)
    values_of = Spread(place, v_buf, vz, v_own, v_left, v_right, v_far, v_sib, v_sent)
    mirror = XS - 1 - x
    half = GROUP * CTX

    line = [lax.rem(x + s, XS) for s in range(4)]
    cols_of = [pl.ds(pl.multiple_of(at * 256, 256), 256) for at in line]
    inputs = []
    for s in range(4):
        for k, (hbm, into) in enumerate(
            ((taps_hbm, taps_in), (first_hbm, first_in), (value_hbm, value_in))
        ):
            inputs.append(pltpu.make_async_copy(hbm.at[:, cols_of[s]], into.at[s], in_sem.at[k, s]))
            inputs[-1].start()

    barrier = pltpu.get_barrier_semaphore()

    def greet(to_ctx, to_tp):
        pl.semaphore_signal(
            barrier, inc=1, device_id={"ctx": to_ctx, "tp": to_tp}, device_id_type=MESH
        )

    def greet_group(k, carry):
        greet(lax.rem(me + k, CTX), tp)
        return carry

    def greet_rows(k, carry):
        greet(x * ZS + k, y * 2 + 1 - c)
        greet(mirror * ZS + k, y * 2 + 1 - c)
        return carry

    lax.fori_loop(1, CTX, greet_group, 0)
    lax.fori_loop(0, ZS, greet_rows, 0)
    for k in (1, 3):
        greet(me, lax.rem(y + k, YS) * 2 + c)

    tables_in = []
    for k, (hbm, into) in enumerate((
        (spread_hbm, spread_t), (turn_hbm, turn), (mix_hbm, mix_t), (unmix_hbm, unmix_t),
        (gather_hbm, gather_t), (skip_hbm, skip),
    )):
        tables_in.append(pltpu.make_async_copy(hbm, into, table_sem.at[k]))
        tables_in[-1].start()
    gates_in = []
    for s in range(4):
        gates_in.append(
            pltpu.make_async_copy(second_hbm.at[:, cols_of[s]], second_in.at[s], in_sem.at[3, s])
        )
        gates_in[-1].start()

    def post(h, s, k):
        zt = lax.rem(z + k, ZS)
        pltpu.make_async_remote_copy(
            src_ref=send.at[h, s, zt], dst_ref=recv.at[h, me],
            send_sem=send_sem.at[h], recv_sem=recv_sem.at[h],
            device_id={"ctx": line[s] * ZS + zt}, device_id_type=MESH,
        ).start()

    def post_line(h, s):
        def one(k, carry):
            post(h, s, k)
            return carry

        if s == 0:
            pltpu.make_async_copy(send.at[h, 0, z], recv.at[h, me], recv_sem.at[h]).start()
        lax.fori_loop(1 if s == 0 else 0, ZS, one, 0)

    def same(rows):
        down = lax.broadcasted_iota(jnp.int32, (rows, rows), 0)
        across = lax.broadcasted_iota(jnp.int32, (rows, rows), 1)
        return jnp.where(down == across, 1.0, 0.0).astype(BF)

    eye = same(ROWS)
    for s in range(4):
        for copy in inputs[3 * s:3 * s + 3]:
            copy.wait()
        prod = (first_in[s].astype(F32) * value_in[s].astype(F32)).astype(BF)
        product[s] = prod
        for kind, block in ((0, prod), (1, taps_in[s])):
            turned = nt(eye, block).astype(BF)
            for dl in range(8):
                for h in range(2):
                    at = dl * 32 + h * GROUP
                    send[h, s, dl, kind] = turned[at:at + GROUP]
        if s == 0:
            pl.semaphore_wait(barrier, CTX - 1 + 2 * ZS + 2)
        post_line(0, s)
    for s in range(4):
        post_line(1, s)

    order = [(other, lax.rem(y + k, YS)) for other in (1, 0) for k in (2, 1, 3, 0)]
    loads = []
    for k, (other, to_y) in enumerate(order):
        col = to_y * 2 + (1 - c if other else c)
        loads.append(pltpu.make_async_copy(
            weight_ref.at[:, pl.ds(pl.multiple_of(col * HEAD, HEAD), HEAD)], weights.at[k], w_sem.at[k]
        ))
        loads[-1].start()
    for copy in tables_in:
        copy.wait()

    for h in range(2):
        pltpu.make_async_copy(recv.at[h], recv.at[h], recv_sem.at[h]).wait()
        tr, ti = turn[:CTX], turn[CTX:]
        xs = recv[h, :, 0].reshape(half, ROWS)
        ws = recv[h, :, 1].reshape(half, ROWS)
        d = spectrum(xs, spread_t[...], mix_t[...], tr, ti)
        e = spectrum(ws, spread_t[...], mix_t[...], tr, ti)
        d_re, d_im, e_re, e_im = d[:, :ROWS], d[:, ROWS:], e[:, :ROWS], e[:, ROWS:]
        y_re = (d_re * e_re - d_im * e_im).astype(BF)
        y_im = (d_re * e_im + d_im * e_re).astype(BF)
        b = nn(jnp.concatenate([y_re, y_im], axis=1), unmix_t[...])
        b_re = b[:, :ROWS].reshape(GROUP, CTX, ROWS)
        b_im = b[:, ROWS:].reshape(GROUP, CTX, ROWS)
        c_re = (b_re * tr + b_im * ti).reshape(half, ROWS).astype(BF)
        c_im = (b_im * tr - b_re * ti).reshape(half, ROWS).astype(BF)
        out = nn(gather_t[...], jnp.concatenate([c_re, c_im], axis=0))
        out_send[h] = out.astype(BF).reshape(CTX, GROUP, ROWS)

        def reply(k, carry, h=h):
            to = lax.rem(me + k, CTX)
            pltpu.make_async_remote_copy(
                src_ref=out_send.at[h, to], dst_ref=out_recv.at[h, me],
                send_sem=back_send_sem.at[h], recv_sem=back_recv_sem.at[h],
                device_id={"ctx": to}, device_id_type=MESH,
            ).start()
            return carry

        pltpu.make_async_copy(out_send.at[h, me], out_recv.at[h, me], back_recv_sem.at[h]).start()
        lax.fori_loop(1, CTX, reply, 0)

    for copy in gates_in:
        copy.wait()
    for h in range(2):
        pltpu.make_async_copy(out_recv.at[h], out_recv.at[h], back_recv_sem.at[h]).wait()

    keys_of.scatter(keys_ref, True)
    far_pair = lax.min(z, ZS - 1 - z)
    q_x = lax.select(far_pair < 2, x, mirror)
    q_core = lax.rem(far_pair, 2)
    q_slot = lax.div(far_pair, 2) * 2 + lax.div(z, 4)

    def query_copies(j):
        to = 4 * c + j
        alone = (to == z) & (q_core == c) & (far_pair < 2)
        part = queries_ref.at[:, pl.ds(j * HS, HS)]
        slot = q_buf.at[q_slot]
        sem = q_recv_sem.at[q_slot]
        local = lambda: pltpu.make_async_copy(part, slot, sem)
        away = lambda: pltpu.make_async_remote_copy(
            src_ref=part, dst_ref=slot, send_sem=q_send_sem.at[j], recv_sem=sem,
            device_id={"ctx": q_x * ZS + to, "tp": y * 2 + q_core}, device_id_type=MESH,
        )
        return alone, local, away

    for j in range(4):
        start_either(*query_copies(j))

    for s in range(4):
        parts = [out_recv[h, line[s] * 8 + dl] for dl in range(8) for h in range(2)]
        filtered = nt(eye, jnp.concatenate(parts, axis=0)).astype(BF).astype(F32)
        gated_ref[:, cols_of[s]] = (
            second_in[s].astype(F32) * (filtered + skip[:, cols_of[s]] * product[s].astype(F32))
        ).astype(BF)

    gated = gated_ref[...]
    swaps = []
    for k in range(4):
        loads[k].wait()
        sib_send[k] = nn(gated, weights[k]).astype(BF)
        swaps.append(pltpu.make_async_remote_copy(
            src_ref=sib_send.at[k], dst_ref=sib_recv.at[k],
            send_sem=sib_send_sem.at[k], recv_sem=sib_recv_sem.at[k],
            device_id={"tp": y * 2 + 1 - c}, device_id_type=MESH,
        ))
        swaps[-1].start()
    for k in range(4):
        loads[4 + k].wait()
        own_part[k] = nn(gated, weights[4 + k])

    def chip_sum(k):
        swaps[k].wait_recv()
        return own_part[k] + sib_recv[k].astype(F32)

    right, left = lax.rem(y + 1, YS) * 2 + c, lax.rem(y + 3, YS) * 2 + c
    far = chip_sum(0).astype(BF)
    hops = []
    for h, to in ((0, right), (1, left)):
        y_send[h] = far[:, h * 256:(h + 1) * 256]
        hops.append(pltpu.make_async_remote_copy(
            src_ref=y_send.at[h], dst_ref=y_recv.at[h],
            send_sem=y_send_sem.at[h], recv_sem=y_recv_sem.at[h],
            device_id={"tp": to}, device_id_type=MESH,
        ))
        hops[-1].start()
    for k in range(1, 4):
        own_part[k] = chip_sum(k)
    for i in range(4):
        keys_of.step_own(i)
    for h, to in ((0, right), (1, left)):
        hops[h].wait_recv()
        cols = pl.ds(h * 256, 256)
        own_part[1 + h, :, cols] += y_recv[h].astype(F32)
        near_send[h] = own_part[1 + h].astype(BF)
        hops.append(pltpu.make_async_remote_copy(
            src_ref=near_send.at[h], dst_ref=near_recv.at[h],
            send_sem=near_send_sem.at[h], recv_sem=near_recv_sem.at[h],
            device_id={"tp": to}, device_id_type=MESH,
        ))
        hops[-1].start()
    for i in range(4):
        keys_of.step_near(i)
    for h in range(2):
        hops[2 + h].wait_recv()
    mixed = (own_part[3] + near_recv[0].astype(F32) + near_recv[1].astype(F32)).astype(BF)
    mine[...] = mixed
    values_of.scatter(mine, True)
    mixed_ref[...] = mixed
    for i in range(4):
        keys_of.step_far(i)
    for i in range(4):
        keys_of.finish(i)

    scale = 1.0 / math.sqrt(HS) * math.log2(math.e)
    blocks, first_step = [], []
    steps_before = 0
    for i in range(4):
        row = x if i < 2 else mirror
        pair = c + 2 * (i // 2)
        zq = pair if i % 2 == 0 else ZS - 1 - pair
        rank = row * ZS + zq
        blocks.append((row, zq, rank, lax.div(rank, 2)))
        first_step.append(steps_before)
        steps_before = steps_before + lax.div(rank, 2) + 1

    def chunk(buf, step):
        return buf[lax.div(step, 4), pl.ds(lax.rem(step, 4) * 2, 2)].reshape(KEYS, HS)

    def fold(op, top, s):
        for at in range(0, KEYS, 128):
            top = op(top, s[:, at:at + 128])
        return top

    def weigh(i):
        row, zq, rank, last = blocks[i]
        pltpu.make_async_copy(q_buf.at[i], q_buf.at[i], q_recv_sem.at[i]).wait()
        query = q_buf[i]

        def score(step, top):
            s = nt(query, chunk(k_buf, step))
            scores[step] = s
            return fold(jnp.maximum, top, s)

        top = lax.fori_loop(0, last, score, jnp.full((ROWS, 128), NEG, F32))
        s = nt(query, chunk(k_buf, last))
        key_pos = lax.broadcasted_iota(jnp.int32, (ROWS, KEYS), 1) + last * KEYS
        query_pos = lax.broadcasted_iota(jnp.int32, (ROWS, KEYS), 0) + rank * ROWS
        s = jnp.where(key_pos <= query_pos, s, NEG)
        scores[last] = s
        top = jnp.max(fold(jnp.maximum, top, s), axis=1, keepdims=True)

        def weight(step, total):
            w = jnp.exp2((scores[step] - top) * scale)
            rounded[first_step[i] + step] = w.astype(BF)
            return fold(jnp.add, total, w)

        total = lax.fori_loop(0, last + 1, weight, jnp.zeros((ROWS, 128), F32))
        totals[i] = jnp.broadcast_to(jnp.sum(total, axis=1, keepdims=True), (ROWS, 128))

    weigh(0)
    weigh(1)
    for i in range(4):
        values_of.step_own(i)
    weigh(2)
    weigh(3)
    for i in range(4):
        values_of.step_near(i)
    for i in range(4):
        values_of.step_far(i)
    for i in range(4):
        values_of.finish(i)

    def output_copies(i):
        row, zq, rank, last = blocks[i]
        core, j = lax.div(z, 4), lax.rem(z, 4)
        alone = (zq == z) & (core == c) & (row == x)
        local = lambda: pltpu.make_async_copy(o_send.at[i], o_recv.at[j], o_recv_sem.at[j])
        away = lambda: pltpu.make_async_remote_copy(
            src_ref=o_send.at[i], dst_ref=o_recv.at[j],
            send_sem=o_send_sem.at[i], recv_sem=o_recv_sem.at[j],
            device_id={"ctx": row * ZS + zq, "tp": y * 2 + core}, device_id_type=MESH,
        )
        return alone, local, away

    for i in range(4):
        row, zq, rank, last = blocks[i]

        def value(step, acc, i=i):
            return acc + nn(rounded[first_step[i] + step], chunk(v_buf, step))

        acc = lax.fori_loop(0, last + 1, value, jnp.zeros((ROWS, HS), F32))
        o_send[i] = (acc / totals[i]).astype(BF)
        start_either(*output_copies(i))

    for h in range(2):
        some = recv.at[h, pl.ds(0, CTX - 1)]
        pltpu.make_async_copy(some, some, send_sem.at[h]).wait()
        some = out_recv.at[h, pl.ds(0, CTX - 1)]
        pltpu.make_async_copy(some, some, back_send_sem.at[h]).wait()
    keys_of.scatter(keys_ref, False)
    values_of.scatter(mine, False)
    for j in range(4):
        alone, local, away = query_copies(j)
        pl.when(jnp.logical_not(alone))(lambda away=away: away().wait_send())
        swaps[j].wait_send()
        hops[j].wait_send()
    for j in range(4):
        pltpu.make_async_copy(o_recv.at[j], o_recv.at[j], o_recv_sem.at[j]).wait()
        attended_ref[:, j * HS:(j + 1) * HS] = o_recv[j]
    for i in range(4):
        alone, local, away = output_copies(i)
        pl.when(jnp.logical_not(alone))(lambda away=away: away().wait_send())


def start_either(alone, local, away):
    pl.when(alone)(lambda: local().start())
    pl.when(jnp.logical_not(alone))(lambda: away().start())


def vmem(count):
    return [pl.BlockSpec(memory_space=pltpu.VMEM)] * count


def hbm(count):
    return [pl.BlockSpec(memory_space=pl.ANY)] * count


def hand_over(a, b, a_out, b_out, sem):
    copies = [
        pltpu.make_async_copy(a, a_out, sem.at[0]),
        pltpu.make_async_copy(b, b_out, sem.at[1]),
    ]
    for copy in copies:
        copy.start()
    for copy in copies:
        copy.wait()


def per_device(
    first_input, second_input, value_input, filter_taps, skip_gain, out_weight, queries, keys
):
    spread, mix, unmix, gather, turn_re, turn_im = tables()
    consts = [jnp.asarray(t) for t in (spread, mix, unmix, gather, np.concatenate([turn_re, turn_im]))]
    dma = lambda *shape: pltpu.SemaphoreType.DMA(shape)
    bf = lambda *shape: pltpu.VMEM(shape, BF)
    fl = lambda *shape: pltpu.VMEM(shape, F32)
    sems = [dma(4), dma(4), dma(4), dma(4), dma(2, 4), dma(4), dma(4)]
    out = jax.ShapeDtypeStruct((ROWS, HEAD), BF)
    mixed, attended = pl.pallas_call(
        whole_kernel,
        out_shape=(out, out),
        in_specs=hbm(13),
        out_specs=tuple(vmem(2)),
        scratch_shapes=[
            bf(4, ROWS, 256), bf(4, ROWS, 256), bf(4, ROWS, 256), bf(4, ROWS, 256),
            fl(1, 1024), bf(1024, 512), bf(512, 512), bf(512, 512), bf(512, 1024), fl(2 * CTX, ROWS),
            bf(4, ROWS, 256),
            bf(2, 4, 8, 2, GROUP, ROWS), bf(2, CTX, 2, GROUP, ROWS),
            bf(2, CTX, GROUP, ROWS), bf(2, CTX, GROUP, ROWS),
            bf(ROWS, 1024),
            bf(8, 1024, HEAD), fl(4, ROWS, HEAD), bf(4, ROWS, HEAD), bf(4, ROWS, HEAD),
            bf(2, ROWS, 256), bf(2, ROWS, 256), bf(2, ROWS, HEAD), bf(2, ROWS, HEAD), bf(ROWS, HEAD),
            bf(XS, ZS, ROWS, HS), bf(XS, ZS, ROWS, HS), bf(4, ROWS, HS),
            fl(TOTAL // KEYS, ROWS, KEYS), bf(CHUNKS, ROWS, KEYS), fl(4, ROWS, 128),
            bf(4, ROWS, HS), bf(4, ROWS, HS),
            dma(4, 4), dma(6), dma(2), dma(2), dma(2), dma(2),
            dma(8), dma(4), dma(4), dma(2), dma(2), dma(2), dma(2),
            dma(4), dma(4), dma(4), dma(4),
        ] + sems + sems,
        compiler_params=pltpu.CompilerParams(
            collective_id=0, has_side_effects=True, vmem_limit_bytes=60 * 1024 * 1024
        ),
        name="whole",
    )(first_input, second_input, value_input, filter_taps, skip_gain.reshape(1, 1024), out_weight,
      queries, keys, *consts)
    return pl.pallas_call(
        hand_over,
        out_shape=(out, out),
        in_specs=hbm(2),
        out_specs=tuple(hbm(2)),
        scratch_shapes=[dma(2)],
        name="hand_over",
    )(mixed, attended)


def solution(mesh):
    return jax.shard_map(
        per_device,
        mesh=mesh,
        in_specs=(
            P("ctx", "tp"),
            P("ctx", "tp"),
            P("ctx", "tp"),
            P("ctx", "tp"),
            P("tp"),
            P("tp", None),
            P("ctx", "tp"),
            P("ctx", "tp"),
        ),
        out_specs=(P("ctx", "tp"), P("ctx", "tp")),
        check_vma=False,
    )
```

```python
import functools
import math

import jax
import jax.numpy as jnp
import numpy as np
from jax import lax
from jax.experimental import pallas as pl
from jax.experimental.pallas import tpu as pltpu
from jax.sharding import PartitionSpec as P

HS = 128
MESH = pl.DeviceIdType.MESH
BF = jnp.bfloat16
F32 = jnp.float32
CTX = 32
ROWS = 256
GROUP = 16
TOTAL = CTX * ROWS


def nt(a, b):
    return lax.dot_general(a, b, (((1,), (1,)), ((), ())), preferred_element_type=F32)


def nn(a, b):
    return jnp.dot(a, b, preferred_element_type=F32)


def tables():
    r = np.arange(CTX, dtype=np.float64)
    q = np.arange(CTX, dtype=np.float64)
    a = np.arange(ROWS, dtype=np.float64)
    rows = np.exp(-2j * np.pi * np.outer(q + 0.25, r) / CTX)
    turn = np.exp(-2j * np.pi * np.outer(q + 0.25, a) / TOTAL)
    cols = np.exp(-2j * np.pi * np.outer(a, a) / ROWS)
    eye = np.eye(GROUP)
    spread = lambda m: np.einsum("qr,cd->cqrd", m, eye).reshape(GROUP * CTX, CTX * GROUP)
    first = np.concatenate([spread(rows.real), spread(rows.imag)], axis=0)
    back = np.conj(rows).T
    gather = lambda m: np.einsum("rq,cd->rcdq", m, eye).reshape(CTX * GROUP, GROUP * CTX)
    last = np.concatenate([gather(back.real), -gather(back.imag)], axis=1)
    mix = np.block([[cols.real, cols.imag], [-cols.imag, cols.real]])
    unmix = np.block([[cols.real, -cols.imag], [cols.imag, cols.real]]) / TOTAL
    cast = lambda m: np.asarray(m, np.float32).astype(jnp.bfloat16)
    return (cast(first), cast(mix), cast(unmix), cast(last),
            np.asarray(turn.real, np.float32), np.asarray(turn.imag, np.float32))


def spectrum(x, first, mix, turn_re, turn_im):
    half = GROUP * CTX
    a = nn(first, x)
    a_re = a[:half].reshape(GROUP, CTX, ROWS)
    a_im = a[half:].reshape(GROUP, CTX, ROWS)
    z_re = (a_re * turn_re - a_im * turn_im).reshape(half, ROWS).astype(BF)
    z_im = (a_re * turn_im + a_im * turn_re).reshape(half, ROWS).astype(BF)
    return nn(jnp.concatenate([z_re, z_im], axis=1), mix)


XS, ZS, YS = 4, 8, 4
HEAD = 512
KEYS = 512
NEG = -1e30


class Spread:
    def __init__(self, place, buf, parts, z_send, own, left, right, far, sib, sent):
        self.x, self.z, self.y, self.c = place
        self.buf, self.z_send, self.own, self.left, self.right, self.far, self.sib, self.sent = (
            buf, z_send, own, left, right, far, sib, sent
        )
        self.rows = ROWS // parts
        self.xl, self.xr, self.x2 = (lax.rem(self.x + k, XS) for k in (3, 1, 2))

    def device(self, x, z, c):
        return {"ctx": x * ZS + z, "tp": self.y * 2 + c}

    def span(self, p):
        return pl.ds(p * self.rows, self.rows)

    def scatter(self, source, p, start):
        x, z, c = self.x, self.z, self.c
        core = lax.rem(z, 2)
        for j in range(4):
            to = 4 * c + j
            alone = (to == z) & (core == c)
            part = source.at[self.span(p), pl.ds(j * HS, HS)]
            slot = self.buf.at[x, core, lax.div(z, 2), self.span(p)]
            local = lambda: pltpu.make_async_copy(part, slot, self.own.at[p])
            away = lambda: pltpu.make_async_remote_copy(
                src_ref=part, dst_ref=slot, send_sem=self.z_send.at[p, j], recv_sem=self.own.at[p],
                device_id=self.device(x, to, core), device_id_type=MESH,
            )
            if start:
                start_either(alone, local, away)
            else:
                pl.when(jnp.logical_not(alone))(lambda: away().wait_send())

    def push(self, block, p, x, c, sem, late=1):
        pltpu.make_async_remote_copy(
            src_ref=block, dst_ref=block, send_sem=self.sent.at[late, p], recv_sem=sem,
            device_id=self.device(x, self.z, c), device_id_type=MESH,
        ).start()

    def arrived(self, block, sem):
        pltpu.make_async_copy(block, block, sem).wait()

    def step_own(self, p):
        block = self.buf.at[self.x, self.c, :, self.span(p)]
        self.arrived(block, self.own.at[p])
        self.push(block, p, self.xr, self.c, self.left.at[p], 0)
        self.push(block, p, self.xl, self.c, self.right.at[p], 0)
        self.push(block, p, self.x, 1 - self.c, self.sib.at[self.x, p], 0)

    def half(self, x, p, h):
        return self.buf.at[x, self.c, :, pl.ds(p * self.rows + h * (self.rows // 2), self.rows // 2)]

    def step_near(self, p):
        for h, x, on, sem in ((0, self.xl, self.xr, self.left), (1, self.xr, self.xl, self.right)):
            block = self.buf.at[x, self.c, :, self.span(p)]
            self.arrived(block, sem.at[p])
            self.push(self.half(x, p, h), p, on, self.c, self.far.at[h, p])
            self.push(block, p, self.x, 1 - self.c, self.sib.at[x, p])

    def step_far(self, p):
        for h in range(2):
            half = self.half(self.x2, p, h)
            self.arrived(half, self.far.at[h, p])
            self.push(half, p, self.x, 1 - self.c, self.sib.at[self.x2, p])

    def finish(self, p):
        for x in range(XS):
            self.arrived(self.buf.at[x, 1 - self.c, :, self.span(p)], self.sib.at[x, p])

    def drain(self, p):
        self.arrived(self.buf.at[pl.ds(0, 3), 0, :, self.span(p)], self.sent.at[0, p])
        self.arrived(self.buf.at[:, 0, :, self.span(p)], self.sent.at[1, p])


PARTS = 2
CHUNKS = 36


def whole_kernel(
    first_hbm, second_hbm, value_hbm, taps_hbm, skip_hbm, weight_ref, queries_ref, keys_ref,
    spread_hbm, mix_hbm, unmix_hbm, gather_hbm, turn_hbm, mixed_ref, attended_ref,
    first_in, value_in, taps_in, second_in, skip, spread_t, mix_t, unmix_t, gather_t, turn,
    product, send, recv, out_send, out_recv, gated_ref,
    weights, own_part, sib_send, sib_recv, y_send, y_recv, near_send, near_recv, mine,
    k_buf, v_buf, q_buf, scores, rounded, totals, o_send, o_recv,
    in_sem, table_sem, send_sem, recv_sem, back_send_sem, back_recv_sem,
    w_sem, sib_send_sem, sib_recv_sem, y_send_sem, y_recv_sem, near_send_sem, near_recv_sem,
    q_send_sem, q_recv_sem, o_send_sem, o_recv_sem,
    kz, k_own, k_left, k_right, k_far, k_sib, k_sent,
    vz, v_own, v_left, v_right, v_far, v_sib, v_sent,
):
    me, tp = lax.axis_index("ctx"), lax.axis_index("tp")
    x, z = lax.div(me, ZS), lax.rem(me, ZS)
    y, c = lax.div(tp, 2), lax.rem(tp, 2)
    place = (x, z, y, c)
    keys_of = Spread(place, k_buf, 1, kz, k_own, k_left, k_right, k_far, k_sib, k_sent)
    values_of = Spread(place, v_buf, PARTS, vz, v_own, v_left, v_right, v_far, v_sib, v_sent)
    mirror = XS - 1 - x
    half = GROUP * CTX

    line = [lax.rem(x + s, XS) for s in range(4)]
    cols_of = [pl.ds(pl.multiple_of(at * 256, 256), 256) for at in line]
    inputs = []
    for s in range(4):
        for k, (hbm, into) in enumerate(
            ((taps_hbm, taps_in), (first_hbm, first_in), (value_hbm, value_in))
        ):
            inputs.append(pltpu.make_async_copy(hbm.at[:, cols_of[s]], into.at[s], in_sem.at[k, s]))
            inputs[-1].start()

    barrier = pltpu.get_barrier_semaphore()

    def greet(to_ctx, to_tp):
        pl.semaphore_signal(
            barrier, inc=1, device_id={"ctx": to_ctx, "tp": to_tp}, device_id_type=MESH
        )

    def greet_group(k, carry):
        greet(lax.rem(me + k, CTX), tp)
        return carry

    def greet_rows(k, carry):
        greet(x * ZS + k, y * 2 + 1 - c)
        greet(mirror * ZS + k, y * 2 + 1 - c)
        return carry

    lax.fori_loop(1, CTX, greet_group, 0)
    lax.fori_loop(0, ZS, greet_rows, 0)
    for k in (1, 3):
        greet(me, lax.rem(y + k, YS) * 2 + c)

    tables_in = []
    for k, (hbm, into) in enumerate((
        (spread_hbm, spread_t), (turn_hbm, turn), (mix_hbm, mix_t), (unmix_hbm, unmix_t),
        (gather_hbm, gather_t), (skip_hbm, skip),
    )):
        tables_in.append(pltpu.make_async_copy(hbm, into, table_sem.at[k]))
        tables_in[-1].start()
    gates_in = []
    for s in range(4):
        gates_in.append(
            pltpu.make_async_copy(second_hbm.at[:, cols_of[s]], second_in.at[s], in_sem.at[3, s])
        )
        gates_in[-1].start()

    def post(h, s, k):
        zt = lax.rem(z + k, ZS)
        pltpu.make_async_remote_copy(
            src_ref=send.at[h, s, zt], dst_ref=recv.at[h, me],
            send_sem=send_sem.at[h], recv_sem=recv_sem.at[h],
            device_id={"ctx": line[s] * ZS + zt}, device_id_type=MESH,
        ).start()

    def post_line(h, s):
        def one(k, carry):
            post(h, s, k)
            return carry

        if s == 0:
            pltpu.make_async_copy(send.at[h, 0, z], recv.at[h, me], recv_sem.at[h]).start()
        lax.fori_loop(1 if s == 0 else 0, ZS, one, 0)

    def same(rows):
        down = lax.broadcasted_iota(jnp.int32, (rows, rows), 0)
        across = lax.broadcasted_iota(jnp.int32, (rows, rows), 1)
        return jnp.where(down == across, 1.0, 0.0).astype(BF)

    eye = same(ROWS)
    for s in range(4):
        for copy in inputs[3 * s:3 * s + 3]:
            copy.wait()
        prod = (first_in[s].astype(F32) * value_in[s].astype(F32)).astype(BF)
        product[s] = prod
        for kind, block in ((0, prod), (1, taps_in[s])):
            turned = nt(eye, block).astype(BF)
            for dl in range(8):
                for h in range(2):
                    at = h * 128 + dl * GROUP
                    send[h, s, dl, kind] = turned[at:at + GROUP]
        if s == 0:
            pl.semaphore_wait(barrier, CTX - 1 + 2 * ZS + 2)
        post_line(0, s)
    for s in range(4):
        post_line(1, s)
    keys_of.scatter(keys_ref, 0, True)

    order = [(other, lax.rem(y + k, YS)) for other in (1, 0) for k in (2, 1, 3, 0)]
    loads = []
    for k, (other, to_y) in enumerate(order):
        col = to_y * 2 + (1 - c if other else c)
        loads.append(pltpu.make_async_copy(
            weight_ref.at[:, pl.ds(pl.multiple_of(col * HEAD, HEAD), HEAD)], weights.at[k], w_sem.at[k]
        ))
        loads[-1].start()
    for copy in tables_in:
        copy.wait()

    for h in range(2):
        pltpu.make_async_copy(recv.at[h], recv.at[h], recv_sem.at[h]).wait()
        tr, ti = turn[:CTX], turn[CTX:]
        xs = recv[h, :, 0].reshape(half, ROWS)
        ws = recv[h, :, 1].reshape(half, ROWS)
        d = spectrum(xs, spread_t[...], mix_t[...], tr, ti)
        e = spectrum(ws, spread_t[...], mix_t[...], tr, ti)
        d_re, d_im, e_re, e_im = d[:, :ROWS], d[:, ROWS:], e[:, :ROWS], e[:, ROWS:]
        y_re = (d_re * e_re - d_im * e_im).astype(BF)
        y_im = (d_re * e_im + d_im * e_re).astype(BF)
        b = nn(jnp.concatenate([y_re, y_im], axis=1), unmix_t[...])
        b_re = b[:, :ROWS].reshape(GROUP, CTX, ROWS)
        b_im = b[:, ROWS:].reshape(GROUP, CTX, ROWS)
        c_re = (b_re * tr + b_im * ti).reshape(half, ROWS).astype(BF)
        c_im = (b_im * tr - b_re * ti).reshape(half, ROWS).astype(BF)
        out = nn(gather_t[...], jnp.concatenate([c_re, c_im], axis=0))
        out_send[h] = out.astype(BF).reshape(CTX, GROUP, ROWS)

        def reply(k, carry, h=h):
            to = lax.rem(me + k, CTX)
            pltpu.make_async_remote_copy(
                src_ref=out_send.at[h, to], dst_ref=out_recv.at[h, me],
                send_sem=back_send_sem.at[h], recv_sem=back_recv_sem.at[h],
                device_id={"ctx": to}, device_id_type=MESH,
            ).start()
            return carry

        pltpu.make_async_copy(out_send.at[h, me], out_recv.at[h, me], back_recv_sem.at[h]).start()
        lax.fori_loop(1, CTX, reply, 0)
        if h == 0:
            keys_of.step_own(0)
        else:
            keys_of.step_near(0)

    for copy in gates_in:
        copy.wait()
    for h in range(2):
        pltpu.make_async_copy(out_recv.at[h], out_recv.at[h], back_recv_sem.at[h]).wait()
        for s in range(4):
            parts = [out_recv[h, line[s] * 8 + dl] for dl in range(8)]
            filtered = nt(eye, jnp.concatenate(parts, axis=0)).astype(BF).astype(F32)
            lanes = slice(h * 128, (h + 1) * 128)
            cols = pl.ds(pl.multiple_of(line[s] * 256 + h * 128, 128), 128)
            gated_ref[:, cols] = (
                second_in[s, :, lanes].astype(F32)
                * (filtered + skip[:, cols] * product[s, :, lanes].astype(F32))
            ).astype(BF)

    far_pair = lax.min(z, ZS - 1 - z)
    q_x = lax.select(far_pair < 2, x, mirror)
    q_core = lax.rem(far_pair, 2)
    q_slot = lax.div(far_pair, 2) * 2 + lax.div(z, 4)

    def query_copies(j):
        to = 4 * c + j
        alone = (to == z) & (q_core == c) & (far_pair < 2)
        part = queries_ref.at[:, pl.ds(j * HS, HS)]
        slot = q_buf.at[q_slot]
        sem = q_recv_sem.at[q_slot]
        local = lambda: pltpu.make_async_copy(part, slot, sem)
        away = lambda: pltpu.make_async_remote_copy(
            src_ref=part, dst_ref=slot, send_sem=q_send_sem.at[j], recv_sem=sem,
            device_id={"ctx": q_x * ZS + to, "tp": y * 2 + q_core}, device_id_type=MESH,
        )
        return alone, local, away

    for j in range(4):
        start_either(*query_copies(j))

    gated = gated_ref[...]
    swaps = []
    for k in range(4):
        loads[k].wait()
        sib_send[k] = nn(gated, weights[k]).astype(BF)
        swaps.append(pltpu.make_async_remote_copy(
            src_ref=sib_send.at[k], dst_ref=sib_recv.at[k],
            send_sem=sib_send_sem.at[k], recv_sem=sib_recv_sem.at[k],
            device_id={"tp": y * 2 + 1 - c}, device_id_type=MESH,
        ))
        swaps[-1].start()
    for k in range(4):
        loads[4 + k].wait()
        own_part[k] = nn(gated, weights[4 + k])

    def chip_sum(k):
        swaps[k].wait_recv()
        return own_part[k] + sib_recv[k].astype(F32)

    right, left = lax.rem(y + 1, YS) * 2 + c, lax.rem(y + 3, YS) * 2 + c
    depth = ROWS // PARTS
    spans = [pl.ds(p * depth, depth) for p in range(PARTS)]

    def hop(source, into, send_sems, recv_sems, h, p):
        return pltpu.make_async_remote_copy(
            src_ref=source.at[h, spans[p]], dst_ref=into.at[h, spans[p]],
            send_sem=send_sems.at[h, p], recv_sem=recv_sems.at[h, p],
            device_id={"tp": (right, left)[h]}, device_id_type=MESH,
        )

    far = chip_sum(0).astype(BF)
    far_hops, near_hops = {}, {}
    for h in range(2):
        y_send[h] = far[:, h * 256:(h + 1) * 256]
    for p in range(PARTS):
        for h in range(2):
            far_hops[h, p] = hop(y_send, y_recv, y_send_sem, y_recv_sem, h, p)
            far_hops[h, p].start()
    for k in range(1, 4):
        own_part[k] = chip_sum(k)
    keys_of.step_far(0)
    for p in range(PARTS):
        for h in range(2):
            far_hops[h, p].wait_recv()
            own_part[1 + h, spans[p], pl.ds(h * 256, 256)] += y_recv[h, spans[p]].astype(F32)
            near_send[h, spans[p]] = own_part[1 + h, spans[p]].astype(BF)
            near_hops[h, p] = hop(near_send, near_recv, near_send_sem, near_recv_sem, h, p)
            near_hops[h, p].start()
    keys_of.finish(0)

    scale = 1.0 / math.sqrt(HS) * math.log2(math.e)
    blocks, first_step = [], []
    steps_before = 0
    for i in range(4):
        row = x if i < 2 else mirror
        pair = c + 2 * (i // 2)
        zq = pair if i % 2 == 0 else ZS - 1 - pair
        rank = row * ZS + zq
        blocks.append((row, zq, rank, lax.div(rank, 2)))
        first_step.append(steps_before)
        steps_before = steps_before + lax.div(rank, 2) + 1

    def chunk(buf, step):
        row, i = lax.div(step, 4), lax.rem(step, 4)
        return jnp.concatenate([buf[row, 0, i], buf[row, 1, i]], axis=0)

    def fold(op, top, s):
        for at in range(0, KEYS, 128):
            top = op(top, s[:, at:at + 128])
        return top

    def weigh(i):
        row, zq, rank, last = blocks[i]
        pltpu.make_async_copy(q_buf.at[i], q_buf.at[i], q_recv_sem.at[i]).wait()
        query = q_buf[i]

        def score(step, top):
            s = nt(query, chunk(k_buf, step))
            scores[step] = s
            return fold(jnp.maximum, top, s)

        top = lax.fori_loop(0, last, score, jnp.full((ROWS, 128), NEG, F32))
        s = nt(query, chunk(k_buf, last))
        key_pos = lax.broadcasted_iota(jnp.int32, (ROWS, KEYS), 1) + last * KEYS
        query_pos = lax.broadcasted_iota(jnp.int32, (ROWS, KEYS), 0) + rank * ROWS
        s = jnp.where(key_pos <= query_pos, s, NEG)
        scores[last] = s
        top = jnp.max(fold(jnp.maximum, top, s), axis=1, keepdims=True)

        def weight(step, total):
            w = jnp.exp2((scores[step] - top) * scale)
            rounded[first_step[i] + step] = w.astype(BF)
            return fold(jnp.add, total, w)

        total = lax.fori_loop(0, last + 1, weight, jnp.zeros((ROWS, 128), F32))
        totals[i] = jnp.broadcast_to(jnp.sum(total, axis=1, keepdims=True), (ROWS, 128))

    weigh(0)
    for p in range(PARTS):
        for h in range(2):
            near_hops[h, p].wait_recv()
        mixed = (
            own_part[3, spans[p]] + near_recv[0, spans[p]].astype(F32) + near_recv[1, spans[p]].astype(F32)
        ).astype(BF)
        mine[spans[p]] = mixed
        values_of.scatter(mine, p, True)
        mixed_ref[spans[p]] = mixed
    weigh(1)
    values_of.step_own(0)
    weigh(2)
    values_of.step_own(1)
    values_of.step_near(0)
    weigh(3)
    values_of.step_near(1)
    values_of.step_far(0)
    values_of.step_far(1)
    for p in range(PARTS):
        values_of.finish(p)

    def output_copies(i):
        row, zq, rank, last = blocks[i]
        core, j = lax.div(z, 4), lax.rem(z, 4)
        alone = (zq == z) & (core == c) & (row == x)
        local = lambda: pltpu.make_async_copy(o_send.at[i], o_recv.at[j], o_recv_sem.at[j])
        away = lambda: pltpu.make_async_remote_copy(
            src_ref=o_send.at[i], dst_ref=o_recv.at[j],
            send_sem=o_send_sem.at[i], recv_sem=o_recv_sem.at[j],
            device_id={"ctx": row * ZS + zq, "tp": y * 2 + core}, device_id_type=MESH,
        )
        return alone, local, away

    for i in range(4):
        row, zq, rank, last = blocks[i]

        def value(step, acc, i=i):
            return acc + nn(rounded[first_step[i] + step], chunk(v_buf, step))

        acc = lax.fori_loop(0, last + 1, value, jnp.zeros((ROWS, HS), F32))
        o_send[i] = (acc / totals[i]).astype(BF)
        start_either(*output_copies(i))

    for h in range(2):
        some = recv.at[h, pl.ds(0, CTX - 1)]
        pltpu.make_async_copy(some, some, send_sem.at[h]).wait()
        some = out_recv.at[h, pl.ds(0, CTX - 1)]
        pltpu.make_async_copy(some, some, back_send_sem.at[h]).wait()
    keys_of.scatter(keys_ref, 0, False)
    keys_of.drain(0)
    for p in range(PARTS):
        values_of.scatter(mine, p, False)
        values_of.drain(p)
        for h in range(2):
            far_hops[h, p].wait_send()
            near_hops[h, p].wait_send()
    for j in range(4):
        alone, local, away = query_copies(j)
        pl.when(jnp.logical_not(alone))(lambda away=away: away().wait_send())
        swaps[j].wait_send()
    for j in range(4):
        pltpu.make_async_copy(o_recv.at[j], o_recv.at[j], o_recv_sem.at[j]).wait()
        attended_ref[:, j * HS:(j + 1) * HS] = o_recv[j]
    for i in range(4):
        alone, local, away = output_copies(i)
        pl.when(jnp.logical_not(alone))(lambda away=away: away().wait_send())


def start_either(alone, local, away):
    pl.when(alone)(lambda: local().start())
    pl.when(jnp.logical_not(alone))(lambda: away().start())


def vmem(count):
    return [pl.BlockSpec(memory_space=pltpu.VMEM)] * count


def hbm(count):
    return [pl.BlockSpec(memory_space=pl.ANY)] * count


def hand_over(a, b, a_out, b_out):
    a_out[...] = a[...]
    b_out[...] = b[...]


def per_device(
    first_input, second_input, value_input, filter_taps, skip_gain, out_weight, queries, keys
):
    spread, mix, unmix, gather, turn_re, turn_im = tables()
    consts = [jnp.asarray(t) for t in (spread, mix, unmix, gather, np.concatenate([turn_re, turn_im]))]
    dma = lambda *shape: pltpu.SemaphoreType.DMA(shape)
    bf = lambda *shape: pltpu.VMEM(shape, BF)
    fl = lambda *shape: pltpu.VMEM(shape, F32)
    sems = lambda p: [dma(p, 4), dma(p), dma(p), dma(p), dma(2, p), dma(XS, p), dma(2, p)]
    out = jax.ShapeDtypeStruct((ROWS, HEAD), BF)
    mixed, attended = pl.pallas_call(
        whole_kernel,
        out_shape=(out, out),
        in_specs=hbm(13),
        out_specs=tuple(vmem(2)),
        scratch_shapes=[
            bf(4, ROWS, 256), bf(4, ROWS, 256), bf(4, ROWS, 256), bf(4, ROWS, 256),
            fl(1, 1024), bf(1024, 512), bf(512, 512), bf(512, 512), bf(512, 1024), fl(2 * CTX, ROWS),
            bf(4, ROWS, 256),
            bf(2, 4, 8, 2, GROUP, ROWS), bf(2, CTX, 2, GROUP, ROWS),
            bf(2, CTX, GROUP, ROWS), bf(2, CTX, GROUP, ROWS),
            bf(ROWS, 1024),
            bf(8, 1024, HEAD), fl(4, ROWS, HEAD), bf(4, ROWS, HEAD), bf(4, ROWS, HEAD),
            bf(2, ROWS, 256), bf(2, ROWS, 256), bf(2, ROWS, HEAD), bf(2, ROWS, HEAD), bf(ROWS, HEAD),
            bf(XS, 2, ZS // 2, ROWS, HS), bf(XS, 2, ZS // 2, ROWS, HS), bf(4, ROWS, HS),
            fl(TOTAL // KEYS, ROWS, KEYS), bf(CHUNKS, ROWS, KEYS), fl(4, ROWS, 128),
            bf(4, ROWS, HS), bf(4, ROWS, HS),
            dma(4, 4), dma(6), dma(2), dma(2), dma(2), dma(2),
            dma(8), dma(4), dma(4), dma(2, PARTS), dma(2, PARTS), dma(2, PARTS), dma(2, PARTS),
            dma(4), dma(4), dma(4), dma(4),
        ] + sems(1) + sems(PARTS),
        compiler_params=pltpu.CompilerParams(
            collective_id=0, has_side_effects=True, vmem_limit_bytes=60 * 1024 * 1024
        ),
        name="whole",
    )(first_input, second_input, value_input, filter_taps, skip_gain.reshape(1, 1024), out_weight,
      queries, keys, *consts)
    return pl.pallas_call(
        hand_over,
        out_shape=(out, out),
        in_specs=vmem(2),
        out_specs=tuple(vmem(2)),
        name="hand_over",
    )(mixed, attended)


def solution(mesh):
    return jax.shard_map(
        per_device,
        mesh=mesh,
        in_specs=(
            P("ctx", "tp"),
            P("ctx", "tp"),
            P("ctx", "tp"),
            P("ctx", "tp"),
            P("tp"),
            P("tp", None),
            P("ctx", "tp"),
            P("ctx", "tp"),
        ),
        out_specs=(P("ctx", "tp"), P("ctx", "tp")),
        check_vma=False,
    )
```

```python
import functools
import math

import jax
import jax.numpy as jnp
import numpy as np
from jax import lax
from jax.experimental import pallas as pl
from jax.experimental.pallas import tpu as pltpu
from jax.sharding import PartitionSpec as P

HS = 128
MESH = pl.DeviceIdType.MESH
BF = jnp.bfloat16
F32 = jnp.float32
CTX = 32
ROWS = 256
GROUP = 16
TOTAL = CTX * ROWS


def nt(a, b):
    return lax.dot_general(a, b, (((1,), (1,)), ((), ())), preferred_element_type=F32)


def nn(a, b):
    return jnp.dot(a, b, preferred_element_type=F32)


def tables():
    r = np.arange(CTX, dtype=np.float64)
    q = np.arange(CTX, dtype=np.float64)
    a = np.arange(ROWS, dtype=np.float64)
    rows = np.exp(-2j * np.pi * np.outer(q + 0.25, r) / CTX)
    turn = np.exp(-2j * np.pi * np.outer(q + 0.25, a) / TOTAL)
    cols = np.exp(-2j * np.pi * np.outer(a, a) / ROWS)
    eye = np.eye(GROUP)
    spread = lambda m: np.einsum("qr,cd->cqrd", m, eye).reshape(GROUP * CTX, CTX * GROUP)
    first = np.concatenate([spread(rows.real), spread(rows.imag)], axis=0)
    back = np.conj(rows).T
    gather = lambda m: np.einsum("rq,cd->rcdq", m, eye).reshape(CTX * GROUP, GROUP * CTX)
    last = np.concatenate([gather(back.real), -gather(back.imag)], axis=1)
    mix = np.block([[cols.real, cols.imag], [-cols.imag, cols.real]])
    unmix = np.block([[cols.real, -cols.imag], [cols.imag, cols.real]]) / TOTAL
    cast = lambda m: np.asarray(m, np.float32).astype(jnp.bfloat16)
    return (cast(first), cast(mix), cast(unmix), cast(last),
            np.asarray(turn.real, np.float32), np.asarray(turn.imag, np.float32))


def spectrum(x, first, mix, turn_re, turn_im):
    half = GROUP * CTX
    a = nn(first, x)
    a_re = a[:half].reshape(GROUP, CTX, ROWS)
    a_im = a[half:].reshape(GROUP, CTX, ROWS)
    z_re = (a_re * turn_re - a_im * turn_im).reshape(half, ROWS).astype(BF)
    z_im = (a_re * turn_im + a_im * turn_re).reshape(half, ROWS).astype(BF)
    return nn(jnp.concatenate([z_re, z_im], axis=1), mix)


XS, ZS, YS = 4, 8, 4
HEAD = 512
KEYS = 512
NEG = -1e30


class Spread:
    def __init__(self, place, buf, parts, z_send, own, left, right, far, sib, sent):
        self.x, self.z, self.y, self.c = place
        self.buf, self.z_send, self.own, self.left, self.right, self.far, self.sib, self.sent = (
            buf, z_send, own, left, right, far, sib, sent
        )
        self.rows = ROWS // parts
        self.xl, self.xr, self.x2 = (lax.rem(self.x + k, XS) for k in (3, 1, 2))

    def device(self, x, z, c):
        return {"ctx": x * ZS + z, "tp": self.y * 2 + c}

    def span(self, p):
        return pl.ds(p * self.rows, self.rows)

    def scatter(self, source, p, start):
        x, z, c = self.x, self.z, self.c
        core = lax.rem(z, 2)
        for j in range(4):
            to = 4 * c + j
            alone = (to == z) & (core == c)
            part = source.at[self.span(p), pl.ds(j * HS, HS)]
            slot = self.buf.at[x, core, lax.div(z, 2), self.span(p)]
            local = lambda: pltpu.make_async_copy(part, slot, self.own.at[p])
            away = lambda: pltpu.make_async_remote_copy(
                src_ref=part, dst_ref=slot, send_sem=self.z_send.at[p, j], recv_sem=self.own.at[p],
                device_id=self.device(x, to, core), device_id_type=MESH,
            )
            if start:
                start_either(alone, local, away)
            else:
                pl.when(jnp.logical_not(alone))(lambda: away().wait_send())

    def push(self, block, p, x, c, sem, late=1):
        pltpu.make_async_remote_copy(
            src_ref=block, dst_ref=block, send_sem=self.sent.at[late, p], recv_sem=sem,
            device_id=self.device(x, self.z, c), device_id_type=MESH,
        ).start()

    def arrived(self, block, sem):
        pltpu.make_async_copy(block, block, sem).wait()

    def step_own(self, p):
        block = self.buf.at[self.x, self.c, :, self.span(p)]
        self.arrived(block, self.own.at[p])
        self.push(block, p, self.xr, self.c, self.left.at[p], 0)
        self.push(block, p, self.xl, self.c, self.right.at[p], 0)
        self.push(block, p, self.x, 1 - self.c, self.sib.at[self.x, p], 0)

    def half(self, x, p, h):
        return self.buf.at[x, self.c, :, pl.ds(p * self.rows + h * (self.rows // 2), self.rows // 2)]

    def step_near(self, p):
        for h, x, on, sem in ((0, self.xl, self.xr, self.left), (1, self.xr, self.xl, self.right)):
            block = self.buf.at[x, self.c, :, self.span(p)]
            self.arrived(block, sem.at[p])
            self.push(self.half(x, p, h), p, on, self.c, self.far.at[h, p])
            self.push(block, p, self.x, 1 - self.c, self.sib.at[x, p])

    def step_far(self, p):
        for h in range(2):
            half = self.half(self.x2, p, h)
            self.arrived(half, self.far.at[h, p])
            self.push(half, p, self.x, 1 - self.c, self.sib.at[self.x2, p])

    def finish(self, p):
        for x in range(XS):
            self.arrived(self.buf.at[x, 1 - self.c, :, self.span(p)], self.sib.at[x, p])

    def drain(self, p):
        self.arrived(self.buf.at[pl.ds(0, 3), 0, :, self.span(p)], self.sent.at[0, p])
        self.arrived(self.buf.at[:, 0, :, self.span(p)], self.sent.at[1, p])


PARTS = 2
CHUNKS = 36


def whole_kernel(
    first_hbm, second_hbm, value_hbm, taps_hbm, skip_hbm, weight_ref, queries_ref, keys_ref,
    spread_hbm, mix_hbm, unmix_hbm, gather_hbm, turn_hbm, mixed_ref, attended_ref,
    first_in, value_in, taps_in, second_in, skip, spread_t, mix_t, unmix_t, gather_t, turn,
    product, send, recv, taps_spectrum, out_send, out_recv, gated_ref,
    weights, partial, own_part, sib_send, sib_recv, y_send, y_recv, near_send, near_recv, mine,
    k_buf, v_buf, q_buf, scores, rounded, totals, o_send, o_recv,
    in_sem, table_sem, send_sem, recv_sem, back_send_sem, back_recv_sem,
    w_sem, sib_send_sem, sib_recv_sem, y_send_sem, y_recv_sem, near_send_sem, near_recv_sem,
    q_send_sem, q_recv_sem, o_send_sem, o_recv_sem,
    kz, k_own, k_left, k_right, k_far, k_sib, k_sent,
    vz, v_own, v_left, v_right, v_far, v_sib, v_sent,
):
    me, tp = lax.axis_index("ctx"), lax.axis_index("tp")
    x, z = lax.div(me, ZS), lax.rem(me, ZS)
    y, c = lax.div(tp, 2), lax.rem(tp, 2)
    place = (x, z, y, c)
    keys_of = Spread(place, k_buf, 1, kz, k_own, k_left, k_right, k_far, k_sib, k_sent)
    values_of = Spread(place, v_buf, PARTS, vz, v_own, v_left, v_right, v_far, v_sib, v_sent)
    mirror = XS - 1 - x
    half = GROUP * CTX

    base = [lax.rem(lax.div(me, 16) + g, 2) * 16 for g in range(2)]
    cols_of = [
        [pl.ds(pl.multiple_of(h * 512 + base[g] * GROUP, 256), 256) for g in range(2)] for h in range(2)
    ]
    inputs = {}
    for h in range(2):
        for k, (hbm, into) in enumerate(
            ((taps_hbm, taps_in), (first_hbm, first_in), (value_hbm, value_in))
        ):
            for g in range(2):
                inputs[k, h, g] = pltpu.make_async_copy(
                    hbm.at[:, cols_of[h][g]], into.at[h, g], in_sem.at[k, 2 * h + g]
                )
                inputs[k, h, g].start()

    barrier = pltpu.get_barrier_semaphore()

    def greet(to_ctx, to_tp):
        pl.semaphore_signal(
            barrier, inc=1, device_id={"ctx": to_ctx, "tp": to_tp}, device_id_type=MESH
        )

    def greet_group(k, carry):
        greet(lax.rem(me + k, CTX), tp)
        return carry

    def greet_rows(k, carry):
        greet(x * ZS + k, y * 2 + 1 - c)
        greet(mirror * ZS + k, y * 2 + 1 - c)
        return carry

    lax.fori_loop(1, CTX, greet_group, 0)
    lax.fori_loop(0, ZS, greet_rows, 0)
    for k in (1, 3):
        greet(me, lax.rem(y + k, YS) * 2 + c)

    tables_in = []
    for k, (hbm, into) in enumerate((
        (spread_hbm, spread_t), (turn_hbm, turn), (mix_hbm, mix_t), (unmix_hbm, unmix_t),
        (gather_hbm, gather_t), (skip_hbm, skip),
    )):
        tables_in.append(pltpu.make_async_copy(hbm, into, table_sem.at[k]))
        tables_in[-1].start()
    gates_in = []
    for h in range(2):
        for g in range(2):
            gates_in.append(pltpu.make_async_copy(
                second_hbm.at[:, cols_of[h][g]], second_in.at[h, g], in_sem.at[3, 2 * h + g]
            ))
            gates_in[-1].start()

    def post_line(kind, h, g):
        def one(k, carry):
            o = lax.rem(me + k, 16)
            pltpu.make_async_remote_copy(
                src_ref=send.at[kind, h, g, o], dst_ref=recv.at[kind, h, me],
                send_sem=send_sem.at[kind, h], recv_sem=recv_sem.at[kind, h],
                device_id={"ctx": base[g] + o}, device_id_type=MESH,
            ).start()
            return carry

        if g == 0:
            pltpu.make_async_copy(
                send.at[kind, h, 0, lax.rem(me, 16)], recv.at[kind, h, me], recv_sem.at[kind, h]
            ).start()
        lax.fori_loop(1 if g == 0 else 0, 16, one, 0)

    down = lax.broadcasted_iota(jnp.int32, (ROWS, ROWS), 0)
    across = lax.broadcasted_iota(jnp.int32, (ROWS, ROWS), 1)
    eye = jnp.where(down == across, 1.0, 0.0).astype(BF)
    for h in range(2):
        for kind in (1, 0):
            for g in range(2):
                if kind == 1:
                    inputs[0, h, g].wait()
                    block = taps_in[h, g]
                else:
                    inputs[1, h, g].wait()
                    inputs[2, h, g].wait()
                    block = (first_in[h, g].astype(F32) * value_in[h, g].astype(F32)).astype(BF)
                    product[h, g] = block
                send[kind, h, g] = nt(eye, block).astype(BF).reshape(16, GROUP, ROWS)
                if (h, kind, g) == (0, 1, 0):
                    pl.semaphore_wait(barrier, CTX - 1 + 2 * ZS + 2)
                post_line(kind, h, g)
    keys_of.scatter(keys_ref, 0, True)

    order = [(other, lax.rem(y + k, YS)) for other in (1, 0) for k in (2, 1, 3, 0)]
    loads = []
    for k, (other, to_y) in enumerate(order):
        col = to_y * 2 + (1 - c if other else c)
        loads.append(pltpu.make_async_copy(
            weight_ref.at[:, pl.ds(pl.multiple_of(col * HEAD, HEAD), HEAD)], weights.at[k], w_sem.at[k]
        ))
        loads[-1].start()
    for copy in tables_in:
        copy.wait()

    for h in range(2):
        tr, ti = turn[:CTX], turn[CTX:]
        pltpu.make_async_copy(recv.at[1, h], recv.at[1, h], recv_sem.at[1, h]).wait()
        taps_spectrum[...] = spectrum(
            recv[1, h].reshape(half, ROWS), spread_t[...], mix_t[...], tr, ti
        )
        pltpu.make_async_copy(recv.at[0, h], recv.at[0, h], recv_sem.at[0, h]).wait()
        d = spectrum(recv[0, h].reshape(half, ROWS), spread_t[...], mix_t[...], tr, ti)
        e = taps_spectrum[...]
        d_re, d_im, e_re, e_im = d[:, :ROWS], d[:, ROWS:], e[:, :ROWS], e[:, ROWS:]
        y_re = (d_re * e_re - d_im * e_im).astype(BF)
        y_im = (d_re * e_im + d_im * e_re).astype(BF)
        b = nn(jnp.concatenate([y_re, y_im], axis=1), unmix_t[...])
        b_re = b[:, :ROWS].reshape(GROUP, CTX, ROWS)
        b_im = b[:, ROWS:].reshape(GROUP, CTX, ROWS)
        c_re = (b_re * tr + b_im * ti).reshape(half, ROWS).astype(BF)
        c_im = (b_im * tr - b_re * ti).reshape(half, ROWS).astype(BF)
        out = nn(gather_t[...], jnp.concatenate([c_re, c_im], axis=0))
        out_send[h] = out.astype(BF).reshape(CTX, GROUP, ROWS)

        def reply(k, carry, h=h):
            to = lax.rem(me + k, CTX)
            pltpu.make_async_remote_copy(
                src_ref=out_send.at[h, to], dst_ref=out_recv.at[h, me],
                send_sem=back_send_sem.at[h], recv_sem=back_recv_sem.at[h],
                device_id={"ctx": to}, device_id_type=MESH,
            ).start()
            return carry

        pltpu.make_async_copy(out_send.at[h, me], out_recv.at[h, me], back_recv_sem.at[h]).start()
        lax.fori_loop(1, CTX, reply, 0)
        if h == 0:
            keys_of.step_own(0)
        else:
            keys_of.step_near(0)

    for copy in gates_in:
        copy.wait()

    def gate(h):
        pltpu.make_async_copy(out_recv.at[h], out_recv.at[h], back_recv_sem.at[h]).wait()
        for g in range(2):
            block = out_recv[h, pl.ds(base[g], 16)].reshape(ROWS, ROWS)
            filtered = nt(eye, block).astype(BF).astype(F32)
            gated_ref[:, cols_of[h][g]] = (
                second_in[h, g].astype(F32)
                * (filtered + skip[:, cols_of[h][g]] * product[h, g].astype(F32))
            ).astype(BF)

    gate(0)
    low = gated_ref[:, :512]
    for k in range(8):
        loads[k].wait()
        partial[k] = nn(low, weights[k, :512])
    gate(1)
    high = gated_ref[:, 512:]

    def projected(k):
        return partial[k] + nn(high, weights[k, 512:])

    far_pair = lax.min(z, ZS - 1 - z)
    q_x = lax.select(far_pair < 2, x, mirror)
    q_core = lax.rem(far_pair, 2)
    q_slot = lax.div(x, 2) * 2 + lax.div(z, 4)

    def query_copies(j):
        to = 4 * c + j
        alone = (to == z) & (q_core == c) & (far_pair < 2)
        part = queries_ref.at[:, pl.ds(j * HS, HS)]
        slot = q_buf.at[q_slot]
        sem = q_recv_sem.at[q_slot]
        local = lambda: pltpu.make_async_copy(part, slot, sem)
        away = lambda: pltpu.make_async_remote_copy(
            src_ref=part, dst_ref=slot, send_sem=q_send_sem.at[j], recv_sem=sem,
            device_id={"ctx": q_x * ZS + to, "tp": y * 2 + q_core}, device_id_type=MESH,
        )
        return alone, local, away

    for j in range(4):
        start_either(*query_copies(j))

    swaps = []
    for k in range(4):
        sib_send[k] = projected(k).astype(BF)
        swaps.append(pltpu.make_async_remote_copy(
            src_ref=sib_send.at[k], dst_ref=sib_recv.at[k],
            send_sem=sib_send_sem.at[k], recv_sem=sib_recv_sem.at[k],
            device_id={"tp": y * 2 + 1 - c}, device_id_type=MESH,
        ))
        swaps[-1].start()

    def chip_sum(k):
        own = projected(4 + k)
        swaps[k].wait_recv()
        return own + sib_recv[k].astype(F32)

    right, left = lax.rem(y + 1, YS) * 2 + c, lax.rem(y + 3, YS) * 2 + c
    depth = ROWS // PARTS
    spans = [pl.ds(p * depth, depth) for p in range(PARTS)]

    def hop(source, into, send_sems, recv_sems, h, p):
        return pltpu.make_async_remote_copy(
            src_ref=source.at[h, spans[p]], dst_ref=into.at[h, spans[p]],
            send_sem=send_sems.at[h, p], recv_sem=recv_sems.at[h, p],
            device_id={"tp": (right, left)[h]}, device_id_type=MESH,
        )

    far = chip_sum(0).astype(BF)
    far_hops, near_hops = {}, {}
    for h in range(2):
        y_send[h] = far[:, h * 256:(h + 1) * 256]
    for p in range(PARTS):
        for h in range(2):
            far_hops[h, p] = hop(y_send, y_recv, y_send_sem, y_recv_sem, h, p)
            far_hops[h, p].start()
    for k in range(1, 4):
        own_part[k] = chip_sum(k)
    keys_of.step_far(0)
    for p in range(PARTS):
        for h in range(2):
            far_hops[h, p].wait_recv()
            own_part[1 + h, spans[p], pl.ds(h * 256, 256)] += y_recv[h, spans[p]].astype(F32)
            near_send[h, spans[p]] = own_part[1 + h, spans[p]].astype(BF)
            near_hops[h, p] = hop(near_send, near_recv, near_send_sem, near_recv_sem, h, p)
            near_hops[h, p].start()
    keys_of.finish(0)

    scale = 1.0 / math.sqrt(HS) * math.log2(math.e)
    blocks, first_step = [], []
    steps_before = 0
    for i in range(4):
        row = lax.min(x, mirror) if i < 2 else lax.max(x, mirror)
        pair = lax.select(row == x, c, c + 2)
        zq = pair if i % 2 == 0 else ZS - 1 - pair
        rank = row * ZS + zq
        blocks.append((row, zq, rank, lax.div(rank, 2)))
        first_step.append(steps_before)
        steps_before = steps_before + lax.div(rank, 2) + 1

    def chunk(buf, step):
        row, i = lax.div(step, 4), lax.rem(step, 4)
        return jnp.concatenate([buf[row, 0, i], buf[row, 1, i]], axis=0)

    def fold(op, top, s):
        for at in range(0, KEYS, 128):
            top = op(top, s[:, at:at + 128])
        return top

    def score_all(i):
        row, zq, rank, last = blocks[i]
        pltpu.make_async_copy(q_buf.at[i], q_buf.at[i], q_recv_sem.at[i]).wait()
        query = q_buf[i]

        def score(step, top):
            s = nt(query, chunk(k_buf, step))
            scores[step] = s
            return fold(jnp.maximum, top, s)

        top = lax.fori_loop(0, last, score, jnp.full((ROWS, 128), NEG, F32))
        s = nt(query, chunk(k_buf, last))
        key_pos = lax.broadcasted_iota(jnp.int32, (ROWS, KEYS), 1) + last * KEYS
        query_pos = lax.broadcasted_iota(jnp.int32, (ROWS, KEYS), 0) + rank * ROWS
        s = jnp.where(key_pos <= query_pos, s, NEG)
        scores[last] = s
        top = jnp.max(fold(jnp.maximum, top, s), axis=1, keepdims=True)
        totals[i] = jnp.broadcast_to(top, (ROWS, 128))

    def weigh_all(i):
        row, zq, rank, last = blocks[i]
        top = totals[i, :, :1]

        def weight(step, total):
            w = jnp.exp2((scores[step] - top) * scale)
            rounded[first_step[i] + step] = w.astype(BF)
            return fold(jnp.add, total, w)

        total = lax.fori_loop(0, last + 1, weight, jnp.zeros((ROWS, 128), F32))
        totals[i] = jnp.broadcast_to(jnp.sum(total, axis=1, keepdims=True), (ROWS, 128))

    def values_out(p):
        for h in range(2):
            near_hops[h, p].wait_recv()
        mixed = (
            own_part[3, spans[p]] + near_recv[0, spans[p]].astype(F32) + near_recv[1, spans[p]].astype(F32)
        ).astype(BF)
        mine[spans[p]] = mixed
        values_of.scatter(mine, p, True)
        mixed_ref[spans[p]] = mixed

    for i in range(2):
        score_all(i)
        weigh_all(i)
    values_out(0)
    score_all(2)
    values_out(1)
    weigh_all(2)
    values_of.step_own(0)
    score_all(3)
    values_of.step_own(1)
    weigh_all(3)
    values_of.step_near(0)
    values_of.step_near(1)
    values_of.step_far(0)
    values_of.step_far(1)
    for p in range(PARTS):
        values_of.finish(p)

    def output_copies(i):
        row, zq, rank, last = blocks[i]
        core, j = lax.div(z, 4), lax.rem(z, 4)
        alone = (zq == z) & (core == c) & (row == x)
        local = lambda: pltpu.make_async_copy(o_send.at[i], o_recv.at[j], o_recv_sem.at[j])
        away = lambda: pltpu.make_async_remote_copy(
            src_ref=o_send.at[i], dst_ref=o_recv.at[j],
            send_sem=o_send_sem.at[i], recv_sem=o_recv_sem.at[j],
            device_id={"ctx": row * ZS + zq, "tp": y * 2 + core}, device_id_type=MESH,
        )
        return alone, local, away

    for i in range(4):
        row, zq, rank, last = blocks[i]

        def value(step, acc, i=i):
            return acc + nn(rounded[first_step[i] + step], chunk(v_buf, step))

        acc = lax.fori_loop(0, last + 1, value, jnp.zeros((ROWS, HS), F32))
        o_send[i] = (acc / totals[i]).astype(BF)
        start_either(*output_copies(i))

    for h in range(2):
        for kind in range(2):
            some = recv.at[kind, h, pl.ds(0, CTX - 1)]
            pltpu.make_async_copy(some, some, send_sem.at[kind, h]).wait()
        some = out_recv.at[h, pl.ds(0, CTX - 1)]
        pltpu.make_async_copy(some, some, back_send_sem.at[h]).wait()
    keys_of.scatter(keys_ref, 0, False)
    keys_of.drain(0)
    for p in range(PARTS):
        values_of.scatter(mine, p, False)
        values_of.drain(p)
        for h in range(2):
            far_hops[h, p].wait_send()
            near_hops[h, p].wait_send()
    for j in range(4):
        alone, local, away = query_copies(j)
        pl.when(jnp.logical_not(alone))(lambda away=away: away().wait_send())
        swaps[j].wait_send()
    for j in range(4):
        pltpu.make_async_copy(o_recv.at[j], o_recv.at[j], o_recv_sem.at[j]).wait()
        attended_ref[:, j * HS:(j + 1) * HS] = o_recv[j]
    for i in range(4):
        alone, local, away = output_copies(i)
        pl.when(jnp.logical_not(alone))(lambda away=away: away().wait_send())


def start_either(alone, local, away):
    pl.when(alone)(lambda: local().start())
    pl.when(jnp.logical_not(alone))(lambda: away().start())


def vmem(count):
    return [pl.BlockSpec(memory_space=pltpu.VMEM)] * count


def hbm(count):
    return [pl.BlockSpec(memory_space=pl.ANY)] * count


def hand_over(a, b, a_out, b_out):
    a_out[...] = a[...]
    b_out[...] = b[...]


def per_device(
    first_input, second_input, value_input, filter_taps, skip_gain, out_weight, queries, keys
):
    spread, mix, unmix, gather, turn_re, turn_im = tables()
    consts = [jnp.asarray(t) for t in (spread, mix, unmix, gather, np.concatenate([turn_re, turn_im]))]
    dma = lambda *shape: pltpu.SemaphoreType.DMA(shape)
    bf = lambda *shape: pltpu.VMEM(shape, BF)
    fl = lambda *shape: pltpu.VMEM(shape, F32)
    sems = lambda p: [dma(p, 4), dma(p), dma(p), dma(p), dma(2, p), dma(XS, p), dma(2, p)]
    out = jax.ShapeDtypeStruct((ROWS, HEAD), BF)
    mixed, attended = pl.pallas_call(
        whole_kernel,
        out_shape=(out, out),
        in_specs=hbm(13),
        out_specs=tuple(vmem(2)),
        scratch_shapes=[
            bf(2, 2, ROWS, 256), bf(2, 2, ROWS, 256), bf(2, 2, ROWS, 256), bf(2, 2, ROWS, 256),
            fl(1, 1024), bf(1024, 512), bf(512, 512), bf(512, 512), bf(512, 1024), fl(2 * CTX, ROWS),
            bf(2, 2, ROWS, 256),
            bf(2, 2, 2, 16, GROUP, ROWS), bf(2, 2, CTX, GROUP, ROWS), fl(512, 512),
            bf(2, CTX, GROUP, ROWS), bf(2, CTX, GROUP, ROWS),
            bf(ROWS, 1024),
            bf(8, 1024, HEAD), fl(8, ROWS, HEAD), fl(4, ROWS, HEAD), bf(4, ROWS, HEAD), bf(4, ROWS, HEAD),
            bf(2, ROWS, 256), bf(2, ROWS, 256), bf(2, ROWS, HEAD), bf(2, ROWS, HEAD), bf(ROWS, HEAD),
            bf(XS, 2, ZS // 2, ROWS, HS), bf(XS, 2, ZS // 2, ROWS, HS), bf(4, ROWS, HS),
            fl(TOTAL // KEYS, ROWS, KEYS), bf(CHUNKS, ROWS, KEYS), fl(4, ROWS, 128),
            bf(4, ROWS, HS), bf(4, ROWS, HS),
            dma(4, 4), dma(6), dma(2, 2), dma(2, 2), dma(2), dma(2),
            dma(8), dma(4), dma(4), dma(2, PARTS), dma(2, PARTS), dma(2, PARTS), dma(2, PARTS),
            dma(4), dma(4), dma(4), dma(4),
        ] + sems(1) + sems(PARTS),
        compiler_params=pltpu.CompilerParams(
            collective_id=0, has_side_effects=True, vmem_limit_bytes=60 * 1024 * 1024
        ),
        name="whole",
    )(first_input, second_input, value_input, filter_taps, skip_gain.reshape(1, 1024), out_weight,
      queries, keys, *consts)
    return pl.pallas_call(
        hand_over,
        out_shape=(out, out),
        in_specs=vmem(2),
        out_specs=tuple(vmem(2)),
        name="hand_over",
    )(mixed, attended)


def solution(mesh):
    return jax.shard_map(
        per_device,
        mesh=mesh,
        in_specs=(
            P("ctx", "tp"),
            P("ctx", "tp"),
            P("ctx", "tp"),
            P("ctx", "tp"),
            P("tp"),
            P("tp", None),
            P("ctx", "tp"),
            P("ctx", "tp"),
        ),
        out_specs=(P("ctx", "tp"), P("ctx", "tp")),
        check_vma=False,
    )
```

```python
import functools
import math

import jax
import jax.numpy as jnp
import numpy as np
from jax import lax
from jax.experimental import pallas as pl
from jax.experimental.pallas import tpu as pltpu
from jax.sharding import PartitionSpec as P

HS = 128
MESH = pl.DeviceIdType.MESH
BF = jnp.bfloat16
F32 = jnp.float32
CTX = 32
ROWS = 256
GROUP = 16
TOTAL = CTX * ROWS


def nt(a, b):
    return lax.dot_general(a, b, (((1,), (1,)), ((), ())), preferred_element_type=F32)


def nn(a, b):
    return jnp.dot(a, b, preferred_element_type=F32)


def tables():
    r = np.arange(CTX, dtype=np.float64)
    q = np.arange(CTX, dtype=np.float64)
    a = np.arange(ROWS, dtype=np.float64)
    rows = np.exp(-2j * np.pi * np.outer(q + 0.25, r) / CTX)
    turn = np.exp(-2j * np.pi * np.outer(q + 0.25, a) / TOTAL)
    cols = np.exp(-2j * np.pi * np.outer(a, a) / ROWS)
    eye = np.eye(GROUP)
    spread = lambda m: np.einsum("qr,cd->cqrd", m, eye).reshape(GROUP * CTX, CTX * GROUP)
    first = np.concatenate([spread(rows.real), spread(rows.imag)], axis=0)
    back = np.conj(rows).T
    gather = lambda m: np.einsum("rq,cd->rcdq", m, eye).reshape(CTX * GROUP, GROUP * CTX)
    last = np.concatenate([gather(back.real), -gather(back.imag)], axis=1)
    mix = np.block([[cols.real, cols.imag], [-cols.imag, cols.real]])
    unmix = np.block([[cols.real, -cols.imag], [cols.imag, cols.real]]) / TOTAL
    cast = lambda m: np.asarray(m, np.float32).astype(jnp.bfloat16)
    return (cast(first), cast(mix), cast(unmix), cast(last),
            np.asarray(turn.real, np.float32), np.asarray(turn.imag, np.float32))


def spectrum(x, first, mix, turn_re, turn_im):
    half = GROUP * CTX
    a = nn(first, x)
    a_re = a[:half].reshape(GROUP, CTX, ROWS)
    a_im = a[half:].reshape(GROUP, CTX, ROWS)
    z_re = (a_re * turn_re - a_im * turn_im).reshape(half, ROWS).astype(BF)
    z_im = (a_re * turn_im + a_im * turn_re).reshape(half, ROWS).astype(BF)
    return nn(jnp.concatenate([z_re, z_im], axis=1), mix)


XS, ZS, YS = 4, 8, 4
HEAD = 512
KEYS = 1024
NEG = -1e30


class Spread:
    def __init__(self, place, buf, parts, z_send, own, left, right, far, sib, sent):
        self.x, self.z, self.y, self.c = place
        self.buf, self.z_send, self.own, self.left, self.right, self.far, self.sib, self.sent = (
            buf, z_send, own, left, right, far, sib, sent
        )
        self.rows = ROWS // parts
        self.xl, self.xr, self.x2 = (lax.rem(self.x + k, XS) for k in (3, 1, 2))

    def device(self, x, z, c):
        return {"ctx": x * ZS + z, "tp": self.y * 2 + c}

    def span(self, p):
        return pl.ds(p * self.rows, self.rows)

    def scatter(self, source, p, start):
        x, z, c = self.x, self.z, self.c
        core = lax.rem(z, 2)
        for j in range(4):
            to = 4 * c + j
            alone = (to == z) & (core == c)
            part = source.at[self.span(p), pl.ds(j * HS, HS)]
            slot = self.buf.at[x, core, lax.div(z, 2), self.span(p)]
            local = lambda: pltpu.make_async_copy(part, slot, self.own.at[p])
            away = lambda: pltpu.make_async_remote_copy(
                src_ref=part, dst_ref=slot, send_sem=self.z_send.at[p, j], recv_sem=self.own.at[p],
                device_id=self.device(x, to, core), device_id_type=MESH,
            )
            if start:
                start_either(alone, local, away)
            else:
                pl.when(jnp.logical_not(alone))(lambda: away().wait_send())

    def push(self, block, p, x, c, sem, late=1):
        pltpu.make_async_remote_copy(
            src_ref=block, dst_ref=block, send_sem=self.sent.at[late, p], recv_sem=sem,
            device_id=self.device(x, self.z, c), device_id_type=MESH,
        ).start()

    def arrived(self, block, sem):
        pltpu.make_async_copy(block, block, sem).wait()

    def step_own(self, p):
        block = self.buf.at[self.x, self.c, :, self.span(p)]
        self.arrived(block, self.own.at[p])
        self.push(block, p, self.xr, self.c, self.left.at[p], 0)
        self.push(block, p, self.xl, self.c, self.right.at[p], 0)
        self.push(block, p, self.x, 1 - self.c, self.sib.at[self.x, p], 0)

    def half(self, x, p, h):
        return self.buf.at[x, self.c, :, pl.ds(p * self.rows + h * (self.rows // 2), self.rows // 2)]

    def step_near(self, p):
        for h, x, on, sem in ((0, self.xl, self.xr, self.left), (1, self.xr, self.xl, self.right)):
            block = self.buf.at[x, self.c, :, self.span(p)]
            self.arrived(block, sem.at[p])
            self.push(self.half(x, p, h), p, on, self.c, self.far.at[h, p])
            self.push(block, p, self.x, 1 - self.c, self.sib.at[x, p])

    def step_far(self, p):
        for h in range(2):
            half = self.half(self.x2, p, h)
            self.arrived(half, self.far.at[h, p])
            self.push(half, p, self.x, 1 - self.c, self.sib.at[self.x2, p])

    def finish(self, p):
        for x in range(XS):
            self.arrived(self.buf.at[x, 1 - self.c, :, self.span(p)], self.sib.at[x, p])

    def drain(self, p):
        self.arrived(self.buf.at[pl.ds(0, 3), 0, :, self.span(p)], self.sent.at[0, p])
        self.arrived(self.buf.at[:, 0, :, self.span(p)], self.sent.at[1, p])


PARTS = 2
CHUNKS = 20


def whole_kernel(
    first_hbm, second_hbm, value_hbm, taps_hbm, skip_hbm, weight_ref, queries_ref, keys_ref,
    spread_hbm, mix_hbm, unmix_hbm, gather_hbm, turn_hbm, mixed_ref, attended_ref,
    first_in, value_in, taps_in, second_in, skip, spread_t, mix_t, unmix_t, gather_t, turn,
    product, send, recv, taps_spectrum, out_send, out_recv, gated_ref,
    weights, partial, own_part, sib_send, sib_recv, y_send, y_recv, near_send, near_recv, mine,
    k_buf, v_buf, q_buf, scores, rounded, totals, o_send, o_recv,
    in_sem, table_sem, send_sem, recv_sem, back_send_sem, back_recv_sem,
    w_sem, sib_send_sem, sib_recv_sem, y_send_sem, y_recv_sem, near_send_sem, near_recv_sem,
    q_send_sem, q_recv_sem, o_send_sem, o_recv_sem,
    kz, k_own, k_left, k_right, k_far, k_sib, k_sent,
    vz, v_own, v_left, v_right, v_far, v_sib, v_sent,
):
    me, tp = lax.axis_index("ctx"), lax.axis_index("tp")
    x, z = lax.div(me, ZS), lax.rem(me, ZS)
    y, c = lax.div(tp, 2), lax.rem(tp, 2)
    place = (x, z, y, c)
    keys_of = Spread(place, k_buf, 1, kz, k_own, k_left, k_right, k_far, k_sib, k_sent)
    values_of = Spread(place, v_buf, PARTS, vz, v_own, v_left, v_right, v_far, v_sib, v_sent)
    mirror = XS - 1 - x
    half = GROUP * CTX

    base = [lax.rem(lax.div(me, 16) + g, 2) * 16 for g in range(2)]
    cols_of = [
        [pl.ds(pl.multiple_of(h * 512 + base[g] * GROUP, 256), 256) for g in range(2)] for h in range(2)
    ]
    inputs = {}
    for h in range(2):
        for k, (hbm, into) in enumerate(
            ((taps_hbm, taps_in), (first_hbm, first_in), (value_hbm, value_in))
        ):
            for g in range(2):
                inputs[k, h, g] = pltpu.make_async_copy(
                    hbm.at[:, cols_of[h][g]], into.at[h, g], in_sem.at[k, 2 * h + g]
                )
                inputs[k, h, g].start()

    barrier = pltpu.get_barrier_semaphore()

    def greet(to_ctx, to_tp):
        pl.semaphore_signal(
            barrier, inc=1, device_id={"ctx": to_ctx, "tp": to_tp}, device_id_type=MESH
        )

    def greet_group(k, carry):
        greet(lax.rem(me + k, CTX), tp)
        return carry

    def greet_rows(k, carry):
        greet(x * ZS + k, y * 2 + 1 - c)
        greet(mirror * ZS + k, y * 2 + 1 - c)
        return carry

    lax.fori_loop(1, CTX, greet_group, 0)
    lax.fori_loop(0, ZS, greet_rows, 0)
    for k in (1, 3):
        greet(me, lax.rem(y + k, YS) * 2 + c)

    tables_in = []
    for k, (hbm, into) in enumerate((
        (spread_hbm, spread_t), (turn_hbm, turn), (mix_hbm, mix_t), (unmix_hbm, unmix_t),
        (gather_hbm, gather_t), (skip_hbm, skip),
    )):
        tables_in.append(pltpu.make_async_copy(hbm, into, table_sem.at[k]))
        tables_in[-1].start()
    gates_in = []
    for h in range(2):
        for g in range(2):
            gates_in.append(pltpu.make_async_copy(
                second_hbm.at[:, cols_of[h][g]], second_in.at[h, g], in_sem.at[3, 2 * h + g]
            ))
            gates_in[-1].start()

    def post_line(kind, h, g):
        def one(k, carry):
            o = lax.rem(me + k, 16)
            pltpu.make_async_remote_copy(
                src_ref=send.at[kind, h, g, o], dst_ref=recv.at[kind, h, me],
                send_sem=send_sem.at[kind, h], recv_sem=recv_sem.at[kind, h],
                device_id={"ctx": base[g] + o}, device_id_type=MESH,
            ).start()
            return carry

        if g == 0:
            pltpu.make_async_copy(
                send.at[kind, h, 0, lax.rem(me, 16)], recv.at[kind, h, me], recv_sem.at[kind, h]
            ).start()
        lax.fori_loop(1 if g == 0 else 0, 16, one, 0)

    down = lax.broadcasted_iota(jnp.int32, (ROWS, ROWS), 0)
    across = lax.broadcasted_iota(jnp.int32, (ROWS, ROWS), 1)
    eye = jnp.where(down == across, 1.0, 0.0).astype(BF)
    for h in range(2):
        for kind in (1, 0):
            for g in range(2):
                if kind == 1:
                    inputs[0, h, g].wait()
                    block = taps_in[h, g]
                else:
                    inputs[1, h, g].wait()
                    inputs[2, h, g].wait()
                    block = (first_in[h, g].astype(F32) * value_in[h, g].astype(F32)).astype(BF)
                    product[h, g] = block
                send[kind, h, g] = nt(eye, block).astype(BF).reshape(16, GROUP, ROWS)
                if (h, kind, g) == (0, 1, 0):
                    pl.semaphore_wait(barrier, CTX - 1 + 2 * ZS + 2)
                post_line(kind, h, g)
    keys_of.scatter(keys_ref, 0, True)

    order = [(other, lax.rem(y + k, YS)) for other in (1, 0) for k in (2, 1, 3, 0)]
    loads = []
    for k, (other, to_y) in enumerate(order):
        col = to_y * 2 + (1 - c if other else c)
        loads.append(pltpu.make_async_copy(
            weight_ref.at[:, pl.ds(pl.multiple_of(col * HEAD, HEAD), HEAD)], weights.at[k], w_sem.at[k]
        ))
        loads[-1].start()
    for copy in tables_in:
        copy.wait()

    for h in range(2):
        tr, ti = turn[:CTX], turn[CTX:]
        pltpu.make_async_copy(recv.at[1, h], recv.at[1, h], recv_sem.at[1, h]).wait()
        taps_spectrum[...] = spectrum(
            recv[1, h].reshape(half, ROWS), spread_t[...], mix_t[...], tr, ti
        )
        pltpu.make_async_copy(recv.at[0, h], recv.at[0, h], recv_sem.at[0, h]).wait()
        d = spectrum(recv[0, h].reshape(half, ROWS), spread_t[...], mix_t[...], tr, ti)
        e = taps_spectrum[...]
        d_re, d_im, e_re, e_im = d[:, :ROWS], d[:, ROWS:], e[:, :ROWS], e[:, ROWS:]
        y_re = (d_re * e_re - d_im * e_im).astype(BF)
        y_im = (d_re * e_im + d_im * e_re).astype(BF)
        b = nn(jnp.concatenate([y_re, y_im], axis=1), unmix_t[...])
        b_re = b[:, :ROWS].reshape(GROUP, CTX, ROWS)
        b_im = b[:, ROWS:].reshape(GROUP, CTX, ROWS)
        c_re = (b_re * tr + b_im * ti).reshape(half, ROWS).astype(BF)
        c_im = (b_im * tr - b_re * ti).reshape(half, ROWS).astype(BF)
        out = nn(gather_t[...], jnp.concatenate([c_re, c_im], axis=0))
        out_send[h] = out.astype(BF).reshape(CTX, GROUP, ROWS)

        def reply(k, carry, h=h):
            to = lax.rem(me + k, CTX)
            pltpu.make_async_remote_copy(
                src_ref=out_send.at[h, to], dst_ref=out_recv.at[h, me],
                send_sem=back_send_sem.at[h], recv_sem=back_recv_sem.at[h],
                device_id={"ctx": to}, device_id_type=MESH,
            ).start()
            return carry

        pltpu.make_async_copy(out_send.at[h, me], out_recv.at[h, me], back_recv_sem.at[h]).start()
        lax.fori_loop(1, CTX, reply, 0)
        if h == 0:
            keys_of.step_own(0)
        else:
            keys_of.step_near(0)

    for copy in gates_in:
        copy.wait()

    def gate(h):
        pltpu.make_async_copy(out_recv.at[h], out_recv.at[h], back_recv_sem.at[h]).wait()
        for g in range(2):
            block = out_recv[h, pl.ds(base[g], 16)].reshape(ROWS, ROWS)
            filtered = nt(eye, block).astype(BF).astype(F32)
            gated_ref[:, cols_of[h][g]] = (
                second_in[h, g].astype(F32)
                * (filtered + skip[:, cols_of[h][g]] * product[h, g].astype(F32))
            ).astype(BF)

    gate(0)
    low = gated_ref[:, :512]
    for k in range(8):
        loads[k].wait()
        partial[k] = nn(low, weights[k, :512])
    gate(1)
    high = gated_ref[:, 512:]

    def projected(k):
        return partial[k] + nn(high, weights[k, 512:])

    far_pair = lax.min(z, ZS - 1 - z)
    q_x = lax.select(far_pair < 2, x, mirror)
    q_core = lax.rem(far_pair, 2)
    q_slot = lax.div(x, 2) * 2 + lax.div(z, 4)

    def query_copies(j):
        to = 4 * c + j
        alone = (to == z) & (q_core == c) & (far_pair < 2)
        part = queries_ref.at[:, pl.ds(j * HS, HS)]
        slot = q_buf.at[q_slot]
        sem = q_recv_sem.at[q_slot]
        local = lambda: pltpu.make_async_copy(part, slot, sem)
        away = lambda: pltpu.make_async_remote_copy(
            src_ref=part, dst_ref=slot, send_sem=q_send_sem.at[j], recv_sem=sem,
            device_id={"ctx": q_x * ZS + to, "tp": y * 2 + q_core}, device_id_type=MESH,
        )
        return alone, local, away

    for j in range(4):
        start_either(*query_copies(j))

    swaps = []
    for k in range(4):
        sib_send[k] = projected(k).astype(BF)
        swaps.append(pltpu.make_async_remote_copy(
            src_ref=sib_send.at[k], dst_ref=sib_recv.at[k],
            send_sem=sib_send_sem.at[k], recv_sem=sib_recv_sem.at[k],
            device_id={"tp": y * 2 + 1 - c}, device_id_type=MESH,
        ))
        swaps[-1].start()

    def chip_sum(k):
        own = projected(4 + k)
        swaps[k].wait_recv()
        return own + sib_recv[k].astype(F32)

    right, left = lax.rem(y + 1, YS) * 2 + c, lax.rem(y + 3, YS) * 2 + c
    depth = ROWS // PARTS
    spans = [pl.ds(p * depth, depth) for p in range(PARTS)]

    def hop(source, into, send_sems, recv_sems, h, p):
        return pltpu.make_async_remote_copy(
            src_ref=source.at[h, spans[p]], dst_ref=into.at[h, spans[p]],
            send_sem=send_sems.at[h, p], recv_sem=recv_sems.at[h, p],
            device_id={"tp": (right, left)[h]}, device_id_type=MESH,
        )

    far = chip_sum(0).astype(BF)
    far_hops, near_hops = {}, {}
    for h in range(2):
        y_send[h] = far[:, h * 256:(h + 1) * 256]
    for p in range(PARTS):
        for h in range(2):
            far_hops[h, p] = hop(y_send, y_recv, y_send_sem, y_recv_sem, h, p)
            far_hops[h, p].start()
    for k in range(1, 4):
        own_part[k] = chip_sum(k)
    keys_of.step_far(0)
    for p in range(PARTS):
        for h in range(2):
            far_hops[h, p].wait_recv()
            own_part[1 + h, spans[p], pl.ds(h * 256, 256)] += y_recv[h, spans[p]].astype(F32)
            near_send[h, spans[p]] = own_part[1 + h, spans[p]].astype(BF)
            near_hops[h, p] = hop(near_send, near_recv, near_send_sem, near_recv_sem, h, p)
            near_hops[h, p].start()
    keys_of.finish(0)

    scale = 1.0 / math.sqrt(HS) * math.log2(math.e)
    blocks, first_step = [], []
    steps_before = 0
    for i in range(4):
        row = lax.min(x, mirror) if i < 2 else lax.max(x, mirror)
        pair = lax.select(row == x, c, c + 2)
        zq = pair if i % 2 == 0 else ZS - 1 - pair
        rank = row * ZS + zq
        blocks.append((row, zq, rank, lax.div(rank, 4)))
        first_step.append(steps_before)
        steps_before = steps_before + lax.div(rank, 4) + 1

    def key_block(buf, step, b):
        return buf[lax.div(step, 2), b % 2, lax.rem(step, 2) * 2 + b // 2]

    def score_all(i):
        row, zq, rank, last = blocks[i]
        pltpu.make_async_copy(q_buf.at[i], q_buf.at[i], q_recv_sem.at[i]).wait()
        query = q_buf[i]

        def score(step, top, masked=False):
            for b in range(KEYS // ROWS):
                s = nt(query, key_block(k_buf, step, b))
                if masked:
                    key_pos = across + step * KEYS + b * ROWS
                    s = jnp.where(key_pos <= down + rank * ROWS, s, NEG)
                scores[step, b] = s
                top = jnp.maximum(top, jnp.maximum(s[:, :128], s[:, 128:]))
            return top

        top = lax.fori_loop(0, last, score, jnp.full((ROWS, 128), NEG, F32))
        top = jnp.max(score(last, top, True), axis=1, keepdims=True)
        totals[i] = jnp.broadcast_to(top, (ROWS, 128))

    def weigh_all(i):
        row, zq, rank, last = blocks[i]
        totals_i = []
        for r in range(2):
            rows = slice(r * 128, (r + 1) * 128)
            top = totals[i, rows]

            def weight(step, total):
                for b in range(KEYS // ROWS):
                    for l in range(2):
                        w = jnp.exp2((scores[step, b, rows, l * 128:(l + 1) * 128] - top) * scale)
                        rounded[first_step[i] + step, rows, b * ROWS + l * 128:b * ROWS + (l + 1) * 128] = (
                            w.astype(BF)
                        )
                        total = total + w
                return total

            totals_i.append(lax.fori_loop(0, last + 1, weight, jnp.zeros((128, 128), F32)))
        for r in range(2):
            total = jnp.sum(totals_i[r], axis=1, keepdims=True)
            totals[i, r * 128:(r + 1) * 128] = jnp.broadcast_to(total, (128, 128))

    def values_out(p):
        for h in range(2):
            near_hops[h, p].wait_recv()
        mixed = (
            own_part[3, spans[p]] + near_recv[0, spans[p]].astype(F32) + near_recv[1, spans[p]].astype(F32)
        ).astype(BF)
        mine[spans[p]] = mixed
        values_of.scatter(mine, p, True)
        mixed_ref[spans[p]] = mixed

    for i in range(2):
        score_all(i)
        weigh_all(i)
    values_out(0)
    score_all(2)
    values_out(1)
    weigh_all(2)
    values_of.step_own(0)
    score_all(3)
    values_of.step_own(1)
    weigh_all(3)
    values_of.step_near(0)
    values_of.step_near(1)
    values_of.step_far(0)
    values_of.step_far(1)
    for p in range(PARTS):
        values_of.finish(p)

    def output_copies(i):
        row, zq, rank, last = blocks[i]
        core, j = lax.div(z, 4), lax.rem(z, 4)
        alone = (zq == z) & (core == c) & (row == x)
        local = lambda: pltpu.make_async_copy(o_send.at[i], o_recv.at[j], o_recv_sem.at[j])
        away = lambda: pltpu.make_async_remote_copy(
            src_ref=o_send.at[i], dst_ref=o_recv.at[j],
            send_sem=o_send_sem.at[i], recv_sem=o_recv_sem.at[j],
            device_id={"ctx": row * ZS + zq, "tp": y * 2 + core}, device_id_type=MESH,
        )
        return alone, local, away

    for i in range(4):
        row, zq, rank, last = blocks[i]

        def value(step, acc, i=i):
            part = jnp.concatenate([key_block(v_buf, step, b) for b in range(KEYS // ROWS)], axis=0)
            return acc + nn(rounded[first_step[i] + step], part)

        acc = lax.fori_loop(0, last + 1, value, jnp.zeros((ROWS, HS), F32))
        o_send[i] = (acc / totals[i]).astype(BF)
        start_either(*output_copies(i))

    for h in range(2):
        for kind in range(2):
            some = recv.at[kind, h, pl.ds(0, CTX - 1)]
            pltpu.make_async_copy(some, some, send_sem.at[kind, h]).wait()
        some = out_recv.at[h, pl.ds(0, CTX - 1)]
        pltpu.make_async_copy(some, some, back_send_sem.at[h]).wait()
    keys_of.scatter(keys_ref, 0, False)
    keys_of.drain(0)
    for p in range(PARTS):
        values_of.scatter(mine, p, False)
        values_of.drain(p)
        for h in range(2):
            far_hops[h, p].wait_send()
            near_hops[h, p].wait_send()
    for j in range(4):
        alone, local, away = query_copies(j)
        pl.when(jnp.logical_not(alone))(lambda away=away: away().wait_send())
        swaps[j].wait_send()
    for j in range(4):
        pltpu.make_async_copy(o_recv.at[j], o_recv.at[j], o_recv_sem.at[j]).wait()
        attended_ref[:, j * HS:(j + 1) * HS] = o_recv[j]
    for i in range(4):
        alone, local, away = output_copies(i)
        pl.when(jnp.logical_not(alone))(lambda away=away: away().wait_send())


def start_either(alone, local, away):
    pl.when(alone)(lambda: local().start())
    pl.when(jnp.logical_not(alone))(lambda: away().start())


def vmem(count):
    return [pl.BlockSpec(memory_space=pltpu.VMEM)] * count


def hbm(count):
    return [pl.BlockSpec(memory_space=pl.ANY)] * count


def hand_over(a, b, a_out, b_out):
    a_out[...] = a[...]
    b_out[...] = b[...]


def per_device(
    first_input, second_input, value_input, filter_taps, skip_gain, out_weight, queries, keys
):
    spread, mix, unmix, gather, turn_re, turn_im = tables()
    consts = [jnp.asarray(t) for t in (spread, mix, unmix, gather, np.concatenate([turn_re, turn_im]))]
    dma = lambda *shape: pltpu.SemaphoreType.DMA(shape)
    bf = lambda *shape: pltpu.VMEM(shape, BF)
    fl = lambda *shape: pltpu.VMEM(shape, F32)
    sems = lambda p: [dma(p, 4), dma(p), dma(p), dma(p), dma(2, p), dma(XS, p), dma(2, p)]
    out = jax.ShapeDtypeStruct((ROWS, HEAD), BF)
    mixed, attended = pl.pallas_call(
        whole_kernel,
        out_shape=(out, out),
        in_specs=hbm(13),
        out_specs=tuple(vmem(2)),
        scratch_shapes=[
            bf(2, 2, ROWS, 256), bf(2, 2, ROWS, 256), bf(2, 2, ROWS, 256), bf(2, 2, ROWS, 256),
            fl(1, 1024), bf(1024, 512), bf(512, 512), bf(512, 512), bf(512, 1024), fl(2 * CTX, ROWS),
            bf(2, 2, ROWS, 256),
            bf(2, 2, 2, 16, GROUP, ROWS), bf(2, 2, CTX, GROUP, ROWS), fl(512, 512),
            bf(2, CTX, GROUP, ROWS), bf(2, CTX, GROUP, ROWS),
            bf(ROWS, 1024),
            bf(8, 1024, HEAD), fl(8, ROWS, HEAD), fl(4, ROWS, HEAD), bf(4, ROWS, HEAD), bf(4, ROWS, HEAD),
            bf(2, ROWS, 256), bf(2, ROWS, 256), bf(2, ROWS, HEAD), bf(2, ROWS, HEAD), bf(ROWS, HEAD),
            bf(XS, 2, ZS // 2, ROWS, HS), bf(XS, 2, ZS // 2, ROWS, HS), bf(4, ROWS, HS),
            fl(TOTAL // KEYS, KEYS // ROWS, ROWS, ROWS), bf(CHUNKS, ROWS, KEYS), fl(4, ROWS, 128),
            bf(4, ROWS, HS), bf(4, ROWS, HS),
            dma(4, 4), dma(6), dma(2, 2), dma(2, 2), dma(2), dma(2),
            dma(8), dma(4), dma(4), dma(2, PARTS), dma(2, PARTS), dma(2, PARTS), dma(2, PARTS),
            dma(4), dma(4), dma(4), dma(4),
        ] + sems(1) + sems(PARTS),
        compiler_params=pltpu.CompilerParams(
            collective_id=0, has_side_effects=True, vmem_limit_bytes=60 * 1024 * 1024
        ),
        name="whole",
    )(first_input, second_input, value_input, filter_taps, skip_gain.reshape(1, 1024), out_weight,
      queries, keys, *consts)
    return pl.pallas_call(
        hand_over,
        out_shape=(out, out),
        in_specs=vmem(2),
        out_specs=tuple(vmem(2)),
        name="hand_over",
    )(mixed, attended)


def solution(mesh):
    return jax.shard_map(
        per_device,
        mesh=mesh,
        in_specs=(
            P("ctx", "tp"),
            P("ctx", "tp"),
            P("ctx", "tp"),
            P("ctx", "tp"),
            P("tp"),
            P("tp", None),
            P("ctx", "tp"),
            P("ctx", "tp"),
        ),
        out_specs=(P("ctx", "tp"), P("ctx", "tp")),
        check_vma=False,
    )
```

```python
import functools
import math

import jax
import jax.numpy as jnp
import numpy as np
from jax import lax
from jax.experimental import pallas as pl
from jax.experimental.pallas import tpu as pltpu
from jax.sharding import PartitionSpec as P

HS = 128
MESH = pl.DeviceIdType.MESH
BF = jnp.bfloat16
F32 = jnp.float32
CTX = 32
ROWS = 256
GROUP = 16
TOTAL = CTX * ROWS


def nt(a, b):
    return lax.dot_general(a, b, (((1,), (1,)), ((), ())), preferred_element_type=F32)


def nn(a, b):
    return jnp.dot(a, b, preferred_element_type=F32)


def tables():
    r = np.arange(CTX, dtype=np.float64)
    q = np.arange(CTX, dtype=np.float64)
    a = np.arange(ROWS, dtype=np.float64)
    rows = np.exp(-2j * np.pi * np.outer(q + 0.25, r) / CTX)
    turn = np.exp(-2j * np.pi * np.outer(q + 0.25, a) / TOTAL)
    cols = np.exp(-2j * np.pi * np.outer(a, a) / ROWS)
    eye = np.eye(GROUP)
    spread = lambda m: np.einsum("qr,cd->cqrd", m, eye).reshape(GROUP * CTX, CTX * GROUP)
    first = np.concatenate([spread(rows.real), spread(rows.imag)], axis=0)
    back = np.conj(rows).T
    gather = lambda m: np.einsum("rq,cd->rcdq", m, eye).reshape(CTX * GROUP, GROUP * CTX)
    last = np.concatenate([gather(back.real), -gather(back.imag)], axis=1)
    mix = np.block([[cols.real, cols.imag], [-cols.imag, cols.real]])
    unmix = np.block([[cols.real, -cols.imag], [cols.imag, cols.real]]) / TOTAL
    cast = lambda m: np.asarray(m, np.float32).astype(jnp.bfloat16)
    return (cast(first), cast(mix), cast(unmix), cast(last),
            np.asarray(turn.real, np.float32), np.asarray(turn.imag, np.float32))


def spectrum(x, first, mix, turn_re, turn_im):
    half = GROUP * CTX
    a = nn(first, x)
    a_re = a[:half].reshape(GROUP, CTX, ROWS)
    a_im = a[half:].reshape(GROUP, CTX, ROWS)
    z_re = (a_re * turn_re - a_im * turn_im).reshape(half, ROWS).astype(BF)
    z_im = (a_re * turn_im + a_im * turn_re).reshape(half, ROWS).astype(BF)
    return nn(jnp.concatenate([z_re, z_im], axis=1), mix)


XS, ZS, YS = 4, 8, 4
HEAD = 512
KEYS = 1024
NEG = -1e30


class Spread:
    def __init__(self, place, buf, parts, z_send, own, left, right, far, sib, sent):
        self.x, self.z, self.y, self.c = place
        self.buf, self.z_send, self.own, self.left, self.right, self.far, self.sib, self.sent = (
            buf, z_send, own, left, right, far, sib, sent
        )
        self.rows = ROWS // parts
        self.xl, self.xr, self.x2 = (lax.rem(self.x + k, XS) for k in (3, 1, 2))

    def device(self, x, z, c):
        return {"ctx": x * ZS + z, "tp": self.y * 2 + c}

    def span(self, p):
        return pl.ds(p * self.rows, self.rows)

    def scatter(self, source, p, start):
        x, z, c = self.x, self.z, self.c
        core = lax.rem(z, 2)
        for j in range(4):
            to = 4 * c + j
            alone = (to == z) & (core == c)
            part = source.at[self.span(p), pl.ds(j * HS, HS)]
            slot = self.buf.at[x, core, lax.div(z, 2), self.span(p)]
            local = lambda: pltpu.make_async_copy(part, slot, self.own.at[p])
            away = lambda: pltpu.make_async_remote_copy(
                src_ref=part, dst_ref=slot, send_sem=self.z_send.at[p, j], recv_sem=self.own.at[p],
                device_id=self.device(x, to, core), device_id_type=MESH,
            )
            if start:
                start_either(alone, local, away)
            else:
                pl.when(jnp.logical_not(alone))(lambda: away().wait_send())

    def push(self, block, p, x, c, sem, late=1):
        pltpu.make_async_remote_copy(
            src_ref=block, dst_ref=block, send_sem=self.sent.at[late, p], recv_sem=sem,
            device_id=self.device(x, self.z, c), device_id_type=MESH,
        ).start()

    def arrived(self, block, sem):
        pltpu.make_async_copy(block, block, sem).wait()

    def step_own(self, p):
        block = self.buf.at[self.x, self.c, :, self.span(p)]
        self.arrived(block, self.own.at[p])
        self.push(block, p, self.xr, self.c, self.left.at[p], 0)
        self.push(block, p, self.xl, self.c, self.right.at[p], 0)
        self.push(block, p, self.x, 1 - self.c, self.sib.at[self.x, p], 0)

    def half(self, x, p, h):
        return self.buf.at[x, self.c, :, pl.ds(p * self.rows + h * (self.rows // 2), self.rows // 2)]

    def step_near(self, p):
        for h, x, on, sem in ((0, self.xl, self.xr, self.left), (1, self.xr, self.xl, self.right)):
            block = self.buf.at[x, self.c, :, self.span(p)]
            self.arrived(block, sem.at[p])
            self.push(self.half(x, p, h), p, on, self.c, self.far.at[h, p])
            self.push(block, p, self.x, 1 - self.c, self.sib.at[x, p])

    def step_far(self, p):
        for h in range(2):
            half = self.half(self.x2, p, h)
            self.arrived(half, self.far.at[h, p])
            self.push(half, p, self.x, 1 - self.c, self.sib.at[self.x2, p])

    def finish(self, x, parts):
        for p in range(parts):
            self.arrived(self.buf.at[x, 1 - self.c, :, self.span(p)], self.sib.at[x, p])

    def drain(self, p):
        self.arrived(self.buf.at[pl.ds(0, 3), 0, :, self.span(p)], self.sent.at[0, p])
        self.arrived(self.buf.at[:, 0, :, self.span(p)], self.sent.at[1, p])


PARTS = 2
CHUNKS = 20


def whole_kernel(
    first_hbm, second_hbm, value_hbm, taps_hbm, skip_hbm, weight_ref, queries_ref, keys_ref,
    spread_hbm, mix_hbm, unmix_hbm, gather_hbm, turn_hbm, mixed_ref, attended_ref,
    first_in, value_in, taps_in, second_in, skip, spread_t, mix_t, unmix_t, gather_t, turn,
    product, send, recv, taps_spectrum, out_send, out_recv, gated_ref,
    weights, partial, own_part, sib_send, sib_recv, y_send, y_recv, near_send, near_recv, mine,
    k_buf, v_buf, q_buf, scores, rounded, totals, attended_sum, o_send, o_recv,
    in_sem, table_sem, send_sem, recv_sem, back_send_sem, back_recv_sem,
    w_sem, sib_send_sem, sib_recv_sem, y_send_sem, y_recv_sem, near_send_sem, near_recv_sem,
    q_send_sem, q_recv_sem, o_send_sem, o_recv_sem,
    kz, k_own, k_left, k_right, k_far, k_sib, k_sent,
    vz, v_own, v_left, v_right, v_far, v_sib, v_sent,
):
    me, tp = lax.axis_index("ctx"), lax.axis_index("tp")
    x, z = lax.div(me, ZS), lax.rem(me, ZS)
    y, c = lax.div(tp, 2), lax.rem(tp, 2)
    place = (x, z, y, c)
    keys_of = Spread(place, k_buf, 1, kz, k_own, k_left, k_right, k_far, k_sib, k_sent)
    values_of = Spread(place, v_buf, PARTS, vz, v_own, v_left, v_right, v_far, v_sib, v_sent)
    mirror = XS - 1 - x
    half = GROUP * CTX

    base = [lax.rem(lax.div(me, 16) + g, 2) * 16 for g in range(2)]
    cols_of = [
        [pl.ds(pl.multiple_of(h * 512 + base[g] * GROUP, 256), 256) for g in range(2)] for h in range(2)
    ]
    inputs = {}
    for h in range(2):
        for k, (hbm, into) in enumerate(
            ((taps_hbm, taps_in), (first_hbm, first_in), (value_hbm, value_in))
        ):
            for g in range(2):
                inputs[k, h, g] = pltpu.make_async_copy(
                    hbm.at[:, cols_of[h][g]], into.at[h, g], in_sem.at[k, 2 * h + g]
                )
                inputs[k, h, g].start()

    barrier = pltpu.get_barrier_semaphore()

    def greet(to_ctx, to_tp):
        pl.semaphore_signal(
            barrier, inc=1, device_id={"ctx": to_ctx, "tp": to_tp}, device_id_type=MESH
        )

    def greet_group(k, carry):
        greet(lax.rem(me + k, CTX), tp)
        return carry

    def greet_rows(k, carry):
        greet(x * ZS + k, y * 2 + 1 - c)
        greet(mirror * ZS + k, y * 2 + 1 - c)
        return carry

    lax.fori_loop(1, CTX, greet_group, 0)
    lax.fori_loop(0, ZS, greet_rows, 0)
    for k in (1, 3):
        greet(me, lax.rem(y + k, YS) * 2 + c)

    tables_in = []
    for k, (hbm, into) in enumerate((
        (spread_hbm, spread_t), (turn_hbm, turn), (mix_hbm, mix_t), (unmix_hbm, unmix_t),
        (gather_hbm, gather_t), (skip_hbm, skip),
    )):
        tables_in.append(pltpu.make_async_copy(hbm, into, table_sem.at[k]))
        tables_in[-1].start()
    gates_in = []
    for h in range(2):
        for g in range(2):
            gates_in.append(pltpu.make_async_copy(
                second_hbm.at[:, cols_of[h][g]], second_in.at[h, g], in_sem.at[3, 2 * h + g]
            ))
            gates_in[-1].start()

    def post_line(kind, h, g):
        def one(k, carry):
            o = lax.rem(me + k, 16)
            pltpu.make_async_remote_copy(
                src_ref=send.at[kind, h, g, o], dst_ref=recv.at[kind, h, me],
                send_sem=send_sem.at[kind, h], recv_sem=recv_sem.at[kind, h],
                device_id={"ctx": base[g] + o}, device_id_type=MESH,
            ).start()
            return carry

        if g == 0:
            pltpu.make_async_copy(
                send.at[kind, h, 0, lax.rem(me, 16)], recv.at[kind, h, me], recv_sem.at[kind, h]
            ).start()
        lax.fori_loop(1 if g == 0 else 0, 16, one, 0)

    down = lax.broadcasted_iota(jnp.int32, (ROWS, ROWS), 0)
    across = lax.broadcasted_iota(jnp.int32, (ROWS, ROWS), 1)
    eye = jnp.where(down == across, 1.0, 0.0).astype(BF)
    for h in range(2):
        for kind in (1, 0):
            for g in range(2):
                if kind == 1:
                    inputs[0, h, g].wait()
                    block = taps_in[h, g]
                else:
                    inputs[1, h, g].wait()
                    inputs[2, h, g].wait()
                    block = (first_in[h, g].astype(F32) * value_in[h, g].astype(F32)).astype(BF)
                    product[h, g] = block
                send[kind, h, g] = nt(eye, block).astype(BF).reshape(16, GROUP, ROWS)
                if (h, kind, g) == (0, 1, 0):
                    pl.semaphore_wait(barrier, CTX - 1 + 2 * ZS + 2)
                post_line(kind, h, g)
    keys_of.scatter(keys_ref, 0, True)

    order = [(other, lax.rem(y + k, YS)) for other in (1, 0) for k in (2, 1, 3, 0)]
    loads = []
    for k, (other, to_y) in enumerate(order):
        col = to_y * 2 + (1 - c if other else c)
        loads.append(pltpu.make_async_copy(
            weight_ref.at[:, pl.ds(pl.multiple_of(col * HEAD, HEAD), HEAD)], weights.at[k], w_sem.at[k]
        ))
        loads[-1].start()
    for copy in tables_in:
        copy.wait()

    for h in range(2):
        tr, ti = turn[:CTX], turn[CTX:]
        pltpu.make_async_copy(recv.at[1, h], recv.at[1, h], recv_sem.at[1, h]).wait()
        taps_spectrum[...] = spectrum(
            recv[1, h].reshape(half, ROWS), spread_t[...], mix_t[...], tr, ti
        )
        pltpu.make_async_copy(recv.at[0, h], recv.at[0, h], recv_sem.at[0, h]).wait()
        d = spectrum(recv[0, h].reshape(half, ROWS), spread_t[...], mix_t[...], tr, ti)
        e = taps_spectrum[...]
        d_re, d_im, e_re, e_im = d[:, :ROWS], d[:, ROWS:], e[:, :ROWS], e[:, ROWS:]
        y_re = (d_re * e_re - d_im * e_im).astype(BF)
        y_im = (d_re * e_im + d_im * e_re).astype(BF)
        b = nn(jnp.concatenate([y_re, y_im], axis=1), unmix_t[...])
        b_re = b[:, :ROWS].reshape(GROUP, CTX, ROWS)
        b_im = b[:, ROWS:].reshape(GROUP, CTX, ROWS)
        c_re = (b_re * tr + b_im * ti).reshape(half, ROWS).astype(BF)
        c_im = (b_im * tr - b_re * ti).reshape(half, ROWS).astype(BF)
        out = nn(gather_t[...], jnp.concatenate([c_re, c_im], axis=0))
        out_send[h] = out.astype(BF).reshape(CTX, GROUP, ROWS)

        def reply(k, carry, h=h):
            to = lax.rem(me + k, CTX)
            pltpu.make_async_remote_copy(
                src_ref=out_send.at[h, to], dst_ref=out_recv.at[h, me],
                send_sem=back_send_sem.at[h], recv_sem=back_recv_sem.at[h],
                device_id={"ctx": to}, device_id_type=MESH,
            ).start()
            return carry

        pltpu.make_async_copy(out_send.at[h, me], out_recv.at[h, me], back_recv_sem.at[h]).start()
        lax.fori_loop(1, CTX, reply, 0)
        if h == 0:
            keys_of.step_own(0)
        else:
            keys_of.step_near(0)

    for copy in gates_in:
        copy.wait()

    def gate(h):
        pltpu.make_async_copy(out_recv.at[h], out_recv.at[h], back_recv_sem.at[h]).wait()
        for g in range(2):
            block = out_recv[h, pl.ds(base[g], 16)].reshape(ROWS, ROWS)
            filtered = nt(eye, block).astype(BF).astype(F32)
            gated_ref[:, cols_of[h][g]] = (
                second_in[h, g].astype(F32)
                * (filtered + skip[:, cols_of[h][g]] * product[h, g].astype(F32))
            ).astype(BF)

    gate(0)
    low = gated_ref[:, :512]
    for k in range(8):
        loads[k].wait()
        partial[k] = nn(low, weights[k, :512])
    gate(1)
    high = gated_ref[:, 512:]

    def projected(k):
        return partial[k] + nn(high, weights[k, 512:])

    far_pair = lax.min(z, ZS - 1 - z)
    q_x = lax.select(far_pair < 2, x, mirror)
    q_core = lax.rem(far_pair, 2)
    q_slot = lax.div(x, 2) * 2 + lax.div(z, 4)

    def query_copies(j):
        to = 4 * c + j
        alone = (to == z) & (q_core == c) & (far_pair < 2)
        part = queries_ref.at[:, pl.ds(j * HS, HS)]
        slot = q_buf.at[q_slot]
        sem = q_recv_sem.at[q_slot]
        local = lambda: pltpu.make_async_copy(part, slot, sem)
        away = lambda: pltpu.make_async_remote_copy(
            src_ref=part, dst_ref=slot, send_sem=q_send_sem.at[j], recv_sem=sem,
            device_id={"ctx": q_x * ZS + to, "tp": y * 2 + q_core}, device_id_type=MESH,
        )
        return alone, local, away

    for j in range(4):
        start_either(*query_copies(j))

    swaps = []
    for k in range(4):
        sib_send[k] = projected(k).astype(BF)
        swaps.append(pltpu.make_async_remote_copy(
            src_ref=sib_send.at[k], dst_ref=sib_recv.at[k],
            send_sem=sib_send_sem.at[k], recv_sem=sib_recv_sem.at[k],
            device_id={"tp": y * 2 + 1 - c}, device_id_type=MESH,
        ))
        swaps[-1].start()

    def chip_sum(k):
        own = projected(4 + k)
        swaps[k].wait_recv()
        return own + sib_recv[k].astype(F32)

    right, left = lax.rem(y + 1, YS) * 2 + c, lax.rem(y + 3, YS) * 2 + c
    depth = ROWS // PARTS
    spans = [pl.ds(p * depth, depth) for p in range(PARTS)]

    def hop(source, into, send_sems, recv_sems, h, p):
        return pltpu.make_async_remote_copy(
            src_ref=source.at[h, spans[p]], dst_ref=into.at[h, spans[p]],
            send_sem=send_sems.at[h, p], recv_sem=recv_sems.at[h, p],
            device_id={"tp": (right, left)[h]}, device_id_type=MESH,
        )

    far = chip_sum(0).astype(BF)
    far_hops, near_hops = {}, {}
    for h in range(2):
        y_send[h] = far[:, h * 256:(h + 1) * 256]
    for p in range(PARTS):
        for h in range(2):
            far_hops[h, p] = hop(y_send, y_recv, y_send_sem, y_recv_sem, h, p)
            far_hops[h, p].start()
    for k in range(1, 4):
        own_part[k] = chip_sum(k)
    keys_of.step_far(0)
    for p in range(PARTS):
        for h in range(2):
            far_hops[h, p].wait_recv()
            own_part[1 + h, spans[p], pl.ds(h * 256, 256)] += y_recv[h, spans[p]].astype(F32)
            near_send[h, spans[p]] = own_part[1 + h, spans[p]].astype(BF)
            near_hops[h, p] = hop(near_send, near_recv, near_send_sem, near_recv_sem, h, p)
            near_hops[h, p].start()
    for row in range(XS):
        keys_of.finish(row, 1)

    scale = 1.0 / math.sqrt(HS) * math.log2(math.e)
    blocks, first_step = [], []
    steps_before = 0
    for i in range(4):
        row = lax.min(x, mirror) if i < 2 else lax.max(x, mirror)
        pair = lax.select(row == x, c, c + 2)
        zq = pair if i % 2 == 0 else ZS - 1 - pair
        rank = row * ZS + zq
        blocks.append((row, zq, rank, lax.div(rank, 4)))
        first_step.append(steps_before)
        steps_before = steps_before + lax.div(rank, 4) + 1

    def key_block(buf, step, b):
        return buf[lax.div(step, 2), b % 2, lax.rem(step, 2) * 2 + b // 2]

    def score_all(i):
        row, zq, rank, last = blocks[i]
        pltpu.make_async_copy(q_buf.at[i], q_buf.at[i], q_recv_sem.at[i]).wait()
        query = q_buf[i]

        def score(step, top, masked=False):
            for b in range(KEYS // ROWS):
                s = nt(query, key_block(k_buf, step, b))
                if masked:
                    key_pos = across + step * KEYS + b * ROWS
                    s = jnp.where(key_pos <= down + rank * ROWS, s, NEG)
                scores[step, b] = s
                top = jnp.maximum(top, jnp.maximum(s[:, :128], s[:, 128:]))
            return top

        top = lax.fori_loop(0, last, score, jnp.full((ROWS, 128), NEG, F32))
        top = jnp.max(score(last, top, True), axis=1, keepdims=True)
        totals[i] = jnp.broadcast_to(top, (ROWS, 128))

    def weigh_half(i, r):
        row, zq, rank, last = blocks[i]
        rows = slice(r * 128, (r + 1) * 128)
        top = totals[i, rows]

        def weight(step, total):
            for b in range(KEYS // ROWS):
                for l in range(2):
                    w = jnp.exp2((scores[step, b, rows, l * 128:(l + 1) * 128] - top) * scale)
                    rounded[first_step[i] + step, rows, b * ROWS + l * 128:b * ROWS + (l + 1) * 128] = (
                        w.astype(BF)
                    )
                    total = total + w
            return total

        total = lax.fori_loop(0, last + 1, weight, jnp.zeros((128, 128), F32))
        totals[i, rows] = jnp.broadcast_to(jnp.sum(total, axis=1, keepdims=True), (128, 128))

    def weigh_all(i):
        for r in range(2):
            weigh_half(i, r)

    def values_out(p):
        for h in range(2):
            near_hops[h, p].wait_recv()
        mixed = (
            own_part[3, spans[p]] + near_recv[0, spans[p]].astype(F32) + near_recv[1, spans[p]].astype(F32)
        ).astype(BF)
        mine[spans[p]] = mixed
        values_of.scatter(mine, p, True)
        mixed_ref[spans[p]] = mixed

    for i in range(2):
        score_all(i)
        weigh_all(i)
    values_out(0)
    score_all(2)
    values_out(1)
    weigh_all(2)
    values_of.step_own(0)
    score_all(3)
    values_of.step_own(1)
    weigh_half(3, 0)
    values_of.step_near(0)
    weigh_half(3, 1)
    values_of.step_near(1)

    def output_copies(i):
        row, zq, rank, last = blocks[i]
        core, j = lax.div(z, 4), lax.rem(z, 4)
        alone = (zq == z) & (core == c) & (row == x)
        local = lambda: pltpu.make_async_copy(o_send.at[i], o_recv.at[j], o_recv_sem.at[j])
        away = lambda: pltpu.make_async_remote_copy(
            src_ref=o_send.at[i], dst_ref=o_recv.at[j],
            send_sem=o_send_sem.at[i], recv_sem=o_recv_sem.at[j],
            device_id={"ctx": row * ZS + zq, "tp": y * 2 + core}, device_id_type=MESH,
        )
        return alone, local, away

    def attend_row(row, i, first=False):
        last = blocks[i][3]

        def value(step, acc):
            part = jnp.concatenate([key_block(v_buf, step, b) for b in range(KEYS // ROWS)], axis=0)
            return acc + nn(rounded[first_step[i] + step], part)

        start = jnp.zeros((ROWS, HS), F32) if first else attended_sum[i]
        attended_sum[i] = lax.fori_loop(2 * row, lax.min(2 * row + 2, last + 1), value, start)

    def output(i):
        o_send[i] = (attended_sum[i] / totals[i]).astype(BF)
        start_either(*output_copies(i))

    def output_low():
        output(0)
        output(1)

    xl, xr, x2 = values_of.xl, values_of.xr, values_of.x2
    values_of.finish(x, PARTS)
    for i in range(4):
        attend_row(x, i, True)
    values_of.step_far(0)
    values_of.step_far(1)
    for row in (xl, xr):
        values_of.finish(row, PARTS)
        for i in range(4):
            attend_row(row, i)
    pl.when(x != 2)(output_low)
    values_of.finish(x2, PARTS)
    for i in (2, 3):
        attend_row(x2, i)
        output(i)
    for i in (0, 1):
        attend_row(x2, i)
    pl.when(x == 2)(output_low)

    for h in range(2):
        for kind in range(2):
            some = recv.at[kind, h, pl.ds(0, CTX - 1)]
            pltpu.make_async_copy(some, some, send_sem.at[kind, h]).wait()
        some = out_recv.at[h, pl.ds(0, CTX - 1)]
        pltpu.make_async_copy(some, some, back_send_sem.at[h]).wait()
    keys_of.scatter(keys_ref, 0, False)
    keys_of.drain(0)
    for p in range(PARTS):
        values_of.scatter(mine, p, False)
        values_of.drain(p)
        for h in range(2):
            far_hops[h, p].wait_send()
            near_hops[h, p].wait_send()
    for j in range(4):
        alone, local, away = query_copies(j)
        pl.when(jnp.logical_not(alone))(lambda away=away: away().wait_send())
        swaps[j].wait_send()
    for j in range(4):
        pltpu.make_async_copy(o_recv.at[j], o_recv.at[j], o_recv_sem.at[j]).wait()
        attended_ref[:, j * HS:(j + 1) * HS] = o_recv[j]
    for i in range(4):
        alone, local, away = output_copies(i)
        pl.when(jnp.logical_not(alone))(lambda away=away: away().wait_send())


def start_either(alone, local, away):
    pl.when(alone)(lambda: local().start())
    pl.when(jnp.logical_not(alone))(lambda: away().start())


def vmem(count):
    return [pl.BlockSpec(memory_space=pltpu.VMEM)] * count


def hbm(count):
    return [pl.BlockSpec(memory_space=pl.ANY)] * count


def hand_over(a, b, a_out, b_out):
    a_out[...] = a[...]
    b_out[...] = b[...]


def per_device(
    first_input, second_input, value_input, filter_taps, skip_gain, out_weight, queries, keys
):
    spread, mix, unmix, gather, turn_re, turn_im = tables()
    consts = [jnp.asarray(t) for t in (spread, mix, unmix, gather, np.concatenate([turn_re, turn_im]))]
    dma = lambda *shape: pltpu.SemaphoreType.DMA(shape)
    bf = lambda *shape: pltpu.VMEM(shape, BF)
    fl = lambda *shape: pltpu.VMEM(shape, F32)
    sems = lambda p: [dma(p, 4), dma(p), dma(p), dma(p), dma(2, p), dma(XS, p), dma(2, p)]
    out = jax.ShapeDtypeStruct((ROWS, HEAD), BF)
    mixed, attended = pl.pallas_call(
        whole_kernel,
        out_shape=(out, out),
        in_specs=hbm(13),
        out_specs=tuple(vmem(2)),
        scratch_shapes=[
            bf(2, 2, ROWS, 256), bf(2, 2, ROWS, 256), bf(2, 2, ROWS, 256), bf(2, 2, ROWS, 256),
            fl(1, 1024), bf(1024, 512), bf(512, 512), bf(512, 512), bf(512, 1024), fl(2 * CTX, ROWS),
            bf(2, 2, ROWS, 256),
            bf(2, 2, 2, 16, GROUP, ROWS), bf(2, 2, CTX, GROUP, ROWS), fl(512, 512),
            bf(2, CTX, GROUP, ROWS), bf(2, CTX, GROUP, ROWS),
            bf(ROWS, 1024),
            bf(8, 1024, HEAD), fl(8, ROWS, HEAD), fl(4, ROWS, HEAD), bf(4, ROWS, HEAD), bf(4, ROWS, HEAD),
            bf(2, ROWS, 256), bf(2, ROWS, 256), bf(2, ROWS, HEAD), bf(2, ROWS, HEAD), bf(ROWS, HEAD),
            bf(XS, 2, ZS // 2, ROWS, HS), bf(XS, 2, ZS // 2, ROWS, HS), bf(4, ROWS, HS),
            fl(TOTAL // KEYS, KEYS // ROWS, ROWS, ROWS), bf(CHUNKS, ROWS, KEYS), fl(4, ROWS, 128), fl(4, ROWS, HS),
            bf(4, ROWS, HS), bf(4, ROWS, HS),
            dma(4, 4), dma(6), dma(2, 2), dma(2, 2), dma(2), dma(2),
            dma(8), dma(4), dma(4), dma(2, PARTS), dma(2, PARTS), dma(2, PARTS), dma(2, PARTS),
            dma(4), dma(4), dma(4), dma(4),
        ] + sems(1) + sems(PARTS),
        compiler_params=pltpu.CompilerParams(
            collective_id=0, has_side_effects=True, vmem_limit_bytes=60 * 1024 * 1024
        ),
        name="whole",
    )(first_input, second_input, value_input, filter_taps, skip_gain.reshape(1, 1024), out_weight,
      queries, keys, *consts)
    return pl.pallas_call(
        hand_over,
        out_shape=(out, out),
        in_specs=vmem(2),
        out_specs=tuple(vmem(2)),
        name="hand_over",
    )(mixed, attended)


def solution(mesh):
    return jax.shard_map(
        per_device,
        mesh=mesh,
        in_specs=(
            P("ctx", "tp"),
            P("ctx", "tp"),
            P("ctx", "tp"),
            P("ctx", "tp"),
            P("tp"),
            P("tp", None),
            P("ctx", "tp"),
            P("ctx", "tp"),
        ),
        out_specs=(P("ctx", "tp"), P("ctx", "tp")),
        check_vma=False,
    )
```

```python
import functools
import math

import jax
import jax.numpy as jnp
import numpy as np
from jax import lax
from jax.experimental import pallas as pl
from jax.experimental.pallas import tpu as pltpu
from jax.sharding import PartitionSpec as P

HS = 128
MESH = pl.DeviceIdType.MESH
BF = jnp.bfloat16
F32 = jnp.float32
CTX = 32
ROWS = 256
GROUP = 16
TOTAL = CTX * ROWS


def nt(a, b):
    return lax.dot_general(a, b, (((1,), (1,)), ((), ())), preferred_element_type=F32)


def nn(a, b):
    return jnp.dot(a, b, preferred_element_type=F32)


def tables():
    r = np.arange(CTX, dtype=np.float64)
    q = np.arange(CTX, dtype=np.float64)
    a = np.arange(ROWS, dtype=np.float64)
    rows = np.exp(-2j * np.pi * np.outer(q + 0.25, r) / CTX)
    turn = np.exp(-2j * np.pi * np.outer(q + 0.25, a) / TOTAL)
    cols = np.exp(-2j * np.pi * np.outer(a, a) / ROWS)
    parts = lambda m: np.concatenate([m.real, m.imag], axis=0)
    cast = lambda m: np.asarray(m, np.float32).astype(jnp.bfloat16)
    return (cast(np.repeat(parts(rows), GROUP, axis=1)), cast(parts(cols)),
            np.asarray(parts(turn), np.float32))


def build_tables(rows_ref, cols_ref, eye, spread_t, mix_t, unmix_t, gather_t):
    column = lax.rem(lax.broadcasted_iota(jnp.int32, (CTX, CTX * GROUP), 1), GROUP)
    half = GROUP * CTX
    for part in range(2):
        values = rows_ref[part * CTX:(part + 1) * CTX].astype(F32)
        for c in range(GROUP):
            at = part * half + c * CTX
            spread_t[at:at + CTX] = jnp.where(column == c, values, 0.0).astype(BF)
    for i in range(2):
        for j in range(4):
            a, b = slice(i * 256, (i + 1) * 256), slice(j * 256, (j + 1) * 256)
            gather_t[a, b] = nt(eye, spread_t[b, a]).astype(BF)
    re, im = cols_ref[:ROWS].astype(F32), cols_ref[ROWS:].astype(F32)
    top, low = slice(0, ROWS), slice(ROWS, 2 * ROWS)
    mix_t[top, top] = re.astype(BF)
    mix_t[low, low] = re.astype(BF)
    mix_t[top, low] = im.astype(BF)
    mix_t[low, top] = (-im).astype(BF)
    re, im = re * (1.0 / TOTAL), im * (1.0 / TOTAL)
    unmix_t[top, top] = re.astype(BF)
    unmix_t[low, low] = re.astype(BF)
    unmix_t[top, low] = (-im).astype(BF)
    unmix_t[low, top] = im.astype(BF)


def spectrum(x, first, mix, turn_re, turn_im):
    half = GROUP * CTX
    a = nn(first, x)
    a_re = a[:half].reshape(GROUP, CTX, ROWS)
    a_im = a[half:].reshape(GROUP, CTX, ROWS)
    z_re = (a_re * turn_re - a_im * turn_im).reshape(half, ROWS).astype(BF)
    z_im = (a_re * turn_im + a_im * turn_re).reshape(half, ROWS).astype(BF)
    return nn(jnp.concatenate([z_re, z_im], axis=1), mix)


XS, ZS, YS = 4, 8, 4
HEAD = 512
KEYS = 1024
NEG = -1e30


class Spread:
    def __init__(self, place, buf, parts, z_send, own, left, right, far, sib, sent):
        self.x, self.z, self.y, self.c = place
        self.buf, self.z_send, self.own, self.left, self.right, self.far, self.sib, self.sent = (
            buf, z_send, own, left, right, far, sib, sent
        )
        self.rows = ROWS // parts
        self.xl, self.xr, self.x2 = (lax.rem(self.x + k, XS) for k in (3, 1, 2))

    def device(self, x, z, c):
        return {"ctx": x * ZS + z, "tp": self.y * 2 + c}

    def span(self, p):
        return pl.ds(p * self.rows, self.rows)

    def scatter(self, source, p, start):
        x, z, c = self.x, self.z, self.c
        core = lax.rem(z, 2)
        for j in range(4):
            to = 4 * c + j
            alone = (to == z) & (core == c)
            part = source.at[self.span(p), pl.ds(j * HS, HS)]
            slot = self.buf.at[x, core, lax.div(z, 2), self.span(p)]
            local = lambda: pltpu.make_async_copy(part, slot, self.own.at[p])
            away = lambda: pltpu.make_async_remote_copy(
                src_ref=part, dst_ref=slot, send_sem=self.z_send.at[p, j], recv_sem=self.own.at[p],
                device_id=self.device(x, to, core), device_id_type=MESH,
            )
            if start:
                start_either(alone, local, away)
            else:
                pl.when(jnp.logical_not(alone))(lambda: away().wait_send())

    def push(self, block, p, x, c, sem, late=1):
        pltpu.make_async_remote_copy(
            src_ref=block, dst_ref=block, send_sem=self.sent.at[late, p], recv_sem=sem,
            device_id=self.device(x, self.z, c), device_id_type=MESH,
        ).start()

    def arrived(self, block, sem):
        pltpu.make_async_copy(block, block, sem).wait()

    def step_own(self, p):
        block = self.buf.at[self.x, self.c, :, self.span(p)]
        self.arrived(block, self.own.at[p])
        self.push(block, p, self.xr, self.c, self.left.at[p], 0)
        self.push(block, p, self.xl, self.c, self.right.at[p], 0)
        self.push(block, p, self.x, 1 - self.c, self.sib.at[self.x, p], 0)

    def half(self, x, p, h):
        return self.buf.at[x, self.c, :, pl.ds(p * self.rows + h * (self.rows // 2), self.rows // 2)]

    def step_near(self, p):
        for h, x, on, sem in ((0, self.xl, self.xr, self.left), (1, self.xr, self.xl, self.right)):
            block = self.buf.at[x, self.c, :, self.span(p)]
            self.arrived(block, sem.at[p])
            self.push(self.half(x, p, h), p, on, self.c, self.far.at[h, p])
            self.push(block, p, self.x, 1 - self.c, self.sib.at[x, p])

    def step_far(self, p):
        for h in range(2):
            half = self.half(self.x2, p, h)
            self.arrived(half, self.far.at[h, p])
            self.push(half, p, self.x, 1 - self.c, self.sib.at[self.x2, p])

    def finish(self, x, parts):
        for p in range(parts):
            self.arrived(self.buf.at[x, 1 - self.c, :, self.span(p)], self.sib.at[x, p])

    def drain(self, p):
        self.arrived(self.buf.at[pl.ds(0, 3), 0, :, self.span(p)], self.sent.at[0, p])
        self.arrived(self.buf.at[:, 0, :, self.span(p)], self.sent.at[1, p])


PARTS = 2
CHUNKS = 20


def whole_kernel(
    first_hbm, second_hbm, value_hbm, taps_hbm, skip_hbm, weight_ref, queries_ref, keys_ref,
    rows_hbm, cols_hbm, turn_hbm, mixed_ref, attended_ref,
    first_in, value_in, taps_in, second_in, skip, rows_in, cols_in, turn, spread_t, mix_t, unmix_t, gather_t,
    product, send, recv, taps_send, taps_recv, taps_spectrum, out_send, out_recv, gated_ref,
    weights, partial, own_part, sib_send, sib_recv, y_send, y_recv, near_send, near_recv, mine,
    k_buf, v_buf, q_buf, scores, rounded, totals, attended_sum, o_send, o_recv,
    in_sem, table_sem, taps_send_sem, taps_recv_sem, send_sem, recv_sem, back_send_sem, back_recv_sem,
    w_sem, sib_send_sem, sib_recv_sem, y_send_sem, y_recv_sem, near_send_sem, near_recv_sem,
    q_send_sem, q_recv_sem, o_send_sem, o_recv_sem,
    kz, k_own, k_left, k_right, k_far, k_sib, k_sent,
    vz, v_own, v_left, v_right, v_far, v_sib, v_sent,
):
    me, tp = lax.axis_index("ctx"), lax.axis_index("tp")
    x, z = lax.div(me, ZS), lax.rem(me, ZS)
    y, c = lax.div(tp, 2), lax.rem(tp, 2)
    place = (x, z, y, c)
    keys_of = Spread(place, k_buf, 1, kz, k_own, k_left, k_right, k_far, k_sib, k_sent)
    values_of = Spread(place, v_buf, PARTS, vz, v_own, v_left, v_right, v_far, v_sib, v_sent)
    mirror = XS - 1 - x
    half = GROUP * CTX

    base = [lax.rem(lax.div(me, 16) + g, 2) * 16 for g in range(2)]
    cols_of = [
        [pl.ds(pl.multiple_of(h * 512 + base[g] * GROUP, 256), 256) for g in range(2)] for h in range(2)
    ]
    inputs = {}

    def fetch(k, hbm, into, h, g):
        inputs[k, h, g] = pltpu.make_async_copy(
            hbm.at[:, cols_of[h][g]], into.at[h, g], in_sem.at[k, 2 * h + g]
        )
        inputs[k, h, g].start()

    for g in range(2):
        for h in range(2):
            fetch(0, taps_hbm, taps_in, h, g)
    for h in range(2):
        for g in range(2):
            fetch(1, first_hbm, first_in, h, g)
            fetch(2, value_hbm, value_in, h, g)

    barrier = pltpu.get_barrier_semaphore()

    def greet(to_ctx, to_tp):
        pl.semaphore_signal(
            barrier, inc=1, device_id={"ctx": to_ctx, "tp": to_tp}, device_id_type=MESH
        )

    def greet_group(k, carry):
        greet(lax.rem(me + k, CTX), tp)
        return carry

    def greet_rows(k, carry):
        greet(x * ZS + k, y * 2 + 1 - c)
        greet(mirror * ZS + k, y * 2 + 1 - c)
        return carry

    lax.fori_loop(1, CTX, greet_group, 0)
    lax.fori_loop(0, ZS, greet_rows, 0)
    for k in (1, 3):
        greet(me, lax.rem(y + k, YS) * 2 + c)

    tables_in = []
    for k, (hbm, into) in enumerate((
        (rows_hbm, rows_in), (cols_hbm, cols_in), (turn_hbm, turn), (skip_hbm, skip),
    )):
        tables_in.append(pltpu.make_async_copy(hbm, into, table_sem.at[k]))
        tables_in[-1].start()
    def post_line(source, into, send_sems, recv_sems, g):
        def one(k, carry):
            o = lax.rem(me + k, 16)
            pltpu.make_async_remote_copy(
                src_ref=source.at[g, o], dst_ref=into.at[me], send_sem=send_sems, recv_sem=recv_sems,
                device_id={"ctx": base[g] + o}, device_id_type=MESH,
            ).start()
            return carry

        if g == 0:
            pltpu.make_async_copy(source.at[0, lax.rem(me, 16)], into.at[me], recv_sems).start()
        lax.fori_loop(1 if g == 0 else 0, 16, one, 0)

    down = lax.broadcasted_iota(jnp.int32, (ROWS, ROWS), 0)
    across = lax.broadcasted_iota(jnp.int32, (ROWS, ROWS), 1)
    eye = jnp.where(down == across, 1.0, 0.0).astype(BF)
    for g in range(2):
        for h in range(2):
            inputs[0, h, g].wait()
            taps_send[g, :, h] = nt(eye, taps_in[h, g]).astype(BF).reshape(16, GROUP, ROWS)
        if g == 0:
            pl.semaphore_wait(barrier, CTX - 1 + 2 * ZS + 2)
        post_line(taps_send, taps_recv, taps_send_sem.at[0], taps_recv_sem.at[0], g)
    for h in range(2):
        for g in range(2):
            inputs[1, h, g].wait()
            inputs[2, h, g].wait()
            block = (first_in[h, g].astype(F32) * value_in[h, g].astype(F32)).astype(BF)
            product[h, g] = block
            send[h, g] = nt(eye, block).astype(BF).reshape(16, GROUP, ROWS)
            post_line(send.at[h], recv.at[h], send_sem.at[h], recv_sem.at[h], g)
    keys_of.scatter(keys_ref, 0, True)

    gates_in = []
    for h in range(2):
        for g in range(2):
            gates_in.append(pltpu.make_async_copy(
                second_hbm.at[:, cols_of[h][g]], second_in.at[h, g], in_sem.at[3, 2 * h + g]
            ))
            gates_in[-1].start()

    order = [(other, lax.rem(y + k, YS)) for other in (1, 0) for k in (2, 1, 3, 0)]
    loads = []
    for k, (other, to_y) in enumerate(order):
        col = to_y * 2 + (1 - c if other else c)
        loads.append(pltpu.make_async_copy(
            weight_ref.at[:, pl.ds(pl.multiple_of(col * HEAD, HEAD), HEAD)], weights.at[k], w_sem.at[k]
        ))
        loads[-1].start()
    for copy in tables_in:
        copy.wait()
    build_tables(rows_in, cols_in, eye, spread_t, mix_t, unmix_t, gather_t)
    pltpu.make_async_copy(taps_recv, taps_recv, taps_recv_sem.at[0]).wait()
    for h in range(2):
        taps_spectrum[h] = spectrum(
            taps_recv[:, h].reshape(half, ROWS), spread_t[...], mix_t[...], turn[:CTX], turn[CTX:]
        )

    for h in range(2):
        tr, ti = turn[:CTX], turn[CTX:]
        pltpu.make_async_copy(recv.at[h], recv.at[h], recv_sem.at[h]).wait()
        d = spectrum(recv[h].reshape(half, ROWS), spread_t[...], mix_t[...], tr, ti)
        e = taps_spectrum[h]
        d_re, d_im, e_re, e_im = d[:, :ROWS], d[:, ROWS:], e[:, :ROWS], e[:, ROWS:]
        y_re = (d_re * e_re - d_im * e_im).astype(BF)
        y_im = (d_re * e_im + d_im * e_re).astype(BF)
        b = nn(jnp.concatenate([y_re, y_im], axis=1), unmix_t[...])
        b_re = b[:, :ROWS].reshape(GROUP, CTX, ROWS)
        b_im = b[:, ROWS:].reshape(GROUP, CTX, ROWS)
        c_re = (b_re * tr + b_im * ti).reshape(half, ROWS).astype(BF)
        c_im = (b_im * tr - b_re * ti).reshape(half, ROWS).astype(BF)
        out = nn(gather_t[...], jnp.concatenate([c_re, c_im], axis=0))
        out_send[h] = out.astype(BF).reshape(CTX, GROUP, ROWS)

        def reply(k, carry, h=h):
            to = lax.rem(me + k, CTX)
            pltpu.make_async_remote_copy(
                src_ref=out_send.at[h, to], dst_ref=out_recv.at[h, me],
                send_sem=back_send_sem.at[h], recv_sem=back_recv_sem.at[h],
                device_id={"ctx": to}, device_id_type=MESH,
            ).start()
            return carry

        pltpu.make_async_copy(out_send.at[h, me], out_recv.at[h, me], back_recv_sem.at[h]).start()
        lax.fori_loop(1, CTX, reply, 0)
        if h == 0:
            keys_of.step_own(0)
        else:
            keys_of.step_near(0)

    for copy in gates_in:
        copy.wait()

    def gate(h):
        pltpu.make_async_copy(out_recv.at[h], out_recv.at[h], back_recv_sem.at[h]).wait()
        for g in range(2):
            block = out_recv[h, pl.ds(base[g], 16)].reshape(ROWS, ROWS)
            filtered = nt(eye, block).astype(BF).astype(F32)
            gated_ref[:, cols_of[h][g]] = (
                second_in[h, g].astype(F32)
                * (filtered + skip[:, cols_of[h][g]] * product[h, g].astype(F32))
            ).astype(BF)

    gate(0)
    low = gated_ref[:, :512]
    for k in range(8):
        loads[k].wait()
        partial[k] = nn(low, weights[k, :512])
    gate(1)
    high = gated_ref[:, 512:]

    def projected(k):
        return partial[k] + nn(high, weights[k, 512:])

    far_pair = lax.min(z, ZS - 1 - z)
    q_x = lax.select(far_pair < 2, x, mirror)
    q_core = lax.rem(far_pair, 2)
    q_slot = lax.div(x, 2) * 2 + lax.div(z, 4)

    def query_copies(j):
        to = 4 * c + j
        alone = (to == z) & (q_core == c) & (far_pair < 2)
        part = queries_ref.at[:, pl.ds(j * HS, HS)]
        slot = q_buf.at[q_slot]
        sem = q_recv_sem.at[q_slot]
        local = lambda: pltpu.make_async_copy(part, slot, sem)
        away = lambda: pltpu.make_async_remote_copy(
            src_ref=part, dst_ref=slot, send_sem=q_send_sem.at[j], recv_sem=sem,
            device_id={"ctx": q_x * ZS + to, "tp": y * 2 + q_core}, device_id_type=MESH,
        )
        return alone, local, away

    for j in range(4):
        start_either(*query_copies(j))

    swaps = []
    for k in range(4):
        sib_send[k] = projected(k).astype(BF)
        swaps.append(pltpu.make_async_remote_copy(
            src_ref=sib_send.at[k], dst_ref=sib_recv.at[k],
            send_sem=sib_send_sem.at[k], recv_sem=sib_recv_sem.at[k],
            device_id={"tp": y * 2 + 1 - c}, device_id_type=MESH,
        ))
        swaps[-1].start()

    def chip_sum(k):
        own = projected(4 + k)
        swaps[k].wait_recv()
        return own + sib_recv[k].astype(F32)

    right, left = lax.rem(y + 1, YS) * 2 + c, lax.rem(y + 3, YS) * 2 + c
    depth = ROWS // PARTS
    spans = [pl.ds(p * depth, depth) for p in range(PARTS)]

    def hop(source, into, send_sems, recv_sems, h, p):
        return pltpu.make_async_remote_copy(
            src_ref=source.at[h, spans[p]], dst_ref=into.at[h, spans[p]],
            send_sem=send_sems.at[h, p], recv_sem=recv_sems.at[h, p],
            device_id={"tp": (right, left)[h]}, device_id_type=MESH,
        )

    far = chip_sum(0).astype(BF)
    far_hops, near_hops = {}, {}
    for h in range(2):
        y_send[h] = far[:, h * 256:(h + 1) * 256]
    for p in range(PARTS):
        for h in range(2):
            far_hops[h, p] = hop(y_send, y_recv, y_send_sem, y_recv_sem, h, p)
            far_hops[h, p].start()
    for k in range(1, 4):
        own_part[k] = chip_sum(k)
    keys_of.step_far(0)
    for p in range(PARTS):
        for h in range(2):
            far_hops[h, p].wait_recv()
            own_part[1 + h, spans[p], pl.ds(h * 256, 256)] += y_recv[h, spans[p]].astype(F32)
            near_send[h, spans[p]] = own_part[1 + h, spans[p]].astype(BF)
            near_hops[h, p] = hop(near_send, near_recv, near_send_sem, near_recv_sem, h, p)
            near_hops[h, p].start()
    for row in range(XS):
        keys_of.finish(row, 1)

    scale = 1.0 / math.sqrt(HS) * math.log2(math.e)
    blocks, first_step = [], []
    steps_before = 0
    for i in range(4):
        row = lax.min(x, mirror) if i < 2 else lax.max(x, mirror)
        pair = lax.select(row == x, c, c + 2)
        zq = pair if i % 2 == 0 else ZS - 1 - pair
        rank = row * ZS + zq
        blocks.append((row, zq, rank, lax.div(rank, 4)))
        first_step.append(steps_before)
        steps_before = steps_before + lax.div(rank, 4) + 1

    def key_block(buf, step, b):
        return buf[lax.div(step, 2), b % 2, lax.rem(step, 2) * 2 + b // 2]

    def score_all(i):
        row, zq, rank, last = blocks[i]
        pltpu.make_async_copy(q_buf.at[i], q_buf.at[i], q_recv_sem.at[i]).wait()
        query = q_buf[i]

        def score(step, top, masked=False):
            for b in range(KEYS // ROWS):
                s = nt(query, key_block(k_buf, step, b))
                if masked:
                    key_pos = across + step * KEYS + b * ROWS
                    s = jnp.where(key_pos <= down + rank * ROWS, s, NEG)
                scores[step, b] = s
                top = jnp.maximum(top, jnp.maximum(s[:, :128], s[:, 128:]))
            return top

        top = lax.fori_loop(0, last, score, jnp.full((ROWS, 128), NEG, F32))
        top = jnp.max(score(last, top, True), axis=1, keepdims=True)
        totals[i] = jnp.broadcast_to(top, (ROWS, 128))

    def weigh_half(i, r):
        row, zq, rank, last = blocks[i]
        rows = slice(r * 128, (r + 1) * 128)
        top = totals[i, rows]

        def weight(step, total):
            for b in range(KEYS // ROWS):
                for l in range(2):
                    w = jnp.exp2((scores[step, b, rows, l * 128:(l + 1) * 128] - top) * scale)
                    rounded[first_step[i] + step, rows, b * ROWS + l * 128:b * ROWS + (l + 1) * 128] = (
                        w.astype(BF)
                    )
                    total = total + w
            return total

        total = lax.fori_loop(0, last + 1, weight, jnp.zeros((128, 128), F32))
        totals[i, rows] = jnp.broadcast_to(jnp.sum(total, axis=1, keepdims=True), (128, 128))

    def weigh_all(i):
        for r in range(2):
            weigh_half(i, r)

    def values_out(p):
        for h in range(2):
            near_hops[h, p].wait_recv()
        mixed = (
            own_part[3, spans[p]] + near_recv[0, spans[p]].astype(F32) + near_recv[1, spans[p]].astype(F32)
        ).astype(BF)
        mine[spans[p]] = mixed
        values_of.scatter(mine, p, True)
        mixed_ref[spans[p]] = mixed

    for i in range(2):
        score_all(i)
        weigh_all(i)
    values_out(0)
    score_all(2)
    values_out(1)
    weigh_all(2)
    values_of.step_own(0)
    score_all(3)
    values_of.step_own(1)
    weigh_half(3, 0)
    values_of.step_near(0)
    weigh_half(3, 1)
    values_of.step_near(1)

    def output_copies(i):
        row, zq, rank, last = blocks[i]
        core, j = lax.div(z, 4), lax.rem(z, 4)
        alone = (zq == z) & (core == c) & (row == x)
        local = lambda: pltpu.make_async_copy(o_send.at[i], o_recv.at[j], o_recv_sem.at[j])
        away = lambda: pltpu.make_async_remote_copy(
            src_ref=o_send.at[i], dst_ref=o_recv.at[j],
            send_sem=o_send_sem.at[i], recv_sem=o_recv_sem.at[j],
            device_id={"ctx": row * ZS + zq, "tp": y * 2 + core}, device_id_type=MESH,
        )
        return alone, local, away

    def attend_row(row, i, first=False):
        last = blocks[i][3]

        def value(step, acc):
            part = jnp.concatenate([key_block(v_buf, step, b) for b in range(KEYS // ROWS)], axis=0)
            return acc + nn(rounded[first_step[i] + step], part)

        start = jnp.zeros((ROWS, HS), F32) if first else attended_sum[i]
        attended_sum[i] = lax.fori_loop(2 * row, lax.min(2 * row + 2, last + 1), value, start)

    def output(i):
        o_send[i] = (attended_sum[i] / totals[i]).astype(BF)
        start_either(*output_copies(i))

    def output_low():
        output(0)
        output(1)

    xl, xr, x2 = values_of.xl, values_of.xr, values_of.x2
    values_of.finish(x, PARTS)
    for i in range(4):
        attend_row(x, i, True)
    values_of.step_far(0)
    values_of.step_far(1)
    for row in (xl, xr):
        values_of.finish(row, PARTS)
        for i in range(4):
            attend_row(row, i)
    pl.when(x != 2)(output_low)
    values_of.finish(x2, PARTS)
    for i in (2, 3):
        attend_row(x2, i)
        output(i)
    for i in (0, 1):
        attend_row(x2, i)
    pl.when(x == 2)(output_low)

    some = taps_recv.at[pl.ds(0, CTX - 1)]
    pltpu.make_async_copy(some, some, taps_send_sem.at[0]).wait()
    for h in range(2):
        some = recv.at[h, pl.ds(0, CTX - 1)]
        pltpu.make_async_copy(some, some, send_sem.at[h]).wait()
        some = out_recv.at[h, pl.ds(0, CTX - 1)]
        pltpu.make_async_copy(some, some, back_send_sem.at[h]).wait()
    keys_of.scatter(keys_ref, 0, False)
    keys_of.drain(0)
    for p in range(PARTS):
        values_of.scatter(mine, p, False)
        values_of.drain(p)
        for h in range(2):
            far_hops[h, p].wait_send()
            near_hops[h, p].wait_send()
    for j in range(4):
        alone, local, away = query_copies(j)
        pl.when(jnp.logical_not(alone))(lambda away=away: away().wait_send())
        swaps[j].wait_send()
    for j in range(4):
        pltpu.make_async_copy(o_recv.at[j], o_recv.at[j], o_recv_sem.at[j]).wait()
        attended_ref[:, j * HS:(j + 1) * HS] = o_recv[j]
    for i in range(4):
        alone, local, away = output_copies(i)
        pl.when(jnp.logical_not(alone))(lambda away=away: away().wait_send())


def start_either(alone, local, away):
    pl.when(alone)(lambda: local().start())
    pl.when(jnp.logical_not(alone))(lambda: away().start())


def vmem(count):
    return [pl.BlockSpec(memory_space=pltpu.VMEM)] * count


def hbm(count):
    return [pl.BlockSpec(memory_space=pl.ANY)] * count


def hand_over(a, b, a_out, b_out):
    a_out[...] = a[...]
    b_out[...] = b[...]


def per_device(
    first_input, second_input, value_input, filter_taps, skip_gain, out_weight, queries, keys
):
    consts = [jnp.asarray(t) for t in tables()]
    dma = lambda *shape: pltpu.SemaphoreType.DMA(shape)
    bf = lambda *shape: pltpu.VMEM(shape, BF)
    fl = lambda *shape: pltpu.VMEM(shape, F32)
    sems = lambda p: [dma(p, 4), dma(p), dma(p), dma(p), dma(2, p), dma(XS, p), dma(2, p)]
    out = jax.ShapeDtypeStruct((ROWS, HEAD), BF)
    mixed, attended = pl.pallas_call(
        whole_kernel,
        out_shape=(out, out),
        in_specs=hbm(11),
        out_specs=tuple(vmem(2)),
        scratch_shapes=[
            bf(2, 2, ROWS, 256), bf(2, 2, ROWS, 256), bf(2, 2, ROWS, 256), bf(2, 2, ROWS, 256),
            fl(1, 1024), bf(2 * CTX, 512), bf(512, 256), fl(2 * CTX, ROWS),
            bf(1024, 512), bf(512, 512), bf(512, 512), bf(512, 1024),
            bf(2, 2, ROWS, 256),
            bf(2, 2, 16, GROUP, ROWS), bf(2, CTX, GROUP, ROWS),
            bf(2, 16, 2, GROUP, ROWS), bf(CTX, 2, GROUP, ROWS), fl(2, 512, 512),
            bf(2, CTX, GROUP, ROWS), bf(2, CTX, GROUP, ROWS),
            bf(ROWS, 1024),
            bf(8, 1024, HEAD), fl(8, ROWS, HEAD), fl(4, ROWS, HEAD), bf(4, ROWS, HEAD), bf(4, ROWS, HEAD),
            bf(2, ROWS, 256), bf(2, ROWS, 256), bf(2, ROWS, HEAD), bf(2, ROWS, HEAD), bf(ROWS, HEAD),
            bf(XS, 2, ZS // 2, ROWS, HS), bf(XS, 2, ZS // 2, ROWS, HS), bf(4, ROWS, HS),
            fl(TOTAL // KEYS, KEYS // ROWS, ROWS, ROWS), bf(CHUNKS, ROWS, KEYS), fl(4, ROWS, 128), fl(4, ROWS, HS),
            bf(4, ROWS, HS), bf(4, ROWS, HS),
            dma(4, 4), dma(4), dma(1), dma(1), dma(2), dma(2), dma(2), dma(2),
            dma(8), dma(4), dma(4), dma(2, PARTS), dma(2, PARTS), dma(2, PARTS), dma(2, PARTS),
            dma(4), dma(4), dma(4), dma(4),
        ] + sems(1) + sems(PARTS),
        compiler_params=pltpu.CompilerParams(
            collective_id=0, has_side_effects=True, vmem_limit_bytes=60 * 1024 * 1024
        ),
        name="whole",
    )(first_input, second_input, value_input, filter_taps, skip_gain.reshape(1, 1024), out_weight,
      queries, keys, *consts)
    return pl.pallas_call(
        hand_over,
        out_shape=(out, out),
        in_specs=vmem(2),
        out_specs=tuple(vmem(2)),
        name="hand_over",
    )(mixed, attended)


def solution(mesh):
    return jax.shard_map(
        per_device,
        mesh=mesh,
        in_specs=(
            P("ctx", "tp"),
            P("ctx", "tp"),
            P("ctx", "tp"),
            P("ctx", "tp"),
            P("tp"),
            P("tp", None),
            P("ctx", "tp"),
            P("ctx", "tp"),
        ),
        out_specs=(P("ctx", "tp"), P("ctx", "tp")),
        check_vma=False,
    )
```

```python
import functools
import math

import jax
import jax.numpy as jnp
import numpy as np
from jax import lax
from jax.experimental import pallas as pl
from jax.experimental.pallas import tpu as pltpu
from jax.sharding import PartitionSpec as P

HS = 128
MESH = pl.DeviceIdType.MESH
BF = jnp.bfloat16
F32 = jnp.float32
CTX = 32
ROWS = 256
GROUP = 16
TOTAL = CTX * ROWS


def nt(a, b):
    return lax.dot_general(a, b, (((1,), (1,)), ((), ())), preferred_element_type=F32)


def nn(a, b):
    return jnp.dot(a, b, preferred_element_type=F32)


def tables():
    r = np.arange(CTX, dtype=np.float64)
    q = np.arange(CTX, dtype=np.float64)
    a = np.arange(ROWS, dtype=np.float64)
    rows = np.exp(-2j * np.pi * np.outer(q + 0.25, r) / CTX)
    turn = np.exp(-2j * np.pi * np.outer(q + 0.25, a) / TOTAL)
    cols = np.exp(-2j * np.pi * np.outer(a, a) / ROWS)
    parts = lambda m: np.concatenate([m.real, m.imag], axis=0)
    cast = lambda m: np.asarray(m, np.float32).astype(jnp.bfloat16)
    return (cast(np.repeat(parts(rows), GROUP, axis=1)), cast(parts(cols)),
            np.asarray(parts(turn), np.float32))


def build_tables(rows_ref, cols_ref, eye, spread_t, mix_t, unmix_t, gather_t):
    column = lax.rem(lax.broadcasted_iota(jnp.int32, (CTX, CTX * GROUP), 1), GROUP)
    half = GROUP * CTX
    for part in range(2):
        values = rows_ref[part * CTX:(part + 1) * CTX].astype(F32)
        for c in range(GROUP):
            at = part * half + c * CTX
            spread_t[at:at + CTX] = jnp.where(column == c, values, 0.0).astype(BF)
    for i in range(2):
        for j in range(4):
            a, b = slice(i * 256, (i + 1) * 256), slice(j * 256, (j + 1) * 256)
            gather_t[a, b] = nt(eye, spread_t[b, a]).astype(BF)
    re, im = cols_ref[:ROWS].astype(F32), cols_ref[ROWS:].astype(F32)
    top, low = slice(0, ROWS), slice(ROWS, 2 * ROWS)
    mix_t[top, top] = re.astype(BF)
    mix_t[low, low] = re.astype(BF)
    mix_t[top, low] = im.astype(BF)
    mix_t[low, top] = (-im).astype(BF)
    re, im = re * (1.0 / TOTAL), im * (1.0 / TOTAL)
    unmix_t[top, top] = re.astype(BF)
    unmix_t[low, low] = re.astype(BF)
    unmix_t[top, low] = (-im).astype(BF)
    unmix_t[low, top] = im.astype(BF)


def spectrum(x, first, mix, turn_re, turn_im):
    half = GROUP * CTX
    a = nn(first, x)
    a_re = a[:half].reshape(GROUP, CTX, ROWS)
    a_im = a[half:].reshape(GROUP, CTX, ROWS)
    z_re = (a_re * turn_re - a_im * turn_im).reshape(half, ROWS).astype(BF)
    z_im = (a_re * turn_im + a_im * turn_re).reshape(half, ROWS).astype(BF)
    return nn(jnp.concatenate([z_re, z_im], axis=1), mix)


XS, ZS, YS = 4, 8, 4
HEAD = 512
KEYS = 1024
NEG = -1e30


class Spread:
    def __init__(self, place, buf, parts, z_send, own, left, right, far, sib, sent):
        self.x, self.z, self.y, self.c = place
        self.buf, self.z_send, self.own, self.left, self.right, self.far, self.sib, self.sent = (
            buf, z_send, own, left, right, far, sib, sent
        )
        self.rows = ROWS // parts
        self.xl, self.xr, self.x2 = (lax.rem(self.x + k, XS) for k in (3, 1, 2))

    def device(self, x, z, c):
        return {"ctx": x * ZS + z, "tp": self.y * 2 + c}

    def span(self, p):
        return pl.ds(p * self.rows, self.rows)

    def scatter(self, source, p, start):
        x, z, c = self.x, self.z, self.c
        core = lax.rem(z, 2)
        for j in range(4):
            to = 4 * c + j
            alone = (to == z) & (core == c)
            part = source.at[self.span(p), pl.ds(j * HS, HS)]
            slot = self.buf.at[x, core, lax.div(z, 2), self.span(p)]
            local = lambda: pltpu.make_async_copy(part, slot, self.own.at[p])
            away = lambda: pltpu.make_async_remote_copy(
                src_ref=part, dst_ref=slot, send_sem=self.z_send.at[p, j], recv_sem=self.own.at[p],
                device_id=self.device(x, to, core), device_id_type=MESH,
            )
            if start:
                start_either(alone, local, away)
            else:
                pl.when(jnp.logical_not(alone))(lambda: away().wait_send())

    def push(self, block, p, x, c, sem, late=1):
        pltpu.make_async_remote_copy(
            src_ref=block, dst_ref=block, send_sem=self.sent.at[late, p], recv_sem=sem,
            device_id=self.device(x, self.z, c), device_id_type=MESH,
        ).start()

    def arrived(self, block, sem):
        pltpu.make_async_copy(block, block, sem).wait()

    def step_own(self, p):
        block = self.buf.at[self.x, self.c, :, self.span(p)]
        self.arrived(block, self.own.at[p])
        self.push(block, p, self.xr, self.c, self.left.at[p], 0)
        self.push(block, p, self.xl, self.c, self.right.at[p], 0)
        self.push(block, p, self.x, 1 - self.c, self.sib.at[self.x, p], 0)

    def half(self, x, p, h):
        return self.buf.at[x, self.c, :, pl.ds(p * self.rows + h * (self.rows // 2), self.rows // 2)]

    def step_near(self, p):
        for h, x, on, sem in ((0, self.xl, self.xr, self.left), (1, self.xr, self.xl, self.right)):
            block = self.buf.at[x, self.c, :, self.span(p)]
            self.arrived(block, sem.at[p])
            self.push(self.half(x, p, h), p, on, self.c, self.far.at[h, p])
            self.push(block, p, self.x, 1 - self.c, self.sib.at[x, p])

    def step_far(self, p):
        for h in range(2):
            half = self.half(self.x2, p, h)
            self.arrived(half, self.far.at[h, p])
            self.push(half, p, self.x, 1 - self.c, self.sib.at[self.x2, p])

    def finish(self, x, parts):
        for p in range(parts):
            self.arrived(self.buf.at[x, 1 - self.c, :, self.span(p)], self.sib.at[x, p])

    def drain(self, p):
        self.arrived(self.buf.at[pl.ds(0, 3), 0, :, self.span(p)], self.sent.at[0, p])
        self.arrived(self.buf.at[:, 0, :, self.span(p)], self.sent.at[1, p])


PARTS = 2
CHUNKS = 20


def whole_kernel(
    first_hbm, second_hbm, value_hbm, taps_hbm, skip_hbm, weight_ref, queries_ref, keys_ref,
    rows_hbm, cols_hbm, turn_hbm, mixed_ref, attended_ref,
    first_in, value_in, taps_in, second_in, skip, rows_in, cols_in, turn, spread_t, mix_t, unmix_t, gather_t,
    product, send, recv, taps_send, taps_recv, taps_spectrum, out_send, out_recv, gated_ref,
    weights, partial, own_part, sib_send, sib_recv, y_send, y_recv, near_send, near_recv, mine,
    k_buf, v_buf, q_buf, scores, rounded, totals, attended_sum, o_send, o_recv,
    in_sem, table_sem, taps_send_sem, taps_recv_sem, send_sem, recv_sem, back_send_sem, back_recv_sem,
    w_sem, sib_send_sem, sib_recv_sem, y_send_sem, y_recv_sem, near_send_sem, near_recv_sem,
    q_send_sem, q_recv_sem, o_send_sem, o_recv_sem,
    kz, k_own, k_left, k_right, k_far, k_sib, k_sent,
    vz, v_own, v_left, v_right, v_far, v_sib, v_sent,
):
    me, tp = lax.axis_index("ctx"), lax.axis_index("tp")
    x, z = lax.div(me, ZS), lax.rem(me, ZS)
    y, c = lax.div(tp, 2), lax.rem(tp, 2)
    place = (x, z, y, c)
    keys_of = Spread(place, k_buf, 1, kz, k_own, k_left, k_right, k_far, k_sib, k_sent)
    values_of = Spread(place, v_buf, PARTS, vz, v_own, v_left, v_right, v_far, v_sib, v_sent)
    mirror = XS - 1 - x
    half = GROUP * CTX

    base = [lax.rem(lax.div(me, 16) + g, 2) * 16 for g in range(2)]
    cols_of = [
        [pl.ds(pl.multiple_of(h * 512 + base[g] * GROUP, 256), 256) for g in range(2)] for h in range(2)
    ]
    inputs = {}

    def fetch(k, hbm, into, h, g):
        inputs[k, h, g] = pltpu.make_async_copy(
            hbm.at[:, cols_of[h][g]], into.at[h, g], in_sem.at[k, 2 * h + g]
        )
        inputs[k, h, g].start()

    for g in range(2):
        for h in range(2):
            fetch(0, taps_hbm, taps_in, h, g)
    for h in range(2):
        for g in range(2):
            fetch(1, first_hbm, first_in, h, g)
            fetch(2, value_hbm, value_in, h, g)

    barrier = pltpu.get_barrier_semaphore()

    def greet(to_ctx, to_tp):
        pl.semaphore_signal(
            barrier, inc=1, device_id={"ctx": to_ctx, "tp": to_tp}, device_id_type=MESH
        )

    def greet_group(k, carry):
        greet(lax.rem(me + k, CTX), tp)
        return carry

    def greet_rows(k, carry):
        greet(x * ZS + k, y * 2 + 1 - c)
        greet(mirror * ZS + k, y * 2 + 1 - c)
        return carry

    lax.fori_loop(1, CTX, greet_group, 0)
    lax.fori_loop(0, ZS, greet_rows, 0)
    for k in (1, 3):
        greet(me, lax.rem(y + k, YS) * 2 + c)

    tables_in = []
    for k, (hbm, into) in enumerate((
        (rows_hbm, rows_in), (cols_hbm, cols_in), (turn_hbm, turn), (skip_hbm, skip),
    )):
        tables_in.append(pltpu.make_async_copy(hbm, into, table_sem.at[k]))
        tables_in[-1].start()
    def post_line(source, into, send_sems, recv_sems, g):
        def one(k, carry):
            o = lax.rem(me + k, 16)
            pltpu.make_async_remote_copy(
                src_ref=source.at[g, o], dst_ref=into.at[me], send_sem=send_sems, recv_sem=recv_sems,
                device_id={"ctx": base[g] + o}, device_id_type=MESH,
            ).start()
            return carry

        if g == 0:
            pltpu.make_async_copy(source.at[0, lax.rem(me, 16)], into.at[me], recv_sems).start()
        lax.fori_loop(1 if g == 0 else 0, 16, one, 0)

    down = lax.broadcasted_iota(jnp.int32, (ROWS, ROWS), 0)
    across = lax.broadcasted_iota(jnp.int32, (ROWS, ROWS), 1)
    eye = jnp.where(down == across, 1.0, 0.0).astype(BF)
    for g in range(2):
        for h in range(2):
            inputs[0, h, g].wait()
            taps_send[g, :, h] = nt(eye, taps_in[h, g]).astype(BF).reshape(16, GROUP, ROWS)
        if g == 0:
            pl.semaphore_wait(barrier, CTX - 1 + 2 * ZS + 2)
        post_line(taps_send, taps_recv, taps_send_sem.at[0], taps_recv_sem.at[0], g)
    for h in range(2):
        for g in range(2):
            inputs[1, h, g].wait()
            inputs[2, h, g].wait()
            block = (first_in[h, g].astype(F32) * value_in[h, g].astype(F32)).astype(BF)
            product[h, g] = block
            send[h, g] = nt(eye, block).astype(BF).reshape(16, GROUP, ROWS)
            post_line(send.at[h], recv.at[h], send_sem.at[h], recv_sem.at[h], g)

    gates_in = []
    for h in range(2):
        for g in range(2):
            gates_in.append(pltpu.make_async_copy(
                second_hbm.at[:, cols_of[h][g]], second_in.at[h, g], in_sem.at[3, 2 * h + g]
            ))
            gates_in[-1].start()

    order = [(other, lax.rem(y + k, YS)) for other in (1, 0) for k in (2, 1, 3, 0)]
    loads = []
    for k, (other, to_y) in enumerate(order):
        col = to_y * 2 + (1 - c if other else c)
        loads.append(pltpu.make_async_copy(
            weight_ref.at[:, pl.ds(pl.multiple_of(col * HEAD, HEAD), HEAD)], weights.at[k], w_sem.at[k]
        ))
        loads[-1].start()
    for copy in tables_in:
        copy.wait()
    build_tables(rows_in, cols_in, eye, spread_t, mix_t, unmix_t, gather_t)
    pltpu.make_async_copy(taps_recv, taps_recv, taps_recv_sem.at[0]).wait()
    for h in range(2):
        taps_spectrum[h] = spectrum(
            taps_recv[:, h].reshape(half, ROWS), spread_t[...], mix_t[...], turn[:CTX], turn[CTX:]
        )

    for h in range(2):
        tr, ti = turn[:CTX], turn[CTX:]
        pltpu.make_async_copy(recv.at[h], recv.at[h], recv_sem.at[h]).wait()
        if h == 1:
            keys_of.scatter(keys_ref, 0, True)
        d = spectrum(recv[h].reshape(half, ROWS), spread_t[...], mix_t[...], tr, ti)
        e = taps_spectrum[h]
        d_re, d_im, e_re, e_im = d[:, :ROWS], d[:, ROWS:], e[:, :ROWS], e[:, ROWS:]
        y_re = (d_re * e_re - d_im * e_im).astype(BF)
        y_im = (d_re * e_im + d_im * e_re).astype(BF)
        b = nn(jnp.concatenate([y_re, y_im], axis=1), unmix_t[...])
        b_re = b[:, :ROWS].reshape(GROUP, CTX, ROWS)
        b_im = b[:, ROWS:].reshape(GROUP, CTX, ROWS)
        c_re = (b_re * tr + b_im * ti).reshape(half, ROWS).astype(BF)
        c_im = (b_im * tr - b_re * ti).reshape(half, ROWS).astype(BF)
        out = nn(gather_t[...], jnp.concatenate([c_re, c_im], axis=0))
        out_send[h] = out.astype(BF).reshape(CTX, GROUP, ROWS)

        def reply(k, carry, h=h):
            to = lax.rem(me + k, CTX)
            pltpu.make_async_remote_copy(
                src_ref=out_send.at[h, to], dst_ref=out_recv.at[h, me],
                send_sem=back_send_sem.at[h], recv_sem=back_recv_sem.at[h],
                device_id={"ctx": to}, device_id_type=MESH,
            ).start()
            return carry

        pltpu.make_async_copy(out_send.at[h, me], out_recv.at[h, me], back_recv_sem.at[h]).start()
        lax.fori_loop(1, CTX, reply, 0)

    for copy in gates_in:
        copy.wait()

    def gate(h):
        pltpu.make_async_copy(out_recv.at[h], out_recv.at[h], back_recv_sem.at[h]).wait()
        for g in range(2):
            block = out_recv[h, pl.ds(base[g], 16)].reshape(ROWS, ROWS)
            filtered = nt(eye, block).astype(BF).astype(F32)
            gated_ref[:, cols_of[h][g]] = (
                second_in[h, g].astype(F32)
                * (filtered + skip[:, cols_of[h][g]] * product[h, g].astype(F32))
            ).astype(BF)

    gate(0)
    low = gated_ref[:, :512]
    for k in range(8):
        loads[k].wait()
        partial[k] = nn(low, weights[k, :512])
    keys_of.step_own(0)
    gate(1)
    high = gated_ref[:, 512:]

    def projected(k):
        return partial[k] + nn(high, weights[k, 512:])

    far_pair = lax.min(z, ZS - 1 - z)
    q_x = lax.select(far_pair < 2, x, mirror)
    q_core = lax.rem(far_pair, 2)
    q_slot = lax.div(x, 2) * 2 + lax.div(z, 4)

    def query_copies(j):
        to = 4 * c + j
        alone = (to == z) & (q_core == c) & (far_pair < 2)
        part = queries_ref.at[:, pl.ds(j * HS, HS)]
        slot = q_buf.at[q_slot]
        sem = q_recv_sem.at[q_slot]
        local = lambda: pltpu.make_async_copy(part, slot, sem)
        away = lambda: pltpu.make_async_remote_copy(
            src_ref=part, dst_ref=slot, send_sem=q_send_sem.at[j], recv_sem=sem,
            device_id={"ctx": q_x * ZS + to, "tp": y * 2 + q_core}, device_id_type=MESH,
        )
        return alone, local, away

    for j in range(4):
        start_either(*query_copies(j))

    swaps = []
    for k in range(4):
        sib_send[k] = projected(k).astype(BF)
        swaps.append(pltpu.make_async_remote_copy(
            src_ref=sib_send.at[k], dst_ref=sib_recv.at[k],
            send_sem=sib_send_sem.at[k], recv_sem=sib_recv_sem.at[k],
            device_id={"tp": y * 2 + 1 - c}, device_id_type=MESH,
        ))
        swaps[-1].start()

    def chip_sum(k):
        own = projected(4 + k)
        swaps[k].wait_recv()
        return own + sib_recv[k].astype(F32)

    right, left = lax.rem(y + 1, YS) * 2 + c, lax.rem(y + 3, YS) * 2 + c
    depth = ROWS // PARTS
    spans = [pl.ds(p * depth, depth) for p in range(PARTS)]

    def hop(source, into, send_sems, recv_sems, h, p):
        return pltpu.make_async_remote_copy(
            src_ref=source.at[h, spans[p]], dst_ref=into.at[h, spans[p]],
            send_sem=send_sems.at[h, p], recv_sem=recv_sems.at[h, p],
            device_id={"tp": (right, left)[h]}, device_id_type=MESH,
        )

    far = chip_sum(0).astype(BF)
    far_hops, near_hops = {}, {}
    for h in range(2):
        y_send[h] = far[:, h * 256:(h + 1) * 256]
    for p in range(PARTS):
        for h in range(2):
            far_hops[h, p] = hop(y_send, y_recv, y_send_sem, y_recv_sem, h, p)
            far_hops[h, p].start()
    for k in range(1, 4):
        own_part[k] = chip_sum(k)
    keys_of.step_near(0)
    for p in range(PARTS):
        for h in range(2):
            far_hops[h, p].wait_recv()
            own_part[1 + h, spans[p], pl.ds(h * 256, 256)] += y_recv[h, spans[p]].astype(F32)
            near_send[h, spans[p]] = own_part[1 + h, spans[p]].astype(BF)
            near_hops[h, p] = hop(near_send, near_recv, near_send_sem, near_recv_sem, h, p)
            near_hops[h, p].start()
    keys_of.step_far(0)

    scale = 1.0 / math.sqrt(HS) * math.log2(math.e)
    blocks, first_step = [], []
    steps_before = 0
    for i in range(4):
        row = lax.min(x, mirror) if i < 2 else lax.max(x, mirror)
        pair = lax.select(row == x, c, c + 2)
        zq = pair if i % 2 == 0 else ZS - 1 - pair
        rank = row * ZS + zq
        blocks.append((row, zq, rank, lax.div(rank, 4)))
        first_step.append(steps_before)
        steps_before = steps_before + lax.div(rank, 4) + 1

    def key_block(buf, step, b):
        return buf[lax.div(step, 2), b % 2, lax.rem(step, 2) * 2 + b // 2]

    def score_all(i):
        row, zq, rank, last = blocks[i]
        pltpu.make_async_copy(q_buf.at[i], q_buf.at[i], q_recv_sem.at[i]).wait()
        query = q_buf[i]

        def score(step, top, masked=False):
            for b in range(KEYS // ROWS):
                s = nt(query, key_block(k_buf, step, b))
                if masked:
                    key_pos = across + step * KEYS + b * ROWS
                    s = jnp.where(key_pos <= down + rank * ROWS, s, NEG)
                scores[step, b] = s
                top = jnp.maximum(top, jnp.maximum(s[:, :128], s[:, 128:]))
            return top

        top = lax.fori_loop(0, last, score, jnp.full((ROWS, 128), NEG, F32))
        top = jnp.max(score(last, top, True), axis=1, keepdims=True)
        totals[i] = jnp.broadcast_to(top, (ROWS, 128))

    def weigh_half(i, r):
        row, zq, rank, last = blocks[i]
        rows = slice(r * 128, (r + 1) * 128)
        top = totals[i, rows]

        def weight(step, total):
            for b in range(KEYS // ROWS):
                for l in range(2):
                    w = jnp.exp2((scores[step, b, rows, l * 128:(l + 1) * 128] - top) * scale)
                    rounded[first_step[i] + step, rows, b * ROWS + l * 128:b * ROWS + (l + 1) * 128] = (
                        w.astype(BF)
                    )
                    total = total + w
            return total

        total = lax.fori_loop(0, last + 1, weight, jnp.zeros((128, 128), F32))
        totals[i, rows] = jnp.broadcast_to(jnp.sum(total, axis=1, keepdims=True), (128, 128))

    def weigh_all(i):
        for r in range(2):
            weigh_half(i, r)

    def values_out(p):
        for h in range(2):
            near_hops[h, p].wait_recv()
        mixed = (
            own_part[3, spans[p]] + near_recv[0, spans[p]].astype(F32) + near_recv[1, spans[p]].astype(F32)
        ).astype(BF)
        mine[spans[p]] = mixed
        values_of.scatter(mine, p, True)
        mixed_ref[spans[p]] = mixed

    values_out(0)
    for row in range(XS):
        keys_of.finish(row, 1)
    score_all(0)
    weigh_all(0)
    values_out(1)
    score_all(1)
    weigh_all(1)
    score_all(2)
    values_of.step_own(0)
    weigh_all(2)
    score_all(3)
    values_of.step_own(1)
    weigh_half(3, 0)
    values_of.step_near(0)
    weigh_half(3, 1)
    values_of.step_near(1)

    def output_copies(i):
        row, zq, rank, last = blocks[i]
        core, j = lax.div(z, 4), lax.rem(z, 4)
        alone = (zq == z) & (core == c) & (row == x)
        local = lambda: pltpu.make_async_copy(o_send.at[i], o_recv.at[j], o_recv_sem.at[j])
        away = lambda: pltpu.make_async_remote_copy(
            src_ref=o_send.at[i], dst_ref=o_recv.at[j],
            send_sem=o_send_sem.at[i], recv_sem=o_recv_sem.at[j],
            device_id={"ctx": row * ZS + zq, "tp": y * 2 + core}, device_id_type=MESH,
        )
        return alone, local, away

    def attend_row(row, i, first=False):
        last = blocks[i][3]

        def value(step, acc):
            part = jnp.concatenate([key_block(v_buf, step, b) for b in range(KEYS // ROWS)], axis=0)
            return acc + nn(rounded[first_step[i] + step], part)

        start = jnp.zeros((ROWS, HS), F32) if first else attended_sum[i]
        attended_sum[i] = lax.fori_loop(2 * row, lax.min(2 * row + 2, last + 1), value, start)

    def output(i):
        o_send[i] = (attended_sum[i] / totals[i]).astype(BF)
        start_either(*output_copies(i))

    def output_low():
        output(0)
        output(1)

    xl, xr, x2 = values_of.xl, values_of.xr, values_of.x2
    values_of.finish(x, PARTS)
    for i in range(4):
        attend_row(x, i, True)
    values_of.step_far(0)
    values_of.step_far(1)
    for row in (xl, xr):
        values_of.finish(row, PARTS)
        for i in range(4):
            attend_row(row, i)
    pl.when(x != 2)(output_low)
    values_of.finish(x2, PARTS)
    for i in (2, 3):
        attend_row(x2, i)
        output(i)
    for i in (0, 1):
        attend_row(x2, i)
    pl.when(x == 2)(output_low)

    some = taps_recv.at[pl.ds(0, CTX - 1)]
    pltpu.make_async_copy(some, some, taps_send_sem.at[0]).wait()
    for h in range(2):
        some = recv.at[h, pl.ds(0, CTX - 1)]
        pltpu.make_async_copy(some, some, send_sem.at[h]).wait()
        some = out_recv.at[h, pl.ds(0, CTX - 1)]
        pltpu.make_async_copy(some, some, back_send_sem.at[h]).wait()
    keys_of.scatter(keys_ref, 0, False)
    keys_of.drain(0)
    for p in range(PARTS):
        values_of.scatter(mine, p, False)
        values_of.drain(p)
        for h in range(2):
            far_hops[h, p].wait_send()
            near_hops[h, p].wait_send()
    for j in range(4):
        alone, local, away = query_copies(j)
        pl.when(jnp.logical_not(alone))(lambda away=away: away().wait_send())
        swaps[j].wait_send()
    for j in range(4):
        pltpu.make_async_copy(o_recv.at[j], o_recv.at[j], o_recv_sem.at[j]).wait()
        attended_ref[:, j * HS:(j + 1) * HS] = o_recv[j]
    for i in range(4):
        alone, local, away = output_copies(i)
        pl.when(jnp.logical_not(alone))(lambda away=away: away().wait_send())


def start_either(alone, local, away):
    pl.when(alone)(lambda: local().start())
    pl.when(jnp.logical_not(alone))(lambda: away().start())


def vmem(count):
    return [pl.BlockSpec(memory_space=pltpu.VMEM)] * count


def hbm(count):
    return [pl.BlockSpec(memory_space=pl.ANY)] * count


def hand_over(a, b, a_out, b_out):
    a_out[...] = a[...]
    b_out[...] = b[...]


def per_device(
    first_input, second_input, value_input, filter_taps, skip_gain, out_weight, queries, keys
):
    consts = [jnp.asarray(t) for t in tables()]
    dma = lambda *shape: pltpu.SemaphoreType.DMA(shape)
    bf = lambda *shape: pltpu.VMEM(shape, BF)
    fl = lambda *shape: pltpu.VMEM(shape, F32)
    sems = lambda p: [dma(p, 4), dma(p), dma(p), dma(p), dma(2, p), dma(XS, p), dma(2, p)]
    out = jax.ShapeDtypeStruct((ROWS, HEAD), BF)
    mixed, attended = pl.pallas_call(
        whole_kernel,
        out_shape=(out, out),
        in_specs=hbm(11),
        out_specs=tuple(vmem(2)),
        scratch_shapes=[
            bf(2, 2, ROWS, 256), bf(2, 2, ROWS, 256), bf(2, 2, ROWS, 256), bf(2, 2, ROWS, 256),
            fl(1, 1024), bf(2 * CTX, 512), bf(512, 256), fl(2 * CTX, ROWS),
            bf(1024, 512), bf(512, 512), bf(512, 512), bf(512, 1024),
            bf(2, 2, ROWS, 256),
            bf(2, 2, 16, GROUP, ROWS), bf(2, CTX, GROUP, ROWS),
            bf(2, 16, 2, GROUP, ROWS), bf(CTX, 2, GROUP, ROWS), fl(2, 512, 512),
            bf(2, CTX, GROUP, ROWS), bf(2, CTX, GROUP, ROWS),
            bf(ROWS, 1024),
            bf(8, 1024, HEAD), fl(8, ROWS, HEAD), fl(4, ROWS, HEAD), bf(4, ROWS, HEAD), bf(4, ROWS, HEAD),
            bf(2, ROWS, 256), bf(2, ROWS, 256), bf(2, ROWS, HEAD), bf(2, ROWS, HEAD), bf(ROWS, HEAD),
            bf(XS, 2, ZS // 2, ROWS, HS), bf(XS, 2, ZS // 2, ROWS, HS), bf(4, ROWS, HS),
            fl(TOTAL // KEYS, KEYS // ROWS, ROWS, ROWS), bf(CHUNKS, ROWS, KEYS), fl(4, ROWS, 128), fl(4, ROWS, HS),
            bf(4, ROWS, HS), bf(4, ROWS, HS),
            dma(4, 4), dma(4), dma(1), dma(1), dma(2), dma(2), dma(2), dma(2),
            dma(8), dma(4), dma(4), dma(2, PARTS), dma(2, PARTS), dma(2, PARTS), dma(2, PARTS),
            dma(4), dma(4), dma(4), dma(4),
        ] + sems(1) + sems(PARTS),
        compiler_params=pltpu.CompilerParams(
            collective_id=0, has_side_effects=True, vmem_limit_bytes=60 * 1024 * 1024
        ),
        name="whole",
    )(first_input, second_input, value_input, filter_taps, skip_gain.reshape(1, 1024), out_weight,
      queries, keys, *consts)
    return pl.pallas_call(
        hand_over,
        out_shape=(out, out),
        in_specs=vmem(2),
        out_specs=tuple(vmem(2)),
        name="hand_over",
    )(mixed, attended)


def solution(mesh):
    return jax.shard_map(
        per_device,
        mesh=mesh,
        in_specs=(
            P("ctx", "tp"),
            P("ctx", "tp"),
            P("ctx", "tp"),
            P("ctx", "tp"),
            P("tp"),
            P("tp", None),
            P("ctx", "tp"),
            P("ctx", "tp"),
        ),
        out_specs=(P("ctx", "tp"), P("ctx", "tp")),
        check_vma=False,
    )
```

```python
import functools
import math

import jax
import jax.numpy as jnp
import numpy as np
from jax import lax
from jax.experimental import pallas as pl
from jax.experimental.pallas import tpu as pltpu
from jax.sharding import PartitionSpec as P

HS = 128
MESH = pl.DeviceIdType.MESH
BF = jnp.bfloat16
F32 = jnp.float32
CTX = 32
ROWS = 256
GROUP = 16
TOTAL = CTX * ROWS


def nt(a, b):
    return lax.dot_general(a, b, (((1,), (1,)), ((), ())), preferred_element_type=F32)


def nn(a, b):
    return jnp.dot(a, b, preferred_element_type=F32)


def tables():
    r = np.arange(CTX, dtype=np.float64)
    q = np.arange(CTX, dtype=np.float64)
    a = np.arange(ROWS, dtype=np.float64)
    rows = np.exp(-2j * np.pi * np.outer(q + 0.25, r) / CTX)
    turn = np.exp(-2j * np.pi * np.outer(q + 0.25, a) / TOTAL)
    cols = np.exp(-2j * np.pi * np.outer(a, a) / ROWS)
    parts = lambda m: np.concatenate([m.real, m.imag], axis=0)
    cast = lambda m: np.asarray(m, np.float32).astype(jnp.bfloat16)
    return (cast(np.repeat(parts(rows), GROUP, axis=1)), cast(parts(cols)),
            np.asarray(parts(turn), np.float32))


def build_tables(rows_ref, cols_ref, eye, spread_t, mix_t, unmix_t, gather_t):
    column = lax.rem(lax.broadcasted_iota(jnp.int32, (CTX, CTX * GROUP), 1), GROUP)
    half = GROUP * CTX
    for part in range(2):
        values = rows_ref[part * CTX:(part + 1) * CTX].astype(F32)
        for c in range(GROUP):
            at = part * half + c * CTX
            spread_t[at:at + CTX] = jnp.where(column == c, values, 0.0).astype(BF)
    for i in range(2):
        for j in range(4):
            a, b = slice(i * 256, (i + 1) * 256), slice(j * 256, (j + 1) * 256)
            gather_t[a, b] = nt(eye, spread_t[b, a]).astype(BF)
    re, im = cols_ref[:ROWS].astype(F32), cols_ref[ROWS:].astype(F32)
    top, low = slice(0, ROWS), slice(ROWS, 2 * ROWS)
    mix_t[top, top] = re.astype(BF)
    mix_t[low, low] = re.astype(BF)
    mix_t[top, low] = im.astype(BF)
    mix_t[low, top] = (-im).astype(BF)
    re, im = re * (1.0 / TOTAL), im * (1.0 / TOTAL)
    unmix_t[top, top] = re.astype(BF)
    unmix_t[low, low] = re.astype(BF)
    unmix_t[top, low] = (-im).astype(BF)
    unmix_t[low, top] = im.astype(BF)


def spectrum(x, first, mix, turn_re, turn_im):
    half = GROUP * CTX
    a = nn(first, x)
    a_re = a[:half].reshape(GROUP, CTX, ROWS)
    a_im = a[half:].reshape(GROUP, CTX, ROWS)
    z_re = (a_re * turn_re - a_im * turn_im).reshape(half, ROWS).astype(BF)
    z_im = (a_re * turn_im + a_im * turn_re).reshape(half, ROWS).astype(BF)
    return nn(jnp.concatenate([z_re, z_im], axis=1), mix)


XS, ZS, YS = 4, 8, 4
HEAD = 512
KEYS = 1024
NEG = -1e30


class Spread:
    def __init__(self, place, buf, parts, z_send, own, left, right, far, sib, sent):
        self.x, self.z, self.y, self.c = place
        self.buf, self.z_send, self.own, self.left, self.right, self.far, self.sib, self.sent = (
            buf, z_send, own, left, right, far, sib, sent
        )
        self.rows = ROWS // parts
        self.xl, self.xr, self.x2 = (lax.rem(self.x + k, XS) for k in (3, 1, 2))

    def device(self, x, z, c):
        return {"ctx": x * ZS + z, "tp": self.y * 2 + c}

    def span(self, p):
        return pl.ds(p * self.rows, self.rows)

    def scatter(self, source, p, start):
        x, z, c = self.x, self.z, self.c
        core = lax.rem(z, 2)
        for j in range(4):
            to = 4 * c + j
            alone = (to == z) & (core == c)
            part = source.at[self.span(p), pl.ds(j * HS, HS)]
            slot = self.buf.at[x, core, lax.div(z, 2), self.span(p)]
            local = lambda: pltpu.make_async_copy(part, slot, self.own.at[p])
            away = lambda: pltpu.make_async_remote_copy(
                src_ref=part, dst_ref=slot, send_sem=self.z_send.at[p, j], recv_sem=self.own.at[p],
                device_id=self.device(x, to, core), device_id_type=MESH,
            )
            if start:
                start_either(alone, local, away)
            else:
                pl.when(jnp.logical_not(alone))(lambda: away().wait_send())

    def push(self, block, p, x, c, sem, late=1):
        pltpu.make_async_remote_copy(
            src_ref=block, dst_ref=block, send_sem=self.sent.at[late, p], recv_sem=sem,
            device_id=self.device(x, self.z, c), device_id_type=MESH,
        ).start()

    def arrived(self, block, sem):
        pltpu.make_async_copy(block, block, sem).wait()

    def step_own(self, p):
        block = self.buf.at[self.x, self.c, :, self.span(p)]
        self.arrived(block, self.own.at[p])
        self.push(block, p, self.xr, self.c, self.left.at[p], 0)
        self.push(block, p, self.xl, self.c, self.right.at[p], 0)
        self.push(block, p, self.x, 1 - self.c, self.sib.at[self.x, p], 0)

    def half(self, x, p, h):
        return self.buf.at[x, self.c, :, pl.ds(p * self.rows + h * (self.rows // 2), self.rows // 2)]

    def step_near(self, p):
        for h, x, on, sem in ((0, self.xl, self.xr, self.left), (1, self.xr, self.xl, self.right)):
            block = self.buf.at[x, self.c, :, self.span(p)]
            self.arrived(block, sem.at[p])
            self.push(self.half(x, p, h), p, on, self.c, self.far.at[h, p])
            self.push(block, p, self.x, 1 - self.c, self.sib.at[x, p])

    def step_far(self, p):
        for h in range(2):
            half = self.half(self.x2, p, h)
            self.arrived(half, self.far.at[h, p])
            self.push(half, p, self.x, 1 - self.c, self.sib.at[self.x2, p])

    def finish(self, x, parts):
        for p in range(parts):
            self.arrived(self.buf.at[x, 1 - self.c, :, self.span(p)], self.sib.at[x, p])

    def drain(self, p):
        self.arrived(self.buf.at[pl.ds(0, 3), 0, :, self.span(p)], self.sent.at[0, p])
        self.arrived(self.buf.at[:, 0, :, self.span(p)], self.sent.at[1, p])


PARTS = 2
CHUNKS = 20


def whole_kernel(
    first_hbm, second_hbm, value_hbm, taps_hbm, skip_hbm, weight_ref, queries_ref, keys_ref,
    rows_hbm, cols_hbm, turn_hbm, mixed_ref, attended_ref,
    first_in, value_in, taps_in, second_in, skip, rows_in, cols_in, turn, spread_t, mix_t, unmix_t, gather_t,
    product, send, recv, taps_send, taps_recv, taps_spectrum, out_send, out_recv, gated_ref,
    weights, partial, own_part, sib_send, sib_recv, y_send, y_recv, near_send, near_recv, mine,
    k_buf, v_buf, q_buf, scores, rounded, totals, attended_sum, o_send, o_recv,
    in_sem, table_sem, taps_send_sem, taps_recv_sem, send_sem, recv_sem, back_send_sem, back_recv_sem,
    w_sem, sib_send_sem, sib_recv_sem, y_send_sem, y_recv_sem, near_send_sem, near_recv_sem,
    q_send_sem, q_recv_sem, o_send_sem, o_recv_sem,
    kz, k_own, k_left, k_right, k_far, k_sib, k_sent,
    vz, v_own, v_left, v_right, v_far, v_sib, v_sent,
):
    me, tp = lax.axis_index("ctx"), lax.axis_index("tp")
    x, z = lax.div(me, ZS), lax.rem(me, ZS)
    y, c = lax.div(tp, 2), lax.rem(tp, 2)
    place = (x, z, y, c)
    keys_of = Spread(place, k_buf, 1, kz, k_own, k_left, k_right, k_far, k_sib, k_sent)
    values_of = Spread(place, v_buf, PARTS, vz, v_own, v_left, v_right, v_far, v_sib, v_sent)
    mirror = XS - 1 - x
    half = GROUP * CTX

    base = [lax.rem(lax.div(me, 16) + g, 2) * 16 for g in range(2)]
    cols_of = [
        [pl.ds(pl.multiple_of(h * 512 + base[g] * GROUP, 256), 256) for g in range(2)] for h in range(2)
    ]
    inputs = {}

    def fetch(k, hbm, into, h, g):
        inputs[k, h, g] = pltpu.make_async_copy(
            hbm.at[:, cols_of[h][g]], into.at[h, g], in_sem.at[k, 2 * h + g]
        )
        inputs[k, h, g].start()

    for g in range(2):
        for h in range(2):
            fetch(0, taps_hbm, taps_in, h, g)
    for h in range(2):
        for g in range(2):
            fetch(1, first_hbm, first_in, h, g)
            fetch(2, value_hbm, value_in, h, g)

    barrier = pltpu.get_barrier_semaphore()

    def greet(to_ctx, to_tp):
        pl.semaphore_signal(
            barrier, inc=1, device_id={"ctx": to_ctx, "tp": to_tp}, device_id_type=MESH
        )

    def greet_group(k, carry):
        greet(lax.rem(me + k, CTX), tp)
        return carry

    def greet_rows(k, carry):
        greet(x * ZS + k, y * 2 + 1 - c)
        greet(mirror * ZS + k, y * 2 + 1 - c)
        return carry

    lax.fori_loop(1, CTX, greet_group, 0)
    lax.fori_loop(0, ZS, greet_rows, 0)
    for k in (1, 3):
        greet(me, lax.rem(y + k, YS) * 2 + c)

    tables_in = []
    for k, (hbm, into) in enumerate((
        (rows_hbm, rows_in), (cols_hbm, cols_in), (turn_hbm, turn), (skip_hbm, skip),
    )):
        tables_in.append(pltpu.make_async_copy(hbm, into, table_sem.at[k]))
        tables_in[-1].start()
    def post_line(source, into, send_sems, recv_sems, g):
        def one(k, carry):
            o = lax.rem(me + k, 16)
            pltpu.make_async_remote_copy(
                src_ref=source.at[g, o], dst_ref=into.at[me], send_sem=send_sems, recv_sem=recv_sems,
                device_id={"ctx": base[g] + o}, device_id_type=MESH,
            ).start()
            return carry

        if g == 0:
            pltpu.make_async_copy(source.at[0, lax.rem(me, 16)], into.at[me], recv_sems).start()
        lax.fori_loop(1 if g == 0 else 0, 16, one, 0)

    down = lax.broadcasted_iota(jnp.int32, (ROWS, ROWS), 0)
    across = lax.broadcasted_iota(jnp.int32, (ROWS, ROWS), 1)
    eye = jnp.where(down == across, 1.0, 0.0).astype(BF)
    for g in range(2):
        for h in range(2):
            inputs[0, h, g].wait()
            taps_send[g, :, h] = nt(eye, taps_in[h, g]).astype(BF).reshape(16, GROUP, ROWS)
        if g == 0:
            pl.semaphore_wait(barrier, CTX - 1 + 2 * ZS + 2)
        post_line(taps_send, taps_recv, taps_send_sem.at[0], taps_recv_sem.at[0], g)
    for h in range(2):
        for g in range(2):
            inputs[1, h, g].wait()
            inputs[2, h, g].wait()
            block = (first_in[h, g].astype(F32) * value_in[h, g].astype(F32)).astype(BF)
            product[h, g] = block
            send[h, g] = nt(eye, block).astype(BF).reshape(16, GROUP, ROWS)
            post_line(send.at[h], recv.at[h], send_sem.at[h], recv_sem.at[h], g)

    gates_in = []
    for h in range(2):
        for g in range(2):
            gates_in.append(pltpu.make_async_copy(
                second_hbm.at[:, cols_of[h][g]], second_in.at[h, g], in_sem.at[3, 2 * h + g]
            ))
            gates_in[-1].start()

    order = [(other, lax.rem(y + k, YS)) for other in (1, 0) for k in (2, 1, 3, 0)]
    loads = []
    for k, (other, to_y) in enumerate(order):
        col = to_y * 2 + (1 - c if other else c)
        loads.append(pltpu.make_async_copy(
            weight_ref.at[:, pl.ds(pl.multiple_of(col * HEAD, HEAD), HEAD)], weights.at[k], w_sem.at[k]
        ))
        loads[-1].start()
    for copy in tables_in:
        copy.wait()
    build_tables(rows_in, cols_in, eye, spread_t, mix_t, unmix_t, gather_t)
    pltpu.make_async_copy(taps_recv, taps_recv, taps_recv_sem.at[0]).wait()
    for h in range(2):
        taps_spectrum[h] = spectrum(
            taps_recv[:, h].reshape(half, ROWS), spread_t[...], mix_t[...], turn[:CTX], turn[CTX:]
        )

    for h in range(2):
        tr, ti = turn[:CTX], turn[CTX:]
        pltpu.make_async_copy(recv.at[h], recv.at[h], recv_sem.at[h]).wait()
        if h == 1:
            keys_of.scatter(keys_ref, 0, True)
        d = spectrum(recv[h].reshape(half, ROWS), spread_t[...], mix_t[...], tr, ti)
        e = taps_spectrum[h]
        d_re, d_im, e_re, e_im = d[:, :ROWS], d[:, ROWS:], e[:, :ROWS], e[:, ROWS:]
        y_re = (d_re * e_re - d_im * e_im).astype(BF)
        y_im = (d_re * e_im + d_im * e_re).astype(BF)
        b = nn(jnp.concatenate([y_re, y_im], axis=1), unmix_t[...])
        b_re = b[:, :ROWS].reshape(GROUP, CTX, ROWS)
        b_im = b[:, ROWS:].reshape(GROUP, CTX, ROWS)
        c_re = (b_re * tr + b_im * ti).reshape(half, ROWS).astype(BF)
        c_im = (b_im * tr - b_re * ti).reshape(half, ROWS).astype(BF)
        points = jnp.concatenate([c_re, c_im], axis=0)
        for g in range(2):
            rows = pl.ds(pl.multiple_of(base[g] * GROUP, 256), 256)
            out_send[h, pl.ds(base[g], 16)] = (
                nn(gather_t[rows], points).astype(BF).reshape(16, GROUP, ROWS)
            )

            def reply(k, carry, h=h, g=g):
                to = base[g] + lax.rem(me + k, 16)
                pltpu.make_async_remote_copy(
                    src_ref=out_send.at[h, to], dst_ref=out_recv.at[h, me],
                    send_sem=back_send_sem.at[h], recv_sem=back_recv_sem.at[h],
                    device_id={"ctx": to}, device_id_type=MESH,
                ).start()
                return carry

            if g == 0:
                pltpu.make_async_copy(
                    out_send.at[h, me], out_recv.at[h, me], back_recv_sem.at[h]
                ).start()
            lax.fori_loop(1 if g == 0 else 0, 16, reply, 0)

    for copy in gates_in:
        copy.wait()

    def gate(h):
        pltpu.make_async_copy(out_recv.at[h], out_recv.at[h], back_recv_sem.at[h]).wait()
        for g in range(2):
            block = out_recv[h, pl.ds(base[g], 16)].reshape(ROWS, ROWS)
            filtered = nt(eye, block).astype(BF).astype(F32)
            gated_ref[:, cols_of[h][g]] = (
                second_in[h, g].astype(F32)
                * (filtered + skip[:, cols_of[h][g]] * product[h, g].astype(F32))
            ).astype(BF)

    gate(0)
    low = gated_ref[:, :512]
    for k in range(8):
        loads[k].wait()
        partial[k] = nn(low, weights[k, :512])
    keys_of.step_own(0)
    gate(1)
    high = gated_ref[:, 512:]

    def projected(k):
        return partial[k] + nn(high, weights[k, 512:])

    far_pair = lax.min(z, ZS - 1 - z)
    q_x = lax.select(far_pair < 2, x, mirror)
    q_core = lax.rem(far_pair, 2)
    q_slot = lax.div(x, 2) * 2 + lax.div(z, 4)

    def query_copies(j):
        to = 4 * c + j
        alone = (to == z) & (q_core == c) & (far_pair < 2)
        part = queries_ref.at[:, pl.ds(j * HS, HS)]
        slot = q_buf.at[q_slot]
        sem = q_recv_sem.at[q_slot]
        local = lambda: pltpu.make_async_copy(part, slot, sem)
        away = lambda: pltpu.make_async_remote_copy(
            src_ref=part, dst_ref=slot, send_sem=q_send_sem.at[j], recv_sem=sem,
            device_id={"ctx": q_x * ZS + to, "tp": y * 2 + q_core}, device_id_type=MESH,
        )
        return alone, local, away

    for j in range(4):
        start_either(*query_copies(j))

    swaps = []

    def swap(k):
        sib_send[k] = projected(k).astype(BF)
        swaps.append(pltpu.make_async_remote_copy(
            src_ref=sib_send.at[k], dst_ref=sib_recv.at[k],
            send_sem=sib_send_sem.at[k], recv_sem=sib_recv_sem.at[k],
            device_id={"tp": y * 2 + 1 - c}, device_id_type=MESH,
        ))
        swaps[-1].start()

    swap(0)

    def chip_sum(k):
        own = projected(4 + k)
        swaps[k].wait_recv()
        return own + sib_recv[k].astype(F32)

    right, left = lax.rem(y + 1, YS) * 2 + c, lax.rem(y + 3, YS) * 2 + c
    depth = ROWS // PARTS
    spans = [pl.ds(p * depth, depth) for p in range(PARTS)]

    def hop(source, into, send_sems, recv_sems, h, p):
        return pltpu.make_async_remote_copy(
            src_ref=source.at[h, spans[p]], dst_ref=into.at[h, spans[p]],
            send_sem=send_sems.at[h, p], recv_sem=recv_sems.at[h, p],
            device_id={"tp": (right, left)[h]}, device_id_type=MESH,
        )

    far = chip_sum(0).astype(BF)
    far_hops, near_hops = {}, {}
    for h in range(2):
        y_send[h] = far[:, h * 256:(h + 1) * 256]
    for p in range(PARTS):
        for h in range(2):
            far_hops[h, p] = hop(y_send, y_recv, y_send_sem, y_recv_sem, h, p)
            far_hops[h, p].start()
    for k in range(1, 4):
        swap(k)
    for k in range(1, 4):
        own_part[k] = chip_sum(k)
    keys_of.step_near(0)
    for p in range(PARTS):
        for h in range(2):
            far_hops[h, p].wait_recv()
            own_part[1 + h, spans[p], pl.ds(h * 256, 256)] += y_recv[h, spans[p]].astype(F32)
            near_send[h, spans[p]] = own_part[1 + h, spans[p]].astype(BF)
            near_hops[h, p] = hop(near_send, near_recv, near_send_sem, near_recv_sem, h, p)
            near_hops[h, p].start()
    keys_of.step_far(0)

    scale = 1.0 / math.sqrt(HS) * math.log2(math.e)
    blocks, first_step = [], []
    steps_before = 0
    for i in range(4):
        row = lax.min(x, mirror) if i < 2 else lax.max(x, mirror)
        pair = lax.select(row == x, c, c + 2)
        zq = pair if i % 2 == 0 else ZS - 1 - pair
        rank = row * ZS + zq
        blocks.append((row, zq, rank, lax.div(rank, 4)))
        first_step.append(steps_before)
        steps_before = steps_before + lax.div(rank, 4) + 1

    def key_block(buf, step, b):
        return buf[lax.div(step, 2), b % 2, lax.rem(step, 2) * 2 + b // 2]

    def score_all(i):
        row, zq, rank, last = blocks[i]
        pltpu.make_async_copy(q_buf.at[i], q_buf.at[i], q_recv_sem.at[i]).wait()
        query = q_buf[i]

        def score(step, top, masked=False):
            for b in range(KEYS // ROWS):
                s = nt(query, key_block(k_buf, step, b))
                if masked:
                    key_pos = across + step * KEYS + b * ROWS
                    s = jnp.where(key_pos <= down + rank * ROWS, s, NEG)
                scores[step, b] = s
                top = jnp.maximum(top, jnp.maximum(s[:, :128], s[:, 128:]))
            return top

        top = lax.fori_loop(0, last, score, jnp.full((ROWS, 128), NEG, F32))
        top = jnp.max(score(last, top, True), axis=1, keepdims=True)
        totals[i] = jnp.broadcast_to(top, (ROWS, 128))

    def weigh_half(i, r):
        row, zq, rank, last = blocks[i]
        rows = slice(r * 128, (r + 1) * 128)
        top = totals[i, rows]

        def weight(step, total):
            for b in range(KEYS // ROWS):
                for l in range(2):
                    w = jnp.exp2((scores[step, b, rows, l * 128:(l + 1) * 128] - top) * scale)
                    rounded[first_step[i] + step, rows, b * ROWS + l * 128:b * ROWS + (l + 1) * 128] = (
                        w.astype(BF)
                    )
                    total = total + w
            return total

        total = lax.fori_loop(0, last + 1, weight, jnp.zeros((128, 128), F32))
        totals[i, rows] = jnp.broadcast_to(jnp.sum(total, axis=1, keepdims=True), (128, 128))

    def weigh_all(i):
        for r in range(2):
            weigh_half(i, r)

    def values_out(p):
        for h in range(2):
            near_hops[h, p].wait_recv()
        mixed = (
            own_part[3, spans[p]] + near_recv[0, spans[p]].astype(F32) + near_recv[1, spans[p]].astype(F32)
        ).astype(BF)
        mine[spans[p]] = mixed
        values_of.scatter(mine, p, True)
        mixed_ref[spans[p]] = mixed

    values_out(0)
    for row in range(XS):
        keys_of.finish(row, 1)
    score_all(0)
    weigh_all(0)
    values_out(1)
    score_all(1)
    weigh_all(1)
    score_all(2)
    values_of.step_own(0)
    weigh_all(2)
    score_all(3)
    values_of.step_own(1)
    weigh_half(3, 0)
    values_of.step_near(0)
    weigh_half(3, 1)
    values_of.step_near(1)

    def output_copies(i):
        row, zq, rank, last = blocks[i]
        core, j = lax.div(z, 4), lax.rem(z, 4)
        alone = (zq == z) & (core == c) & (row == x)
        local = lambda: pltpu.make_async_copy(o_send.at[i], o_recv.at[j], o_recv_sem.at[j])
        away = lambda: pltpu.make_async_remote_copy(
            src_ref=o_send.at[i], dst_ref=o_recv.at[j],
            send_sem=o_send_sem.at[i], recv_sem=o_recv_sem.at[j],
            device_id={"ctx": row * ZS + zq, "tp": y * 2 + core}, device_id_type=MESH,
        )
        return alone, local, away

    def attend_row(row, i, first=False):
        last = blocks[i][3]

        def value(step, acc):
            part = jnp.concatenate([key_block(v_buf, step, b) for b in range(KEYS // ROWS)], axis=0)
            return acc + nn(rounded[first_step[i] + step], part)

        start = jnp.zeros((ROWS, HS), F32) if first else attended_sum[i]
        attended_sum[i] = lax.fori_loop(2 * row, lax.min(2 * row + 2, last + 1), value, start)

    def output(i):
        o_send[i] = (attended_sum[i] / totals[i]).astype(BF)
        start_either(*output_copies(i))

    def output_low():
        output(0)
        output(1)

    xl, xr, x2 = values_of.xl, values_of.xr, values_of.x2
    values_of.finish(x, PARTS)
    for i in range(4):
        attend_row(x, i, True)
    values_of.step_far(0)
    values_of.step_far(1)
    for row in (xl, xr):
        values_of.finish(row, PARTS)
        for i in range(4):
            attend_row(row, i)
    pl.when(x != 2)(output_low)
    values_of.finish(x2, PARTS)
    for i in (2, 3):
        attend_row(x2, i)
        output(i)
    for i in (0, 1):
        attend_row(x2, i)
    pl.when(x == 2)(output_low)

    some = taps_recv.at[pl.ds(0, CTX - 1)]
    pltpu.make_async_copy(some, some, taps_send_sem.at[0]).wait()
    for h in range(2):
        some = recv.at[h, pl.ds(0, CTX - 1)]
        pltpu.make_async_copy(some, some, send_sem.at[h]).wait()
        some = out_recv.at[h, pl.ds(0, CTX - 1)]
        pltpu.make_async_copy(some, some, back_send_sem.at[h]).wait()
    keys_of.scatter(keys_ref, 0, False)
    keys_of.drain(0)
    for p in range(PARTS):
        values_of.scatter(mine, p, False)
        values_of.drain(p)
        for h in range(2):
            far_hops[h, p].wait_send()
            near_hops[h, p].wait_send()
    for j in range(4):
        alone, local, away = query_copies(j)
        pl.when(jnp.logical_not(alone))(lambda away=away: away().wait_send())
        swaps[j].wait_send()
    for j in range(4):
        pltpu.make_async_copy(o_recv.at[j], o_recv.at[j], o_recv_sem.at[j]).wait()
        attended_ref[:, j * HS:(j + 1) * HS] = o_recv[j]
    for i in range(4):
        alone, local, away = output_copies(i)
        pl.when(jnp.logical_not(alone))(lambda away=away: away().wait_send())


def start_either(alone, local, away):
    pl.when(alone)(lambda: local().start())
    pl.when(jnp.logical_not(alone))(lambda: away().start())


def vmem(count):
    return [pl.BlockSpec(memory_space=pltpu.VMEM)] * count


def hbm(count):
    return [pl.BlockSpec(memory_space=pl.ANY)] * count


def hand_over(a, b, a_out, b_out):
    a_out[...] = a[...]
    b_out[...] = b[...]


def per_device(
    first_input, second_input, value_input, filter_taps, skip_gain, out_weight, queries, keys
):
    consts = [jnp.asarray(t) for t in tables()]
    dma = lambda *shape: pltpu.SemaphoreType.DMA(shape)
    bf = lambda *shape: pltpu.VMEM(shape, BF)
    fl = lambda *shape: pltpu.VMEM(shape, F32)
    sems = lambda p: [dma(p, 4), dma(p), dma(p), dma(p), dma(2, p), dma(XS, p), dma(2, p)]
    out = jax.ShapeDtypeStruct((ROWS, HEAD), BF)
    mixed, attended = pl.pallas_call(
        whole_kernel,
        out_shape=(out, out),
        in_specs=hbm(11),
        out_specs=tuple(vmem(2)),
        scratch_shapes=[
            bf(2, 2, ROWS, 256), bf(2, 2, ROWS, 256), bf(2, 2, ROWS, 256), bf(2, 2, ROWS, 256),
            fl(1, 1024), bf(2 * CTX, 512), bf(512, 256), fl(2 * CTX, ROWS),
            bf(1024, 512), bf(512, 512), bf(512, 512), bf(512, 1024),
            bf(2, 2, ROWS, 256),
            bf(2, 2, 16, GROUP, ROWS), bf(2, CTX, GROUP, ROWS),
            bf(2, 16, 2, GROUP, ROWS), bf(CTX, 2, GROUP, ROWS), fl(2, 512, 512),
            bf(2, CTX, GROUP, ROWS), bf(2, CTX, GROUP, ROWS),
            bf(ROWS, 1024),
            bf(8, 1024, HEAD), fl(8, ROWS, HEAD), fl(4, ROWS, HEAD), bf(4, ROWS, HEAD), bf(4, ROWS, HEAD),
            bf(2, ROWS, 256), bf(2, ROWS, 256), bf(2, ROWS, HEAD), bf(2, ROWS, HEAD), bf(ROWS, HEAD),
            bf(XS, 2, ZS // 2, ROWS, HS), bf(XS, 2, ZS // 2, ROWS, HS), bf(4, ROWS, HS),
            fl(TOTAL // KEYS, KEYS // ROWS, ROWS, ROWS), bf(CHUNKS, ROWS, KEYS), fl(4, ROWS, 128), fl(4, ROWS, HS),
            bf(4, ROWS, HS), bf(4, ROWS, HS),
            dma(4, 4), dma(4), dma(1), dma(1), dma(2), dma(2), dma(2), dma(2),
            dma(8), dma(4), dma(4), dma(2, PARTS), dma(2, PARTS), dma(2, PARTS), dma(2, PARTS),
            dma(4), dma(4), dma(4), dma(4),
        ] + sems(1) + sems(PARTS),
        compiler_params=pltpu.CompilerParams(
            collective_id=0, has_side_effects=True, vmem_limit_bytes=60 * 1024 * 1024
        ),
        name="whole",
    )(first_input, second_input, value_input, filter_taps, skip_gain.reshape(1, 1024), out_weight,
      queries, keys, *consts)
    return pl.pallas_call(
        hand_over,
        out_shape=(out, out),
        in_specs=vmem(2),
        out_specs=tuple(vmem(2)),
        name="hand_over",
    )(mixed, attended)


def solution(mesh):
    return jax.shard_map(
        per_device,
        mesh=mesh,
        in_specs=(
            P("ctx", "tp"),
            P("ctx", "tp"),
            P("ctx", "tp"),
            P("ctx", "tp"),
            P("tp"),
            P("tp", None),
            P("ctx", "tp"),
            P("ctx", "tp"),
        ),
        out_specs=(P("ctx", "tp"), P("ctx", "tp")),
        check_vma=False,
    )
```

```python
import functools
import math

import jax
import jax.numpy as jnp
import numpy as np
from jax import lax
from jax.experimental import pallas as pl
from jax.experimental.pallas import tpu as pltpu
from jax.sharding import PartitionSpec as P

HS = 128
MESH = pl.DeviceIdType.MESH
BF = jnp.bfloat16
F32 = jnp.float32
CTX = 32
ROWS = 256
GROUP = 16
TOTAL = CTX * ROWS


def nt(a, b):
    return lax.dot_general(a, b, (((1,), (1,)), ((), ())), preferred_element_type=F32)


def nn(a, b):
    return jnp.dot(a, b, preferred_element_type=F32)


def tables():
    r = np.arange(CTX, dtype=np.float64)
    q = np.arange(CTX, dtype=np.float64)
    a = np.arange(ROWS, dtype=np.float64)
    rows = np.exp(-2j * np.pi * np.outer(q + 0.25, r) / CTX)
    turn = np.exp(-2j * np.pi * np.outer(q + 0.25, a) / TOTAL)
    cols = np.exp(-2j * np.pi * np.outer(a, a) / ROWS)
    parts = lambda m: np.concatenate([m.real, m.imag], axis=0)
    cast = lambda m: np.asarray(m, np.float32).astype(jnp.bfloat16)
    return (cast(np.repeat(parts(rows), GROUP, axis=1)), cast(parts(cols)),
            np.asarray(parts(turn), np.float32))


def build_tables(rows_ref, cols_ref, eye, spread_t, mix_t, unmix_t, gather_t):
    column = lax.rem(lax.broadcasted_iota(jnp.int32, (CTX, CTX * GROUP), 1), GROUP)
    half = GROUP * CTX
    for part in range(2):
        values = rows_ref[part * CTX:(part + 1) * CTX].astype(F32)
        for c in range(GROUP):
            at = part * half + c * CTX
            spread_t[at:at + CTX] = jnp.where(column == c, values, 0.0).astype(BF)
    for i in range(2):
        for j in range(4):
            a, b = slice(i * 256, (i + 1) * 256), slice(j * 256, (j + 1) * 256)
            gather_t[a, b] = nt(eye, spread_t[b, a]).astype(BF)
    re, im = cols_ref[:ROWS].astype(F32), cols_ref[ROWS:].astype(F32)
    top, low = slice(0, ROWS), slice(ROWS, 2 * ROWS)
    mix_t[top, top] = re.astype(BF)
    mix_t[low, low] = re.astype(BF)
    mix_t[top, low] = im.astype(BF)
    mix_t[low, top] = (-im).astype(BF)
    re, im = re * (1.0 / TOTAL), im * (1.0 / TOTAL)
    unmix_t[top, top] = re.astype(BF)
    unmix_t[low, low] = re.astype(BF)
    unmix_t[top, low] = (-im).astype(BF)
    unmix_t[low, top] = im.astype(BF)


def spectrum(x, first, mix, turn_re, turn_im):
    half = GROUP * CTX
    a = nn(first, x)
    a_re = a[:half].reshape(GROUP, CTX, ROWS)
    a_im = a[half:].reshape(GROUP, CTX, ROWS)
    z_re = (a_re * turn_re - a_im * turn_im).reshape(half, ROWS).astype(BF)
    z_im = (a_re * turn_im + a_im * turn_re).reshape(half, ROWS).astype(BF)
    return nn(jnp.concatenate([z_re, z_im], axis=1), mix)


XS, ZS, YS = 4, 8, 4
HEAD = 512
KEYS = 1024
NEG = -1e30


class Spread:
    def __init__(self, place, buf, parts, z_send, own, left, right, far, sib, sent):
        self.x, self.z, self.y, self.c = place
        self.buf, self.z_send, self.own, self.left, self.right, self.far, self.sib, self.sent = (
            buf, z_send, own, left, right, far, sib, sent
        )
        self.rows = ROWS // parts
        self.xl, self.xr, self.x2 = (lax.rem(self.x + k, XS) for k in (3, 1, 2))

    def device(self, x, z, c):
        return {"ctx": x * ZS + z, "tp": self.y * 2 + c}

    def span(self, p):
        return pl.ds(p * self.rows, self.rows)

    def scatter(self, source, p, start):
        x, z, c = self.x, self.z, self.c
        core = lax.rem(z, 2)
        for j in range(4):
            to = 4 * c + j
            alone = (to == z) & (core == c)
            part = source.at[self.span(p), pl.ds(j * HS, HS)]
            slot = self.buf.at[x, core, lax.div(z, 2), self.span(p)]
            local = lambda: pltpu.make_async_copy(part, slot, self.own.at[p])
            away = lambda: pltpu.make_async_remote_copy(
                src_ref=part, dst_ref=slot, send_sem=self.z_send.at[p, j], recv_sem=self.own.at[p],
                device_id=self.device(x, to, core), device_id_type=MESH,
            )
            if start:
                start_either(alone, local, away)
            else:
                pl.when(jnp.logical_not(alone))(lambda: away().wait_send())

    def push(self, block, p, x, c, sem, late=1):
        pltpu.make_async_remote_copy(
            src_ref=block, dst_ref=block, send_sem=self.sent.at[late, p], recv_sem=sem,
            device_id=self.device(x, self.z, c), device_id_type=MESH,
        ).start()

    def arrived(self, block, sem):
        pltpu.make_async_copy(block, block, sem).wait()

    def step_own(self, p):
        block = self.buf.at[self.x, self.c, :, self.span(p)]
        self.arrived(block, self.own.at[p])
        self.push(block, p, self.xr, self.c, self.left.at[p], 0)
        self.push(block, p, self.xl, self.c, self.right.at[p], 0)
        self.push(block, p, self.x, 1 - self.c, self.sib.at[self.x, p], 0)

    def half(self, x, p, h):
        return self.buf.at[x, self.c, :, pl.ds(p * self.rows + h * (self.rows // 2), self.rows // 2)]

    def step_near(self, p):
        for h, x, on, sem in ((0, self.xl, self.xr, self.left), (1, self.xr, self.xl, self.right)):
            block = self.buf.at[x, self.c, :, self.span(p)]
            self.arrived(block, sem.at[p])
            self.push(self.half(x, p, h), p, on, self.c, self.far.at[h, p])
            self.push(block, p, self.x, 1 - self.c, self.sib.at[x, p])

    def step_far(self, p):
        for h in range(2):
            half = self.half(self.x2, p, h)
            self.arrived(half, self.far.at[h, p])
            self.push(half, p, self.x, 1 - self.c, self.sib.at[self.x2, p])

    def finish(self, x, parts):
        for p in range(parts):
            self.arrived(self.buf.at[x, 1 - self.c, :, self.span(p)], self.sib.at[x, p])

    def drain(self, p):
        self.arrived(self.buf.at[pl.ds(0, 3), 0, :, self.span(p)], self.sent.at[0, p])
        self.arrived(self.buf.at[:, 0, :, self.span(p)], self.sent.at[1, p])


PARTS = 2
CHUNKS = 20


def whole_kernel(
    first_hbm, second_hbm, value_hbm, taps_hbm, skip_hbm, weight_ref, queries_ref, keys_ref,
    rows_hbm, cols_hbm, turn_hbm, mixed_ref, attended_ref,
    first_in, value_in, taps_in, second_in, skip, rows_in, cols_in, turn, spread_t, mix_t, unmix_t, gather_t,
    product, send, recv, taps_send, taps_recv, taps_spectrum, out_send, out_recv, gated_ref,
    weights, partial, own_part, sib_send, sib_recv, y_send, y_recv, near_send, near_recv, mine,
    k_buf, v_buf, q_buf, scores, rounded, totals, attended_sum, o_send, o_recv,
    in_sem, table_sem, taps_send_sem, taps_recv_sem, send_sem, recv_sem, back_send_sem, back_recv_sem,
    w_sem, sib_send_sem, sib_recv_sem, y_send_sem, y_recv_sem, near_send_sem, near_recv_sem,
    q_send_sem, q_recv_sem, o_send_sem, o_recv_sem,
    kz, k_own, k_left, k_right, k_far, k_sib, k_sent,
    vz, v_own, v_left, v_right, v_far, v_sib, v_sent,
):
    me, tp = lax.axis_index("ctx"), lax.axis_index("tp")
    x, z = lax.div(me, ZS), lax.rem(me, ZS)
    y, c = lax.div(tp, 2), lax.rem(tp, 2)
    place = (x, z, y, c)
    keys_of = Spread(place, k_buf, 1, kz, k_own, k_left, k_right, k_far, k_sib, k_sent)
    values_of = Spread(place, v_buf, PARTS, vz, v_own, v_left, v_right, v_far, v_sib, v_sent)
    mirror = XS - 1 - x
    half = GROUP * CTX

    base = [lax.rem(lax.div(me, 16) + g, 2) * 16 for g in range(2)]
    cols_of = [
        [pl.ds(pl.multiple_of(h * 512 + base[g] * GROUP, 256), 256) for g in range(2)] for h in range(2)
    ]
    inputs = {}

    def fetch(k, hbm, into, h, g):
        inputs[k, h, g] = pltpu.make_async_copy(
            hbm.at[:, cols_of[h][g]], into.at[h, g], in_sem.at[k, 2 * h + g]
        )
        inputs[k, h, g].start()

    for g in range(2):
        for h in range(2):
            fetch(0, taps_hbm, taps_in, h, g)
    for h in range(2):
        for g in range(2):
            fetch(1, first_hbm, first_in, h, g)
            fetch(2, value_hbm, value_in, h, g)

    barrier = pltpu.get_barrier_semaphore()

    def greet(to_ctx, to_tp):
        pl.semaphore_signal(
            barrier, inc=1, device_id={"ctx": to_ctx, "tp": to_tp}, device_id_type=MESH
        )

    def greet_group(k, carry):
        greet(lax.rem(me + k, CTX), tp)
        return carry

    def greet_rows(k, carry):
        greet(x * ZS + k, y * 2 + 1 - c)
        greet(mirror * ZS + k, y * 2 + 1 - c)
        return carry

    lax.fori_loop(1, CTX, greet_group, 0)
    lax.fori_loop(0, ZS, greet_rows, 0)
    for k in (1, 3):
        greet(me, lax.rem(y + k, YS) * 2 + c)

    tables_in = []
    for k, (hbm, into) in enumerate((
        (rows_hbm, rows_in), (cols_hbm, cols_in), (turn_hbm, turn), (skip_hbm, skip),
    )):
        tables_in.append(pltpu.make_async_copy(hbm, into, table_sem.at[k]))
        tables_in[-1].start()
    def post_line(source, into, send_sems, recv_sems, g):
        def one(k, carry):
            o = lax.rem(me + k, 16)
            pltpu.make_async_remote_copy(
                src_ref=source.at[g, o], dst_ref=into.at[me], send_sem=send_sems, recv_sem=recv_sems,
                device_id={"ctx": base[g] + o}, device_id_type=MESH,
            ).start()
            return carry

        if g == 0:
            pltpu.make_async_copy(source.at[0, lax.rem(me, 16)], into.at[me], recv_sems).start()
        lax.fori_loop(1 if g == 0 else 0, 16, one, 0)

    down = lax.broadcasted_iota(jnp.int32, (ROWS, ROWS), 0)
    across = lax.broadcasted_iota(jnp.int32, (ROWS, ROWS), 1)
    eye = jnp.where(down == across, 1.0, 0.0).astype(BF)
    for g in range(2):
        for h in range(2):
            inputs[0, h, g].wait()
            taps_send[g, :, h] = nt(eye, taps_in[h, g]).astype(BF).reshape(16, GROUP, ROWS)
        if g == 0:
            pl.semaphore_wait(barrier, CTX - 1 + 2 * ZS + 2)
        post_line(taps_send, taps_recv, taps_send_sem.at[0], taps_recv_sem.at[0], g)
    for h in range(2):
        for g in range(2):
            inputs[1, h, g].wait()
            inputs[2, h, g].wait()
            block = (first_in[h, g].astype(F32) * value_in[h, g].astype(F32)).astype(BF)
            product[h, g] = block
            send[h, g] = nt(eye, block).astype(BF).reshape(16, GROUP, ROWS)
            post_line(send.at[h], recv.at[h], send_sem.at[h], recv_sem.at[h], g)

    gates_in = []
    for h in range(2):
        for g in range(2):
            gates_in.append(pltpu.make_async_copy(
                second_hbm.at[:, cols_of[h][g]], second_in.at[h, g], in_sem.at[3, 2 * h + g]
            ))
            gates_in[-1].start()

    order = [(other, lax.rem(y + k, YS)) for other in (1, 0) for k in (2, 1, 3, 0)]
    loads = []
    for k, (other, to_y) in enumerate(order):
        col = to_y * 2 + (1 - c if other else c)
        loads.append(pltpu.make_async_copy(
            weight_ref.at[:, pl.ds(pl.multiple_of(col * HEAD, HEAD), HEAD)], weights.at[k], w_sem.at[k]
        ))
        loads[-1].start()
    for copy in tables_in:
        copy.wait()
    build_tables(rows_in, cols_in, eye, spread_t, mix_t, unmix_t, gather_t)
    pltpu.make_async_copy(taps_recv, taps_recv, taps_recv_sem.at[0]).wait()
    for h in range(2):
        taps_spectrum[h] = spectrum(
            taps_recv[:, h].reshape(half, ROWS), spread_t[...], mix_t[...], turn[:CTX], turn[CTX:]
        )

    for h in range(2):
        tr, ti = turn[:CTX], turn[CTX:]
        pltpu.make_async_copy(recv.at[h], recv.at[h], recv_sem.at[h]).wait()
        if h == 1:
            keys_of.scatter(keys_ref, 0, True)
        d = spectrum(recv[h].reshape(half, ROWS), spread_t[...], mix_t[...], tr, ti)
        e = taps_spectrum[h]
        d_re, d_im, e_re, e_im = d[:, :ROWS], d[:, ROWS:], e[:, :ROWS], e[:, ROWS:]
        y_re = (d_re * e_re - d_im * e_im).astype(BF)
        y_im = (d_re * e_im + d_im * e_re).astype(BF)
        b = nn(jnp.concatenate([y_re, y_im], axis=1), unmix_t[...])
        b_re = b[:, :ROWS].reshape(GROUP, CTX, ROWS)
        b_im = b[:, ROWS:].reshape(GROUP, CTX, ROWS)
        c_re = (b_re * tr + b_im * ti).reshape(half, ROWS).astype(BF)
        c_im = (b_im * tr - b_re * ti).reshape(half, ROWS).astype(BF)
        points = jnp.concatenate([c_re, c_im], axis=0)
        for g in range(2):
            rows = pl.ds(pl.multiple_of(base[g] * GROUP, 256), 256)
            out_send[h, pl.ds(base[g], 16)] = (
                nn(gather_t[rows], points).astype(BF).reshape(16, GROUP, ROWS)
            )

            def reply(k, carry, h=h, g=g):
                to = base[g] + lax.rem(me + k, 16)
                pltpu.make_async_remote_copy(
                    src_ref=out_send.at[h, to], dst_ref=out_recv.at[h, me],
                    send_sem=back_send_sem.at[h], recv_sem=back_recv_sem.at[h],
                    device_id={"ctx": to}, device_id_type=MESH,
                ).start()
                return carry

            if g == 0:
                pltpu.make_async_copy(
                    out_send.at[h, me], out_recv.at[h, me], back_recv_sem.at[h]
                ).start()
            lax.fori_loop(1 if g == 0 else 0, 16, reply, 0)

    for copy in gates_in:
        copy.wait()

    def gate(h):
        pltpu.make_async_copy(out_recv.at[h], out_recv.at[h], back_recv_sem.at[h]).wait()
        for g in range(2):
            block = out_recv[h, pl.ds(base[g], 16)].reshape(ROWS, ROWS)
            filtered = nt(eye, block).astype(BF).astype(F32)
            gated_ref[:, cols_of[h][g]] = (
                second_in[h, g].astype(F32)
                * (filtered + skip[:, cols_of[h][g]] * product[h, g].astype(F32))
            ).astype(BF)

    gate(0)
    low = gated_ref[:, :512]
    for k in range(8):
        loads[k].wait()
        partial[k] = nn(low, weights[k, :512])
    keys_of.step_own(0)
    gate(1)
    high = gated_ref[:, 512:]

    def projected(k):
        return partial[k] + nn(high, weights[k, 512:])

    far_pair = lax.min(z, ZS - 1 - z)
    q_x = lax.select(far_pair < 2, x, mirror)
    q_core = lax.rem(far_pair, 2)
    q_slot = lax.div(x, 2) * 2 + lax.div(z, 4)

    def query_copies(j):
        to = 4 * c + j
        alone = (to == z) & (q_core == c) & (far_pair < 2)
        part = queries_ref.at[:, pl.ds(j * HS, HS)]
        slot = q_buf.at[q_slot]
        sem = q_recv_sem.at[q_slot]
        local = lambda: pltpu.make_async_copy(part, slot, sem)
        away = lambda: pltpu.make_async_remote_copy(
            src_ref=part, dst_ref=slot, send_sem=q_send_sem.at[j], recv_sem=sem,
            device_id={"ctx": q_x * ZS + to, "tp": y * 2 + q_core}, device_id_type=MESH,
        )
        return alone, local, away

    for j in range(4):
        start_either(*query_copies(j))

    swaps = []

    def swap(k):
        sib_send[k] = projected(k).astype(BF)
        swaps.append(pltpu.make_async_remote_copy(
            src_ref=sib_send.at[k], dst_ref=sib_recv.at[k],
            send_sem=sib_send_sem.at[k], recv_sem=sib_recv_sem.at[k],
            device_id={"tp": y * 2 + 1 - c}, device_id_type=MESH,
        ))
        swaps[-1].start()

    swap(0)

    def chip_sum(k):
        own = projected(4 + k)
        swaps[k].wait_recv()
        return own + sib_recv[k].astype(F32)

    right, left = lax.rem(y + 1, YS) * 2 + c, lax.rem(y + 3, YS) * 2 + c
    depth = ROWS // PARTS
    spans = [pl.ds(p * depth, depth) for p in range(PARTS)]

    def hop(source, into, send_sems, recv_sems, h, p):
        return pltpu.make_async_remote_copy(
            src_ref=source.at[h, spans[p]], dst_ref=into.at[h, spans[p]],
            send_sem=send_sems.at[h, p], recv_sem=recv_sems.at[h, p],
            device_id={"tp": (right, left)[h]}, device_id_type=MESH,
        )

    far = chip_sum(0).astype(BF)
    far_hops, near_hops = {}, {}
    for h in range(2):
        y_send[h] = far[:, h * 256:(h + 1) * 256]
    for p in range(PARTS):
        for h in range(2):
            far_hops[h, p] = hop(y_send, y_recv, y_send_sem, y_recv_sem, h, p)
            far_hops[h, p].start()
    for k in range(1, 4):
        swap(k)
    for k in range(1, 4):
        own_part[k] = chip_sum(k)
    keys_of.step_near(0)
    for p in range(PARTS):
        for h in range(2):
            far_hops[h, p].wait_recv()
            own_part[1 + h, spans[p], pl.ds(h * 256, 256)] += y_recv[h, spans[p]].astype(F32)
            near_send[h, spans[p]] = own_part[1 + h, spans[p]].astype(BF)
            near_hops[h, p] = hop(near_send, near_recv, near_send_sem, near_recv_sem, h, p)
            near_hops[h, p].start()
    keys_of.step_far(0)

    scale = 1.0 / math.sqrt(HS) * math.log2(math.e)
    blocks, first_step = [], []
    steps_before = 0
    for i in range(4):
        row = lax.min(x, mirror) if i < 2 else lax.max(x, mirror)
        pair = lax.select(row == x, c, c + 2)
        zq = pair if i % 2 == 0 else ZS - 1 - pair
        rank = row * ZS + zq
        blocks.append((row, zq, rank, lax.div(rank, 4)))
        first_step.append(steps_before)
        steps_before = steps_before + lax.div(rank, 4) + 1

    def key_block(buf, step, b):
        return buf[lax.div(step, 2), b % 2, lax.rem(step, 2) * 2 + b // 2]

    def score_all(i):
        row, zq, rank, last = blocks[i]
        pltpu.make_async_copy(q_buf.at[i], q_buf.at[i], q_recv_sem.at[i]).wait()
        query = q_buf[i]

        def score(step, top, masked=False):
            for b in range(KEYS // ROWS):
                s = nt(query, key_block(k_buf, step, b))
                if masked:
                    key_pos = across + step * KEYS + b * ROWS
                    s = jnp.where(key_pos <= down + rank * ROWS, s, NEG)
                scores[step, b] = s
                top = jnp.maximum(top, jnp.maximum(s[:, :128], s[:, 128:]))
            return top

        top = lax.fori_loop(0, last, score, jnp.full((ROWS, 128), NEG, F32))
        top = jnp.max(score(last, top, True), axis=1, keepdims=True)
        totals[i] = jnp.broadcast_to(top, (ROWS, 128))

    def weigh_half(i, r):
        row, zq, rank, last = blocks[i]
        rows = slice(r * 128, (r + 1) * 128)
        top = totals[i, rows]

        def weight(step, total):
            for b in range(KEYS // ROWS):
                for l in range(2):
                    w = jnp.exp2((scores[step, b, rows, l * 128:(l + 1) * 128] - top) * scale)
                    rounded[first_step[i] + step, rows, b * ROWS + l * 128:b * ROWS + (l + 1) * 128] = (
                        w.astype(BF)
                    )
                    total = total + w
            return total

        total = lax.fori_loop(0, last + 1, weight, jnp.zeros((128, 128), F32))
        totals[i, rows] = jnp.broadcast_to(jnp.sum(total, axis=1, keepdims=True), (128, 128))

    def weigh_all(i):
        for r in range(2):
            weigh_half(i, r)

    def values_out(p):
        for h in range(2):
            near_hops[h, p].wait_recv()
        mixed = (
            own_part[3, spans[p]] + near_recv[0, spans[p]].astype(F32) + near_recv[1, spans[p]].astype(F32)
        ).astype(BF)
        mine[spans[p]] = mixed
        values_of.scatter(mine, p, True)
        mixed_ref[spans[p]] = mixed

    values_out(0)
    for row in range(XS):
        keys_of.finish(row, 1)
    score_all(0)
    weigh_all(0)
    values_out(1)
    score_all(1)
    weigh_all(1)
    values_of.step_own(0)
    score_all(2)
    values_of.step_own(1)
    weigh_all(2)
    values_of.step_near(0)
    score_all(3)
    values_of.step_near(1)
    weigh_all(3)

    def output_copies(i):
        row, zq, rank, last = blocks[i]
        core, j = lax.div(z, 4), lax.rem(z, 4)
        alone = (zq == z) & (core == c) & (row == x)
        local = lambda: pltpu.make_async_copy(o_send.at[i], o_recv.at[j], o_recv_sem.at[j])
        away = lambda: pltpu.make_async_remote_copy(
            src_ref=o_send.at[i], dst_ref=o_recv.at[j],
            send_sem=o_send_sem.at[i], recv_sem=o_recv_sem.at[j],
            device_id={"ctx": row * ZS + zq, "tp": y * 2 + core}, device_id_type=MESH,
        )
        return alone, local, away

    def attend_row(row, i, first=False):
        last = blocks[i][3]

        def value(step, acc):
            part = jnp.concatenate([key_block(v_buf, step, b) for b in range(KEYS // ROWS)], axis=0)
            return acc + nn(rounded[first_step[i] + step], part)

        start = jnp.zeros((ROWS, HS), F32) if first else attended_sum[i]
        attended_sum[i] = lax.fori_loop(2 * row, lax.min(2 * row + 2, last + 1), value, start)

    def output(i):
        o_send[i] = (attended_sum[i] / totals[i]).astype(BF)
        start_either(*output_copies(i))

    def output_low():
        output(0)
        output(1)

    xl, xr, x2 = values_of.xl, values_of.xr, values_of.x2
    values_of.finish(x, PARTS)
    for i in range(4):
        attend_row(x, i, True)
    values_of.step_far(0)
    values_of.step_far(1)
    for row in (xl, xr):
        values_of.finish(row, PARTS)
        for i in range(4):
            attend_row(row, i)
    pl.when(x != 2)(output_low)
    values_of.finish(x2, PARTS)
    for i in (2, 3):
        attend_row(x2, i)
        output(i)
    for i in (0, 1):
        attend_row(x2, i)
    pl.when(x == 2)(output_low)

    some = taps_recv.at[pl.ds(0, CTX - 1)]
    pltpu.make_async_copy(some, some, taps_send_sem.at[0]).wait()
    for h in range(2):
        some = recv.at[h, pl.ds(0, CTX - 1)]
        pltpu.make_async_copy(some, some, send_sem.at[h]).wait()
        some = out_recv.at[h, pl.ds(0, CTX - 1)]
        pltpu.make_async_copy(some, some, back_send_sem.at[h]).wait()
    keys_of.scatter(keys_ref, 0, False)
    keys_of.drain(0)
    for p in range(PARTS):
        values_of.scatter(mine, p, False)
        values_of.drain(p)
        for h in range(2):
            far_hops[h, p].wait_send()
            near_hops[h, p].wait_send()
    for j in range(4):
        alone, local, away = query_copies(j)
        pl.when(jnp.logical_not(alone))(lambda away=away: away().wait_send())
        swaps[j].wait_send()
    for j in range(4):
        pltpu.make_async_copy(o_recv.at[j], o_recv.at[j], o_recv_sem.at[j]).wait()
        attended_ref[:, j * HS:(j + 1) * HS] = o_recv[j]
    for i in range(4):
        alone, local, away = output_copies(i)
        pl.when(jnp.logical_not(alone))(lambda away=away: away().wait_send())


def start_either(alone, local, away):
    pl.when(alone)(lambda: local().start())
    pl.when(jnp.logical_not(alone))(lambda: away().start())


def vmem(count):
    return [pl.BlockSpec(memory_space=pltpu.VMEM)] * count


def hbm(count):
    return [pl.BlockSpec(memory_space=pl.ANY)] * count


def hand_over(a, b, a_out, b_out):
    a_out[...] = a[...]
    b_out[...] = b[...]


def per_device(
    first_input, second_input, value_input, filter_taps, skip_gain, out_weight, queries, keys
):
    consts = [jnp.asarray(t) for t in tables()]
    dma = lambda *shape: pltpu.SemaphoreType.DMA(shape)
    bf = lambda *shape: pltpu.VMEM(shape, BF)
    fl = lambda *shape: pltpu.VMEM(shape, F32)
    sems = lambda p: [dma(p, 4), dma(p), dma(p), dma(p), dma(2, p), dma(XS, p), dma(2, p)]
    out = jax.ShapeDtypeStruct((ROWS, HEAD), BF)
    mixed, attended = pl.pallas_call(
        whole_kernel,
        out_shape=(out, out),
        in_specs=hbm(11),
        out_specs=tuple(vmem(2)),
        scratch_shapes=[
            bf(2, 2, ROWS, 256), bf(2, 2, ROWS, 256), bf(2, 2, ROWS, 256), bf(2, 2, ROWS, 256),
            fl(1, 1024), bf(2 * CTX, 512), bf(512, 256), fl(2 * CTX, ROWS),
            bf(1024, 512), bf(512, 512), bf(512, 512), bf(512, 1024),
            bf(2, 2, ROWS, 256),
            bf(2, 2, 16, GROUP, ROWS), bf(2, CTX, GROUP, ROWS),
            bf(2, 16, 2, GROUP, ROWS), bf(CTX, 2, GROUP, ROWS), fl(2, 512, 512),
            bf(2, CTX, GROUP, ROWS), bf(2, CTX, GROUP, ROWS),
            bf(ROWS, 1024),
            bf(8, 1024, HEAD), fl(8, ROWS, HEAD), fl(4, ROWS, HEAD), bf(4, ROWS, HEAD), bf(4, ROWS, HEAD),
            bf(2, ROWS, 256), bf(2, ROWS, 256), bf(2, ROWS, HEAD), bf(2, ROWS, HEAD), bf(ROWS, HEAD),
            bf(XS, 2, ZS // 2, ROWS, HS), bf(XS, 2, ZS // 2, ROWS, HS), bf(4, ROWS, HS),
            fl(TOTAL // KEYS, KEYS // ROWS, ROWS, ROWS), bf(CHUNKS, ROWS, KEYS), fl(4, ROWS, 128), fl(4, ROWS, HS),
            bf(4, ROWS, HS), bf(4, ROWS, HS),
            dma(4, 4), dma(4), dma(1), dma(1), dma(2), dma(2), dma(2), dma(2),
            dma(8), dma(4), dma(4), dma(2, PARTS), dma(2, PARTS), dma(2, PARTS), dma(2, PARTS),
            dma(4), dma(4), dma(4), dma(4),
        ] + sems(1) + sems(PARTS),
        compiler_params=pltpu.CompilerParams(
            collective_id=0, has_side_effects=True, vmem_limit_bytes=60 * 1024 * 1024
        ),
        name="whole",
    )(first_input, second_input, value_input, filter_taps, skip_gain.reshape(1, 1024), out_weight,
      queries, keys, *consts)
    return pl.pallas_call(
        hand_over,
        out_shape=(out, out),
        in_specs=vmem(2),
        out_specs=tuple(vmem(2)),
        name="hand_over",
    )(mixed, attended)


def solution(mesh):
    return jax.shard_map(
        per_device,
        mesh=mesh,
        in_specs=(
            P("ctx", "tp"),
            P("ctx", "tp"),
            P("ctx", "tp"),
            P("ctx", "tp"),
            P("tp"),
            P("tp", None),
            P("ctx", "tp"),
            P("ctx", "tp"),
        ),
        out_specs=(P("ctx", "tp"), P("ctx", "tp")),
        check_vma=False,
    )
```
